256 devices in a mesh: slab: 128 (over x, z, y), chan: 2 (over core).
Axes of the slice: x: 4, y: 4, z: 8, core: 2. Of those that a mesh axis runs over, the one named last changes fastest.
Arguments:
- points: bfloat16 [32768, 64, 128], P(('slab', 'chan')), may hold values from -6 to 6
- near_start: int32 [32768, 128], P(('slab', 'chan')), may hold values from 0 to 120
- near_weight: bfloat16 [32768, 8, 128], P(('slab', 'chan')), may hold values from -2 to 2
- dest_slab: int32 [32768, 1], P(('slab', 'chan')), may hold values from 0 to 127; in each aligned block of 128 rows (0 to 127, 128 to 255, ...) at most 2 rows name the same one
- dest_block: int32 [32768], P(('slab', 'chan')), may hold values from 0 to 127
- live_count: int32 [256], P(('slab', 'chan')), may hold values from 1 to 128, 28672 in all
- lift_w: bfloat16 [64, 64], replicated, may hold values from -0.75 to 0.75
- spec_weight: bfloat16 [2, 64, 64, 32, 1024], P(None, None, None, None, ('slab', 'chan')), may hold values from -8.375 to 8.375
- skip_w: bfloat16 [64, 64], replicated, may hold values from -0.75 to 0.75
- skip_bias: float32 [64], replicated, may hold values from -3 to 3
- proj_in: bfloat16 [64, 128], replicated, may hold values from -0.75 to 0.75
- proj_out: bfloat16 [128], replicated, may hold values from -0.5 to 0.5
Outputs:
- pressure: float32 [32768, 128], P(('slab', 'chan'))
The draws below stay inside these ranges and needn't reach their ends.
Inputs may be any that keep to these rules, and one draw needn't show every extreme that they name: `dest_slab`: among the 128 blocks of one device no slab is named by more than 2 blocks, a bound that some block reaches. `live_count`: blocks of a device at or past its count are padding; some device has all 128 live.
All inputs are finite; a program needn't handle non-finite values.
Results may differ from the reference program's by a relative error of at most 0.015.
Values may be sent and summed in bfloat16 or wider, within the bound.
A program may use at most 128 MiB of HBM per device.

```python
import math
import jax
import jax.numpy as jnp
import numpy as np
from jax import lax

C = 64
G = 128
M = 32
HID = 128
PB = 128
NB = 8
BLK_DEV = 128
CAP = 2
BLOCKS = 32768
NCB = 128
MM = 1024
N_SLAB = 128
N_CHAN = 2


def set_ends(values, rng, smallest, largest):
    index_at = [jax.random.randint(jax.random.fold_in(rng, axis), (), 0, length) for axis, length in enumerate(values.shape)]
    widest = values.shape.index(max(values.shape))
    next_to = index_at[:widest] + [(index_at[widest] + 1) % values.shape[widest]] + index_at[widest + 1:]
    return values.at[tuple(index_at)].set(smallest).at[tuple(next_to)].set(largest)


def block_scale(stream_key, dims, shards, smallest, largest):
    def one(axis_at, blocks):
        steps = jax.random.uniform(jax.random.fold_in(jax.random.fold_in(stream_key, 6), axis_at), (blocks,), jnp.float32, smallest / len(shards), largest / len(shards))
        return jnp.repeat(jnp.exp(steps), dims[axis_at] // blocks).reshape((-1,) + (1,) * (len(dims) - axis_at - 1))

    gain = one(*shards[0])
    for cut in shards[1:]:
        gain = gain * one(*cut)
    return gain


def length_profile(count, total, bound, skew):
    weights = [(1 << 20) // math.isqrt(rank ** skew) + 1 for rank in range(2, count + 1)]
    rest, given = total - bound - (count - 1), [1] * (count - 1)
    while rest > 0:
        free = [i for i in range(count - 1) if given[i] < bound]
        mass, budget = sum([weights[i] for i in free]), rest
        for i in free:
            more = min(bound - given[i], max(1, budget * weights[i] // mass), rest)
            given[i] = given[i] + more
            rest = rest - more
    return np.array([bound] + given)


def ragged(stream_key, amount, total, reach, slope):
    if amount == 2:
        one = jax.random.randint(stream_key, (), max(1, total - reach), min(reach, total - 1) + 1)
        return jnp.stack([one, total - one])
    tallies = jnp.asarray(length_profile(amount, total, reach, slope), jnp.int32)
    couples = (amount - 1) // 2
    donor, receiver = tallies[1:1 + 2 * couples:2], tallies[2:2 + 2 * couples:2]
    slack = jnp.minimum(donor - 1, reach - receiver)
    passed = jax.random.randint(jax.random.fold_in(stream_key, 1), (couples,), 0, 1 << 20) % (slack + 1)
    tallies = tallies.at[1:1 + 2 * couples:2].set(donor - passed).at[2:2 + 2 * couples:2].set(receiver + passed)
    return tallies[jax.random.permutation(jax.random.fold_in(stream_key, 2), amount)]


def assign_block(stream_key, own, number, rows, amount, top, most, lean):
    sequence = jax.random.permutation(stream_key, amount)
    packed, common = portions_of(amount, rows * top, most, lean, True), portions_of(amount, rows * top, most, lean, False)
    places = jnp.arange(amount)

    def named(sizes, rotation):
        used = int((sizes > 0).sum())
        fixed = max(1, used // 4)
        passed = fixed + (places - fixed + rotation * (used - fixed)) % max(1, amount - fixed)
        return jnp.zeros((amount,), jnp.int32).at[sequence[jnp.where(places < fixed, places, passed)]].set(jnp.asarray(sizes, jnp.int32))

    sizes = jnp.where(number % 4 == 0, named(packed, number // 4), named(common, number - number // 4 - 1))
    mixed = jax.random.permutation(jax.random.fold_in(own, 3), amount)
    giver, taker = mixed[0:amount // 2 * 2:2], mixed[1:amount // 2 * 2:2]
    room = jnp.minimum(sizes[giver] - 1, most - sizes[taker]) // 2
    room = jnp.where((giver == sequence[0]) | (taker == sequence[0]) | (sizes[taker] == 0), 0, jnp.maximum(room, 0))
    passed = jax.random.randint(jax.random.fold_in(own, 4), (amount // 2,), 0, 1 << 20) % (room + 1)
    sizes = sizes.at[giver].add(-passed).at[taker].add(passed)
    members = jnp.searchsorted(jnp.cumsum(sizes), jnp.arange(rows * top), side="right").astype(jnp.int32)
    table = members.reshape(top, rows).T
    table = table[jax.random.permutation(jax.random.fold_in(own, 1), rows)]
    rotation = jax.random.randint(jax.random.fold_in(own, 2), (rows, 1), 0, top)
    return jnp.take_along_axis(table, (jnp.arange(top)[None, :] + rotation) % top, axis=1)


def portions_of(count, total, reach, skew, full):
    portions = [(1 << 20) // math.isqrt(rank ** skew) + 1 for rank in range(1, count + 1)]
    largest = reach if full else min(reach, max(-(-total // count), total * portions[0] // sum(portions)))
    least = 1 if total - largest >= count - 1 else 0
    given, rest = [largest] + [least] * (count - 1), total - largest - least * (count - 1)
    while rest > 0:
        candidates = [i for i in range(1, count) if given[i] < largest] or [i for i in range(1, count) if given[i] < reach]
        pool, left = sum([portions[i] for i in candidates]), rest
        for i in candidates:
            extra = min(reach - given[i], max(1, left * portions[i] // pool), rest)
            given[i] = given[i] + extra
            rest = rest - extra
    return np.array(given)


def centred(own_key, shape, width, limit, pieces=(), kind=jnp.bfloat16):
    values = width * jax.random.normal(own_key, shape, jnp.float32)
    if pieces:
        values = values * block_scale(own_key, shape, pieces, -0.22, 0.18)
    return jnp.clip(values, -limit, limit).astype(kind)


def setup_inputs(seed: int = 0) -> dict:
    key_list = jax.random.split(jax.random.key(seed), 13)
    points = centred(key_list[0], (BLOCKS, C, PB), 1.0, 6.0, ((0, 256),))
    near_start = set_ends(jax.random.randint(key_list[1], (BLOCKS, PB), 0, G - NB + 1), jax.random.fold_in(key_list[1], 1), 0, G - NB).astype(jnp.int32)
    near_weight = centred(key_list[2], (BLOCKS, NB, PB), 0.35, 2.0, ((0, 256),))
    dest_slab_keys = jax.random.split(jax.random.fold_in(key_list[3], 1), BLOCKS // BLK_DEV)
    dest_slab_turns = jax.random.permutation(jax.random.fold_in(key_list[3], 3), BLOCKS // BLK_DEV)
    dest_slab = jax.vmap(lambda own, number: assign_block(jax.random.fold_in(key_list[3], 2), own, number, BLK_DEV, N_SLAB, 1, CAP, 2))(dest_slab_keys, dest_slab_turns).reshape((BLOCKS, 1))
    dest_block = set_ends(jax.random.randint(key_list[4], (BLOCKS,), 0, NCB), jax.random.fold_in(key_list[4], 1), 0, NCB - 1).astype(jnp.int32)
    live_count = ragged(key_list[5], N_SLAB * N_CHAN, N_SLAB * N_CHAN * BLK_DEV * 7 // 8, BLK_DEV, 2).astype(jnp.int32)
    lift_w = centred(key_list[6], (C, C), C ** -0.5, 0.75)
    spec_weight = centred(key_list[7], (2, C, C, M, MM), (1.4 * G ** 1.5 / (C ** 0.5 * M ** 1.5 * min(1.0, 0.875 * BLOCKS / (G * G)) ** 0.5)), 8.375, ((4, 256),))
    skip_w = centred(key_list[8], (C, C), C ** -0.5, 0.75)
    skip_bias = centred(key_list[9], (C,), 0.5, 3.0, (), jnp.float32)
    proj_in = centred(key_list[10], (C, HID), C ** -0.5, 0.75)
    proj_out = centred(key_list[11], (HID,), HID ** -0.5, 0.5)
    return dict(points=points, near_start=near_start, near_weight=near_weight, dest_slab=dest_slab, dest_block=dest_block, live_count=live_count, lift_w=lift_w, spec_weight=spec_weight, skip_w=skip_w, skip_bias=skip_bias, proj_in=proj_in, proj_out=proj_out)


def signed_modes(count):
    index = jnp.arange(count, dtype=jnp.int32)
    return jnp.where(index < count // 2, index, index - count)


def angles(length, count):
    positions = jnp.arange(length, dtype=jnp.int32)
    product = jnp.mod(positions[:, None] * signed_modes(count)[None, :], length)
    phase = product.astype(jnp.float32) * (2.0 * math.pi / length)
    return jnp.cos(phase), jnp.sin(phase)


def product_sum(form, left, right):
    return jnp.einsum(form, left.astype(jnp.float32), right.astype(jnp.float32), precision=lax.Precision.HIGHEST)


def per_device(array):
    return array.reshape((N_SLAB * N_CHAN, BLK_DEV) + array.shape[1:])


def reference(points, near_start, near_weight, dest_slab, dest_block, live_count, lift_w, spec_weight, skip_w, skip_bias, proj_in, proj_out):
    cell_line = dest_slab[:, 0] * NCB + dest_block
    block_rows = jnp.arange(BLK_DEV, dtype=jnp.int32)

    def encode(grid, inputs):
        block_points, block_start, block_weight, block_cells, count = inputs
        live = block_rows < count
        lifted = product_sum('bcp,cd->bdp', block_points, lift_w).astype(jnp.bfloat16)
        values = lifted.astype(jnp.float32)[:, None, :, :] * block_weight.astype(jnp.float32)[:, :, None, :]
        values = values.transpose(0, 1, 3, 2)
        targets = block_start[:, None, :] + jnp.arange(NB, dtype=jnp.int32)[None, :, None]
        block_index = jnp.broadcast_to(block_rows[:, None, None], targets.shape)
        part = jnp.zeros((BLK_DEV, G, C), jnp.float32).at[block_index, targets].add(values)
        part = part.transpose(0, 2, 1).astype(jnp.bfloat16)
        where_to = jnp.where(live, block_cells, G * G)
        grid = grid.at[where_to].add(part.astype(jnp.float32), mode="drop")
        return grid, None

    grid_start = jnp.zeros((G * G, C, G), jnp.float32)
    grid, unused = lax.scan(encode, grid_start, (per_device(points), per_device(near_start), per_device(near_weight), per_device(cell_line), live_count))
    latent = grid.reshape(G, G, C, G).transpose(2, 0, 1, 3)
    cosine, sine = angles(G, M)
    z_real = product_sum('cxyz,zk->cxyk', latent, cosine)
    z_imag = -product_sum('cxyz,zk->cxyk', latent, sine)
    y_real = product_sum('cxyk,yq->cxqk', z_real, cosine) + product_sum('cxyk,yq->cxqk', z_imag, sine)
    y_imag = product_sum('cxyk,yq->cxqk', z_imag, cosine) - product_sum('cxyk,yq->cxqk', z_real, sine)
    y_real = y_real.reshape(C, G, M * M).astype(jnp.bfloat16)
    y_imag = y_imag.reshape(C, G, M * M).astype(jnp.bfloat16)
    x_real = product_sum('cxm,xp->pcm', y_real, cosine) + product_sum('cxm,xp->pcm', y_imag, sine)
    x_imag = product_sum('cxm,xp->pcm', y_imag, cosine) - product_sum('cxm,xp->pcm', y_real, sine)

    def mix(inputs):
        real_part, imag_part, weight_slice = inputs
        out_real = product_sum('im,iom->om', real_part, weight_slice[0]) - product_sum('im,iom->om', imag_part, weight_slice[1])
        out_imag = product_sum('im,iom->om', real_part, weight_slice[1]) + product_sum('im,iom->om', imag_part, weight_slice[0])
        return out_real, out_imag

    mixed_real, mixed_imag = lax.map(mix, (x_real, x_imag, spec_weight.transpose(3, 0, 1, 2, 4)))
    back_real = product_sum('pom,xp->oxm', mixed_real, cosine) - product_sum('pom,xp->oxm', mixed_imag, sine)
    back_imag = product_sum('pom,xp->oxm', mixed_imag, cosine) + product_sum('pom,xp->oxm', mixed_real, sine)
    back_real = back_real.astype(jnp.bfloat16).reshape(C, G, M, M)
    back_imag = back_imag.astype(jnp.bfloat16).reshape(C, G, M, M)
    u_real = product_sum('cxqk,yq->cxyk', back_real, cosine) - product_sum('cxqk,yq->cxyk', back_imag, sine)
    u_imag = product_sum('cxqk,yq->cxyk', back_imag, cosine) + product_sum('cxqk,yq->cxyk', back_real, sine)
    spectral = (product_sum('cxyk,zk->cxyz', u_real, cosine) - product_sum('cxyk,zk->cxyz', u_imag, sine)) * (1.0 / (G * G * G))
    mixing = product_sum('io,ixyz->oxyz', skip_w, latent)
    grid_out = jax.nn.gelu(spectral + mixing + skip_bias[:, None, None, None]).astype(jnp.bfloat16)
    table = grid_out.reshape(C, G * G, G).transpose(1, 0, 2)

    def decode(inputs):
        block_start, block_weight, block_cells, count = inputs
        live = block_rows < count
        cells = table[block_cells]
        total = jnp.zeros((BLK_DEV, C, PB), jnp.float32)
        for neighbour in range(NB):
            picked = jnp.take_along_axis(cells, (block_start + neighbour)[:, None, :], axis=2)
            total = total + picked.astype(jnp.float32) * block_weight[:, neighbour, :].astype(jnp.float32)[:, None, :]
        near_val = total.astype(jnp.bfloat16)
        dec_hidden = jax.nn.gelu(product_sum('bcp,ch->bhp', near_val, proj_in)).astype(jnp.bfloat16)
        result = product_sum('bhp,h->bp', dec_hidden, proj_out)
        return jnp.where(live[:, None], result, jnp.zeros((), result.dtype))

    pressure = lax.map(decode, (per_device(near_start), per_device(near_weight), per_device(cell_line), live_count))
    return pressure.reshape(N_SLAB * N_CHAN * BLK_DEV, PB)
```

```python
import math

import jax
import jax.numpy as jnp
import numpy as np
from jax import lax
from jax.experimental import pallas as pl
from jax.experimental.pallas import tpu as pltpu
from jax.sharding import PartitionSpec as P

G = 128
M = 32
PB = 128
NB = 8
C = 64
HALF = 32
BF = jnp.bfloat16
F32 = jnp.float32
LIMIT = 48 * 1024 * 1024
VM = pl.BlockSpec(memory_space=pltpu.VMEM)
SM = pl.BlockSpec(memory_space=pltpu.SMEM)
UNROLL = 4


def trig():
    modes = np.concatenate([np.arange(M // 2), np.arange(M // 2) - M // 2])
    phase = (np.arange(G)[:, None] * modes[None, :] % G) * (2.0 * math.pi / G)
    return np.cos(phase), np.sin(phase)


def call(kernel, out_shape, in_specs, scratch=(), out_specs=None):
    return pl.pallas_call(
        kernel,
        out_shape=out_shape,
        in_specs=in_specs,
        out_specs=VM if out_specs is None else out_specs,
        scratch_shapes=list(scratch),
        compiler_params=pltpu.CompilerParams(vmem_limit_bytes=LIMIT),
    )


def dot(left, right, dims=((1,), (0,))):
    return lax.dot_general(left, right, (dims, ((), ())), preferred_element_type=F32)


def gelu(x):
    inner = x * (0.7978845608028654 + 0.035677408136300125 * (x * x))
    half = 0.5 * x
    return half + half * jnp.tanh(inner)


def near_transposed(start, weight):
    base = lax.broadcasted_iota(jnp.int32, (NB, PB), 0) - start
    which = base & 7
    tile = -(base >> 3)
    picked = jnp.zeros((NB, PB), F32)
    for j in range(NB):
        picked = jnp.where(which == j, weight[j : j + 1, :], picked)
    rows = [jnp.where(tile == t, picked, 0.0) for t in range(G // NB)]
    return jnp.concatenate(rows, axis=0).astype(BF)


def pack_kernel(blk_ref, line_ref, start_ref, weight_ref, out_ref):
    row = lax.broadcasted_iota(jnp.int32, (8, PB), 0)

    def step(s, carry):
        b0, b1 = blk_ref[2 * s], blk_ref[2 * s + 1]
        c0, c1 = jnp.maximum(b0, 0), jnp.maximum(b1, 0)
        l0 = jnp.where(b0 >= 0, line_ref[c0] + 1, 0)
        l1 = jnp.where(b1 >= 0, line_ref[c1] + 1, 0)
        info = jnp.where(
            row == 0,
            start_ref[pl.ds(c0, 1), :],
            jnp.where(
                row == 1,
                start_ref[pl.ds(c1, 1), :],
                jnp.where(row == 2, l0, jnp.where(row == 3, l1, 0)),
            ),
        )
        out_ref[s, 0:8, :] = weight_ref[c0]
        out_ref[s, 8:16, :] = weight_ref[c1]
        out_ref[s, 16:24, :] = info.astype(F32).astype(BF)
        return carry

    lax.fori_loop(0, G, step, 0)


def encode_kernel(slot_ref, count_ref, points_ref, start_ref, weight_ref, lift_ref, out_ref):
    count = count_ref[0]

    def step(group, carry):
        for u in range(UNROLL):
            b = jnp.minimum(group * UNROLL + u, count - 1)
            slot = slot_ref[b]
            slab, rank = slot >> 1, slot & 1
            lifted = dot(lift_ref[...], points_ref[b]).astype(BF)
            near = near_transposed(start_ref[pl.ds(b, 1), :], weight_ref[b].astype(F32))
            part = dot(lifted, near, ((1,), (1,))).astype(BF)
            out_ref[2 * slab, rank] = part[:HALF]
            out_ref[2 * slab + 1, rank] = part[HALF:]
        return carry

    lax.fori_loop(0, (count + UNROLL - 1) // UNROLL, step, 0)


def forward_kernel(line_ref, parts_ref, dy_ref, dz_ref, latent_ref, spec_ref, acc, ybuf):
    acc[...] = jnp.zeros_like(acc)

    def add(src, carry):
        for r in range(2):
            line = line_ref[2 * src + r]
            rows = pl.ds(pl.multiple_of(line * HALF, HALF), HALF)
            acc[rows, :] += parts_ref[src, r].astype(F32)
        return carry

    lax.fori_loop(0, 256, add, 0)
    latent_ref[...] = acc[0 : G * HALF, :].astype(BF)
    for c in range(HALF):
        plane = acc[pl.ds(c, G, stride=HALF), :].astype(BF)
        ybuf[pl.ds(c, 3 * M, stride=HALF), :] = dot(dy_ref[...], plane)
    for q in range(M):
        real = ybuf[q * HALF : (q + 1) * HALF, :].astype(BF)
        imag = ybuf[(M + q) * HALF : (M + q + 1) * HALF, :].astype(BF)
        minus = ybuf[(2 * M + q) * HALF : (2 * M + q + 1) * HALF, :].astype(BF)
        first = jnp.concatenate([real, imag, imag, minus], axis=0)
        second = jnp.concatenate([imag, minus, minus, -imag], axis=0)
        both = jnp.concatenate([first, second], axis=1)
        spec_ref[q * M : (q + 1) * M, :] = dot(dz_ref[...], both, ((1,), (1,))).astype(BF)


def mix_kernel(spec_ref, weight_ref, fwd_ref, bwd_ref, out_ref, xbuf, rhs):
    prod = dot(fwd_ref[...], spec_ref[...])
    for h in range(2):
        cos = prod[h * 256 : h * 256 + 128, 0:64]
        sin = prod[h * 256 + 128 : h * 256 + 256, 64:128]
        xbuf[h] = cos + sin

    def chunk(t, carry):
        rows = pl.ds(pl.multiple_of(t * 32, 32), 32)
        real = jnp.zeros((32, C), F32)
        imag = jnp.zeros((32, C), F32)
        for h in range(2):
            x = xbuf[h, rows, :]
            for c in range(HALF):
                wr = weight_ref[0, h * HALF + c, rows, :].astype(F32)
                wi = weight_ref[1, h * HALF + c, rows, :].astype(F32)
                xr = x[:, c : c + 1]
                xi = x[:, HALF + c : HALF + c + 1]
                real = real + xr * wr - xi * wi
                imag = imag + xr * wi + xi * wr
        for h in range(2):
            mr = real[:, h * HALF : (h + 1) * HALF]
            mi = imag[:, h * HALF : (h + 1) * HALF]
            top = jnp.concatenate([mr, mi, -mi, mr], axis=1).astype(BF)
            low = jnp.concatenate([-mi, mr, -mr, -mi], axis=1).astype(BF)
            rhs[pl.ds(pl.multiple_of(h * 256 + t * 32, 32), 32), :] = top
            rhs[pl.ds(pl.multiple_of(h * 256 + 128 + t * 32, 32), 32), :] = low
        return carry

    lax.fori_loop(0, 4, chunk, 0)
    out_ref[...] = dot(bwd_ref[...], rhs[...]).astype(BF)


def inverse_kernel(back_ref, own_ref, other_ref, skip_ref, bias_ref, ez_ref, ey_ref, out_ref, ubuf, sbuf):
    for q in range(M):
        both = dot(back_ref[q * M : (q + 1) * M, :], ez_ref[...], ((0,), (0,)))
        ubuf[q * C : (q + 1) * C, :] = both[0:C, 0:G] + both[C : 2 * C, G : 2 * G]
    for c in range(HALF):
        lines = ubuf[pl.ds(c, 2 * M, stride=HALF), :].astype(BF)
        sbuf[pl.ds(c, G, stride=HALF), :] = dot(ey_ref[...], lines)

    def step(group, carry):
        for u in range(4):
            rows = pl.ds(pl.multiple_of((group * 4 + u) * HALF, HALF), HALF)
            latent = jnp.concatenate([own_ref[rows, :], other_ref[rows, :]], axis=0)
            total = sbuf[rows, :] + dot(skip_ref[...], latent) + bias_ref[...]
            out_ref[rows, :] = gelu(total).astype(BF)
        return carry

    lax.fori_loop(0, G // 4, step, 0)


def decode_kernel(line_ref, meta_ref, own_ref, other_ref, proj_in_ref, proj_out_ref, out_ref, todo):
    def collect(s, count):
        todo[count] = s
        return count + jnp.where(line_ref[s] < G, 1, 0)

    count = lax.fori_loop(0, 256, collect, 0)

    def step(group, carry):
        for u in range(UNROLL):
            s = todo[jnp.minimum(group * UNROLL + u, count - 1)]
            src, rank = s >> 1, s & 1
            line = line_ref[s]
            rows = pl.ds(pl.multiple_of(line * HALF, HALF), HALF)
            cells = jnp.concatenate([own_ref[rows, :], other_ref[rows, :]], axis=0)
            info = meta_ref[src, 16:24, :].astype(F32)
            start = jnp.where(rank == 0, info[0:1, :], info[1:2, :]).astype(jnp.int32)
            weight = meta_ref[src, pl.ds(pl.multiple_of(rank * 8, 8), 8), :].astype(F32)
            near = near_transposed(start, weight)
            value = dot(cells, near).astype(BF)
            hidden = gelu(dot(proj_in_ref[...], value)).astype(BF)
            out_ref[pl.ds(s, 1), :] = dot(proj_out_ref[...], hidden)[0:1, :]
        return carry

    lax.fori_loop(0, (count + UNROLL - 1) // UNROLL, step, 0)


def unpack_kernel(slot_ref, values_ref, out_ref):
    def step(b, carry):
        slot = slot_ref[b]
        row = values_ref[pl.ds(jnp.maximum(slot, 0), 1), :]
        out_ref[pl.ds(b, 1), :] = jnp.where(slot >= 0, row, 0.0)
        return carry

    lax.fori_loop(0, 128, step, 0, unroll=8)


def shards(
    points,
    near_start,
    near_weight,
    dest_slab,
    dest_block,
    live_count,
    lift_w,
    spec_weight,
    skip_w,
    skip_bias,
    proj_in,
    proj_out,
):
    cos, sin = trig()
    chan = lax.axis_index("chan")
    every = ("slab", "chan")

    ids = jnp.arange(128, dtype=jnp.int32)
    live = ids < live_count[0]
    target = jnp.where(live, dest_slab[:, 0], -1)
    same = (target[:, None] == target[None, :]) & (ids[None, :] < ids[:, None])
    rank = jnp.sum(same.astype(jnp.int32), axis=1)
    slot = jnp.where(live, target * 2 + rank, -1)
    slot_ids = jnp.arange(256, dtype=jnp.int32)
    block = jnp.max(jnp.where(slot[None, :] == slot_ids[:, None], ids[None, :], -1), axis=1)

    meta = call(pack_kernel, jax.ShapeDtypeStruct((128, 24, PB), BF), [SM, SM, VM, VM])(
        block, dest_block, near_start, near_weight
    )
    meta = lax.all_to_all(meta, "slab", split_axis=0, concat_axis=0, tiled=True)
    parts = call(encode_kernel, jax.ShapeDtypeStruct((256, 2, HALF, G), BF), [SM, SM] + [VM] * 4)(
        slot, live_count, points, near_start, near_weight, lift_w.T
    )
    parts = lax.all_to_all(parts, every, split_axis=0, concat_axis=0, tiled=True)

    lines = meta[:, 18:20, 0].astype(jnp.int32)
    lines = jnp.where(lines > 0, lines - 1, G)
    lines_other = lax.ppermute(lines, "chan", [(0, 1), (1, 0)])
    first = jnp.where(chan == 0, lines, lines_other)
    second = jnp.where(chan == 0, lines_other, lines)
    all_lines = jnp.stack([first, second], axis=1).reshape(512)

    dy = jnp.asarray(np.concatenate([cos.T, -sin.T, -cos.T], axis=0), BF)
    dz = jnp.asarray(np.concatenate([cos.T, sin.T], axis=1), BF)
    latent, spectra = call(
        forward_kernel,
        (jax.ShapeDtypeStruct((G * HALF, G), BF), jax.ShapeDtypeStruct((M * M, 128), BF)),
        [SM] + [VM] * 3,
        [pltpu.VMEM(((G + 1) * HALF, G), F32), pltpu.VMEM((3 * M * HALF, G), F32)],
        (VM, VM),
    )(all_lines, parts, dy, dz)
    latent_other = lax.ppermute(latent, "chan", [(0, 1), (1, 0)])
    spectra = lax.all_to_all(spectra.reshape(256, 4, 128), every, split_axis=0, concat_axis=0, tiled=True)

    eye4, eye2 = np.eye(4), np.eye(2)
    table = np.stack([cos.T, sin.T])
    forward = np.einsum("hg,vkx,mn->hvkmxgn", eye2, table, eye4).reshape(512, 1024)
    weight = jnp.transpose(spec_weight, (0, 1, 3, 4, 2)).reshape(2, C, 128, C)
    back = call(
        mix_kernel,
        jax.ShapeDtypeStruct((1024, 128), BF),
        [VM] * 4,
        [pltpu.VMEM((2, 128, C), F32), pltpu.VMEM((512, 128), BF)],
    )(spectra.reshape(1024, 128), weight, jnp.asarray(forward, BF), jnp.asarray(forward.T, BF))
    back = lax.all_to_all(back.reshape(256, 4, 128), every, split_axis=0, concat_axis=0, tiled=True)

    own = chan * HALF
    other = (1 - chan) * HALF
    skip_own = lax.dynamic_slice_in_dim(skip_w, own, HALF, 1)
    skip = jnp.concatenate(
        [
            lax.dynamic_slice_in_dim(skip_own, own, HALF, 0),
            lax.dynamic_slice_in_dim(skip_own, other, HALF, 0),
        ],
        axis=0,
    ).T
    bias = jnp.broadcast_to(lax.dynamic_slice_in_dim(skip_bias, own, HALF, 0)[:, None], (HALF, G))
    ez = jnp.asarray(np.concatenate([cos.T, sin.T], axis=1), BF)
    ey = jnp.asarray(np.stack([cos, -sin], axis=2).reshape(G, 2 * M) / G**3, BF)
    grid = call(
        inverse_kernel,
        jax.ShapeDtypeStruct((G * HALF, G), BF),
        [VM] * 7,
        [pltpu.VMEM((M * C, G), F32), pltpu.VMEM((G * HALF, G), F32)],
    )(back.reshape(1024, 128), latent, latent_other, skip, bias, ez, ey)
    grid_other = lax.ppermute(grid, "chan", [(0, 1), (1, 0)])

    proj = jnp.concatenate(
        [
            lax.dynamic_slice_in_dim(proj_in, own, HALF, 0),
            lax.dynamic_slice_in_dim(proj_in, other, HALF, 0),
        ],
        axis=0,
    ).T
    proj_row = jnp.broadcast_to(proj_out[None, :], (8, 128))
    values = call(
        decode_kernel,
        jax.ShapeDtypeStruct((256, PB), F32),
        [SM] + [VM] * 5,
        [pltpu.SMEM((257,), jnp.int32)],
    )(lines.reshape(256), meta, grid, grid_other, proj, proj_row)
    values = lax.all_to_all(values.reshape(128, 2, PB), "slab", split_axis=0, concat_axis=0, tiled=True)
    return call(unpack_kernel, jax.ShapeDtypeStruct((128, PB), F32), [SM, VM])(slot, values.reshape(256, PB))


def solution(mesh):
    placed = (
        P(("slab", "chan"), None, None),
        P(("slab", "chan"), None),
        P(("slab", "chan"), None, None),
        P(("slab", "chan"), None),
        P(("slab", "chan")),
        P(("slab", "chan")),
        P(),
        P(None, None, None, None, ("slab", "chan")),
        P(),
        P(),
        P(),
        P(),
    )
    return jax.shard_map(
        shards, mesh=mesh, in_specs=placed, out_specs=P(("slab", "chan"), None), check_vma=False
    )
```

```python
import math

import jax
import jax.numpy as jnp
import numpy as np
from jax import lax
from jax.experimental import pallas as pl
from jax.experimental.pallas import tpu as pltpu
from jax.sharding import PartitionSpec as P

G = 128
M = 32
PB = 128
NB = 8
C = 64
HALF = 32
BF = jnp.bfloat16
F32 = jnp.float32
LIMIT = 48 * 1024 * 1024
VM = pl.BlockSpec(memory_space=pltpu.VMEM)
SM = pl.BlockSpec(memory_space=pltpu.SMEM)
WIDE = 16


def trig():
    modes = np.concatenate([np.arange(M // 2), np.arange(M // 2) - M // 2])
    phase = (np.arange(G)[:, None] * modes[None, :] % G) * (2.0 * math.pi / G)
    return np.cos(phase), np.sin(phase)


def call(kernel, out_shape, in_specs, scratch=(), out_specs=None):
    return pl.pallas_call(
        kernel,
        out_shape=out_shape,
        in_specs=in_specs,
        out_specs=VM if out_specs is None else out_specs,
        scratch_shapes=list(scratch),
        compiler_params=pltpu.CompilerParams(vmem_limit_bytes=LIMIT),
    )


def dot(left, right, dims=((1,), (0,))):
    return lax.dot_general(left, right, (dims, ((), ())), preferred_element_type=F32)


def gelu(x):
    inner = x * (0.7978845608028654 + 0.035677408136300125 * (x * x))
    half = 0.5 * x
    return half + half * jnp.tanh(inner)


def near_transposed(start, weight):
    base = lax.broadcasted_iota(jnp.int32, (NB, PB), 0) - start
    which = base & 7
    tile = -(base >> 3)
    picked = jnp.zeros((NB, PB), F32)
    for j in range(NB):
        picked = jnp.where(which == j, weight[j : j + 1, :], picked)
    rows = [jnp.where(tile == t, picked, 0.0) for t in range(G // NB)]
    return jnp.concatenate(rows, axis=0).astype(BF)


def pack_kernel(blk_ref, line_ref, start_ref, weight_ref, out_ref):
    row = lax.broadcasted_iota(jnp.int32, (8, PB), 0)

    def step(s, carry):
        b0, b1 = blk_ref[2 * s], blk_ref[2 * s + 1]
        c0, c1 = jnp.maximum(b0, 0), jnp.maximum(b1, 0)
        l0 = jnp.where(b0 >= 0, line_ref[c0] + 1, 0)
        l1 = jnp.where(b1 >= 0, line_ref[c1] + 1, 0)
        info = jnp.where(
            row == 0,
            start_ref[pl.ds(c0, 1), :],
            jnp.where(
                row == 1,
                start_ref[pl.ds(c1, 1), :],
                jnp.where(row == 2, l0, jnp.where(row == 3, l1, 0)),
            ),
        )
        out_ref[s, 0:8, :] = weight_ref[c0]
        out_ref[s, 8:16, :] = weight_ref[c1]
        out_ref[s, 16:24, :] = info.astype(F32).astype(BF)
        return carry

    lax.fori_loop(0, G, step, 0)


def encode_kernel(slot_ref, count_ref, points_ref, start_ref, weight_ref, lift_ref, out_ref):
    count = count_ref[0]

    def step(group, carry):
        blocks = [jnp.minimum(group * WIDE + u, count - 1) for u in range(WIDE)]
        nears = [
            near_transposed(start_ref[pl.ds(b, 1), :], weight_ref[b].astype(F32)) for b in blocks
        ]
        points = jnp.concatenate([points_ref[b] for b in blocks], axis=1)
        lifted = dot(lift_ref[...], points).astype(BF)
        for u in range(WIDE):
            slot = slot_ref[blocks[u]]
            slab, rank = slot >> 1, slot & 1
            part = dot(lifted[:, u * PB : (u + 1) * PB], nears[u], ((1,), (1,))).astype(BF)
            out_ref[2 * slab, rank] = part[:HALF]
            out_ref[2 * slab + 1, rank] = part[HALF:]
        return carry

    lax.fori_loop(0, (count + WIDE - 1) // WIDE, step, 0)


def forward_kernel(line_ref, parts_ref, dy_ref, dz_ref, latent_ref, spec_ref, acc, ybuf):
    acc[...] = jnp.zeros_like(acc)

    def add(src, carry):
        for r in range(2):
            line = line_ref[2 * src + r]
            rows = pl.ds(pl.multiple_of(line * HALF, HALF), HALF)
            acc[rows, :] += parts_ref[src, r].astype(F32)
        return carry

    lax.fori_loop(0, 256, add, 0)
    latent_ref[...] = acc[0 : G * HALF, :].astype(BF)
    for c in range(HALF):
        plane = acc[pl.ds(c, G, stride=HALF), :].astype(BF)
        ybuf[pl.ds(c, 3 * M, stride=HALF), :] = dot(dy_ref[...], plane)
    for q in range(M):
        real = ybuf[q * HALF : (q + 1) * HALF, :].astype(BF)
        imag = ybuf[(M + q) * HALF : (M + q + 1) * HALF, :].astype(BF)
        minus = ybuf[(2 * M + q) * HALF : (2 * M + q + 1) * HALF, :].astype(BF)
        first = jnp.concatenate([real, imag, imag, minus], axis=0)
        second = jnp.concatenate([imag, minus, minus, -imag], axis=0)
        both = jnp.concatenate([first, second], axis=1)
        spec_ref[q * M : (q + 1) * M, :] = dot(dz_ref[...], both, ((1,), (1,))).astype(BF)


def mix_kernel(spec_ref, weight_ref, fwd_ref, bwd_ref, out_ref, xbuf, rhs):
    prod = dot(fwd_ref[...], spec_ref[...])
    for h in range(2):
        cos = prod[h * 256 : h * 256 + 128, 0:64]
        sin = prod[h * 256 + 128 : h * 256 + 256, 64:128]
        xbuf[h] = cos + sin

    def chunk(t, carry):
        rows = pl.ds(pl.multiple_of(t * 32, 32), 32)
        real = jnp.zeros((32, C), F32)
        imag = jnp.zeros((32, C), F32)
        for h in range(2):
            x = xbuf[h, rows, :]
            for c in range(HALF):
                wr = weight_ref[0, h * HALF + c, rows, :].astype(F32)
                wi = weight_ref[1, h * HALF + c, rows, :].astype(F32)
                xr = x[:, c : c + 1]
                xi = x[:, HALF + c : HALF + c + 1]
                real = real + xr * wr - xi * wi
                imag = imag + xr * wi + xi * wr
        for h in range(2):
            mr = real[:, h * HALF : (h + 1) * HALF]
            mi = imag[:, h * HALF : (h + 1) * HALF]
            top = jnp.concatenate([mr, mi, -mi, mr], axis=1).astype(BF)
            low = jnp.concatenate([-mi, mr, -mr, -mi], axis=1).astype(BF)
            rhs[pl.ds(pl.multiple_of(h * 256 + t * 32, 32), 32), :] = top
            rhs[pl.ds(pl.multiple_of(h * 256 + 128 + t * 32, 32), 32), :] = low
        return carry

    lax.fori_loop(0, 4, chunk, 0)
    out_ref[...] = dot(bwd_ref[...], rhs[...]).astype(BF)


def inverse_kernel(back_ref, own_ref, other_ref, skip_ref, bias_ref, ez_ref, ey_ref, out_ref, ubuf, sbuf):
    for q in range(M):
        both = dot(back_ref[q * M : (q + 1) * M, :], ez_ref[...], ((0,), (0,)))
        ubuf[q * C : (q + 1) * C, :] = both[0:C, 0:G] + both[C : 2 * C, G : 2 * G]
    for c in range(HALF):
        lines = ubuf[pl.ds(c, 2 * M, stride=HALF), :].astype(BF)
        sbuf[pl.ds(c, G, stride=HALF), :] = dot(ey_ref[...], lines)

    def step(group, carry):
        for u in range(4):
            rows = pl.ds(pl.multiple_of((group * 4 + u) * HALF, HALF), HALF)
            latent = jnp.concatenate([own_ref[rows, :], other_ref[rows, :]], axis=0)
            total = sbuf[rows, :] + dot(skip_ref[...], latent) + bias_ref[...]
            out_ref[rows, :] = gelu(total).astype(BF)
        return carry

    lax.fori_loop(0, G // 4, step, 0)


def decode_kernel(line_ref, meta_ref, own_ref, other_ref, proj_in_ref, proj_out_ref, out_ref, todo):
    def collect(s, count):
        todo[count] = s
        return count + jnp.where(line_ref[s] < G, 1, 0)

    count = lax.fori_loop(0, 256, collect, 0)

    def step(group, carry):
        slots, cells, nears = [], [], []
        for u in range(WIDE):
            s = todo[jnp.minimum(group * WIDE + u, count - 1)]
            src, rank = s >> 1, s & 1
            rows = pl.ds(pl.multiple_of(line_ref[s] * HALF, HALF), HALF)
            info = meta_ref[src, 16:24, :].astype(F32)
            start = jnp.where(rank == 0, info[0:1, :], info[1:2, :]).astype(jnp.int32)
            weight = meta_ref[src, pl.ds(pl.multiple_of(rank * 8, 8), 8), :].astype(F32)
            slots.append(s)
            cells.append(jnp.concatenate([own_ref[rows, :], other_ref[rows, :]], axis=0))
            nears.append(near_transposed(start, weight))
        values = [dot(cells[u], nears[u]).astype(BF) for u in range(WIDE)]
        hidden = gelu(dot(proj_in_ref[...], jnp.concatenate(values, axis=1))).astype(BF)
        result = dot(proj_out_ref[...], hidden)
        for u in range(WIDE):
            out_ref[pl.ds(slots[u], 1), :] = result[0:1, u * PB : (u + 1) * PB]
        return carry

    lax.fori_loop(0, (count + WIDE - 1) // WIDE, step, 0)


def unpack_kernel(slot_ref, values_ref, out_ref):
    def step(b, carry):
        slot = slot_ref[b]
        row = values_ref[pl.ds(jnp.maximum(slot, 0), 1), :]
        out_ref[pl.ds(b, 1), :] = jnp.where(slot >= 0, row, 0.0)
        return carry

    lax.fori_loop(0, 128, step, 0, unroll=8)


def shards(
    points,
    near_start,
    near_weight,
    dest_slab,
    dest_block,
    live_count,
    lift_w,
    spec_weight,
    skip_w,
    skip_bias,
    proj_in,
    proj_out,
):
    cos, sin = trig()
    chan = lax.axis_index("chan")
    every = ("slab", "chan")

    ids = jnp.arange(128, dtype=jnp.int32)
    live = ids < live_count[0]
    target = jnp.where(live, dest_slab[:, 0], -1)
    same = (target[:, None] == target[None, :]) & (ids[None, :] < ids[:, None])
    rank = jnp.sum(same.astype(jnp.int32), axis=1)
    slot = jnp.where(live, target * 2 + rank, -1)
    slot_ids = jnp.arange(256, dtype=jnp.int32)
    block = jnp.max(jnp.where(slot[None, :] == slot_ids[:, None], ids[None, :], -1), axis=1)

    meta = call(pack_kernel, jax.ShapeDtypeStruct((128, 24, PB), BF), [SM, SM, VM, VM])(
        block, dest_block, near_start, near_weight
    )
    meta = lax.all_to_all(meta, "slab", split_axis=0, concat_axis=0, tiled=True)
    parts = call(encode_kernel, jax.ShapeDtypeStruct((256, 2, HALF, G), BF), [SM, SM] + [VM] * 4)(
        slot, live_count, points, near_start, near_weight, lift_w.T
    )
    parts = lax.all_to_all(parts, every, split_axis=0, concat_axis=0, tiled=True)

    lines = meta[:, 18:20, 0].astype(jnp.int32)
    lines = jnp.where(lines > 0, lines - 1, G)
    lines_other = lax.ppermute(lines, "chan", [(0, 1), (1, 0)])
    first = jnp.where(chan == 0, lines, lines_other)
    second = jnp.where(chan == 0, lines_other, lines)
    all_lines = jnp.stack([first, second], axis=1).reshape(512)

    dy = jnp.asarray(np.concatenate([cos.T, -sin.T, -cos.T], axis=0), BF)
    dz = jnp.asarray(np.concatenate([cos.T, sin.T], axis=1), BF)
    latent, spectra = call(
        forward_kernel,
        (jax.ShapeDtypeStruct((G * HALF, G), BF), jax.ShapeDtypeStruct((M * M, 128), BF)),
        [SM] + [VM] * 3,
        [pltpu.VMEM(((G + 1) * HALF, G), F32), pltpu.VMEM((3 * M * HALF, G), F32)],
        (VM, VM),
    )(all_lines, parts, dy, dz)
    latent_other = lax.ppermute(latent, "chan", [(0, 1), (1, 0)])
    spectra = lax.all_to_all(spectra.reshape(256, 4, 128), every, split_axis=0, concat_axis=0, tiled=True)

    eye4, eye2 = np.eye(4), np.eye(2)
    table = np.stack([cos.T, sin.T])
    forward = np.einsum("hg,vkx,mn->hvkmxgn", eye2, table, eye4).reshape(512, 1024)
    weight = jnp.transpose(spec_weight, (0, 1, 3, 4, 2)).reshape(2, C, 128, C)
    back = call(
        mix_kernel,
        jax.ShapeDtypeStruct((1024, 128), BF),
        [VM] * 4,
        [pltpu.VMEM((2, 128, C), F32), pltpu.VMEM((512, 128), BF)],
    )(spectra.reshape(1024, 128), weight, jnp.asarray(forward, BF), jnp.asarray(forward.T, BF))
    back = lax.all_to_all(back.reshape(256, 4, 128), every, split_axis=0, concat_axis=0, tiled=True)

    own = chan * HALF
    other = (1 - chan) * HALF
    skip_own = lax.dynamic_slice_in_dim(skip_w, own, HALF, 1)
    skip = jnp.concatenate(
        [
            lax.dynamic_slice_in_dim(skip_own, own, HALF, 0),
            lax.dynamic_slice_in_dim(skip_own, other, HALF, 0),
        ],
        axis=0,
    ).T
    bias = jnp.broadcast_to(lax.dynamic_slice_in_dim(skip_bias, own, HALF, 0)[:, None], (HALF, G))
    ez = jnp.asarray(np.concatenate([cos.T, sin.T], axis=1), BF)
    ey = jnp.asarray(np.stack([cos, -sin], axis=2).reshape(G, 2 * M) / G**3, BF)
    grid = call(
        inverse_kernel,
        jax.ShapeDtypeStruct((G * HALF, G), BF),
        [VM] * 7,
        [pltpu.VMEM((M * C, G), F32), pltpu.VMEM((G * HALF, G), F32)],
    )(back.reshape(1024, 128), latent, latent_other, skip, bias, ez, ey)
    grid_other = lax.ppermute(grid, "chan", [(0, 1), (1, 0)])

    proj = jnp.concatenate(
        [
            lax.dynamic_slice_in_dim(proj_in, own, HALF, 0),
            lax.dynamic_slice_in_dim(proj_in, other, HALF, 0),
        ],
        axis=0,
    ).T
    proj_row = jnp.broadcast_to(proj_out[None, :], (8, 128))
    values = call(
        decode_kernel,
        jax.ShapeDtypeStruct((256, PB), F32),
        [SM] + [VM] * 5,
        [pltpu.SMEM((257,), jnp.int32)],
    )(lines.reshape(256), meta, grid, grid_other, proj, proj_row)
    values = lax.all_to_all(values.reshape(128, 2, PB), "slab", split_axis=0, concat_axis=0, tiled=True)
    return call(unpack_kernel, jax.ShapeDtypeStruct((128, PB), F32), [SM, VM])(slot, values.reshape(256, PB))


def solution(mesh):
    placed = (
        P(("slab", "chan"), None, None),
        P(("slab", "chan"), None),
        P(("slab", "chan"), None, None),
        P(("slab", "chan"), None),
        P(("slab", "chan")),
        P(("slab", "chan")),
        P(),
        P(None, None, None, None, ("slab", "chan")),
        P(),
        P(),
        P(),
        P(),
    )
    return jax.shard_map(
        shards, mesh=mesh, in_specs=placed, out_specs=P(("slab", "chan"), None), check_vma=False
    )
```

```python
import math

import jax
import jax.numpy as jnp
import numpy as np
from jax import lax
from jax.experimental import pallas as pl
from jax.experimental.pallas import tpu as pltpu
from jax.sharding import PartitionSpec as P

G = 128
M = 32
PB = 128
NB = 8
C = 64
HALF = 32
BF = jnp.bfloat16
F32 = jnp.float32
LIMIT = 48 * 1024 * 1024
VM = pl.BlockSpec(memory_space=pltpu.VMEM)
SM = pl.BlockSpec(memory_space=pltpu.SMEM)
WIDE = 16
ROWS = 152


def trig():
    modes = np.concatenate([np.arange(M // 2), np.arange(M // 2) - M // 2])
    phase = (np.arange(G)[:, None] * modes[None, :] % G) * (2.0 * math.pi / G)
    return np.cos(phase), np.sin(phase)


def call(kernel, out_shape, in_specs, scratch=(), out_specs=None):
    return pl.pallas_call(
        kernel,
        out_shape=out_shape,
        in_specs=in_specs,
        out_specs=VM if out_specs is None else out_specs,
        scratch_shapes=list(scratch),
        compiler_params=pltpu.CompilerParams(vmem_limit_bytes=LIMIT),
    )


def dot(left, right, dims=((1,), (0,))):
    return lax.dot_general(left, right, (dims, ((), ())), preferred_element_type=F32)


def gelu(x):
    inner = x * (0.7978845608028654 + 0.035677408136300125 * (x * x))
    half = 0.5 * x
    return half + half * jnp.tanh(inner)


def near_transposed(start, weight):
    base = lax.broadcasted_iota(jnp.int32, (NB, PB), 0) - start
    which = base & 7
    tile = -(base >> 3)
    picked = jnp.zeros((NB, PB), F32)
    for j in range(NB):
        picked = jnp.where(which == j, weight[j : j + 1, :], picked)
    rows = [jnp.where(tile == t, picked, 0.0) for t in range(G // NB)]
    return jnp.concatenate(rows, axis=0).astype(BF)


def dispatch_kernel(
    blk_ref, line_ref, points_ref, start_ref, weight_ref, lift_ref, out_ref, stage, send_sem, recv_sem, own_sem
):
    me, chan = lax.axis_index("slab"), lax.axis_index("chan")
    x, z, y = me // 32, (me // 4) % 8, me % 4
    barrier = pltpu.get_barrier_semaphore()

    def greet(i, carry):
        pl.semaphore_signal(
            barrier, inc=1, device_id=((me + i) % G, chan), device_id_type=pl.DeviceIdType.MESH
        )
        return carry

    lax.fori_loop(1, G, greet, 0)
    pl.semaphore_wait(barrier, G - 1)
    row = lax.broadcasted_iota(jnp.int32, (8, PB), 0)

    def group(g, carry):
        line_x = (x + g // 4) % 4 * 32 + (y + g % 4) % 4
        targets, blocks, nears = [], [], []
        for j in range(8):
            hop = (j + 1) // 2
            target = line_x + (z + (4 + hop if j % 2 else 4 - hop)) % 8 * 4
            found = [blk_ref[2 * target + r] for r in range(2)]
            taken = [jnp.maximum(b, 0) for b in found]
            lines = [jnp.where(b >= 0, line_ref[c] + 1, 0) for b, c in zip(found, taken)]
            starts = [start_ref[pl.ds(c, 1), :] for c in taken]
            info = jnp.where(row == 2, lines[0], jnp.where(row == 3, lines[1], 0))
            info = jnp.where(row == 0, starts[0], jnp.where(row == 1, starts[1], info))
            weights = [weight_ref[c] for c in taken]
            stage[g * 8 + j, 128:136, :] = weights[0]
            stage[g * 8 + j, 136:144, :] = weights[1]
            stage[g * 8 + j, 144:152, :] = info.astype(F32).astype(BF)
            targets.append(target)
            blocks.extend(taken)
            nears.extend(near_transposed(s, w.astype(F32)) for s, w in zip(starts, weights))
        points = jnp.concatenate([points_ref[b] for b in blocks], axis=1)
        lifted = dot(lift_ref[...], points).astype(BF)
        for j in range(8):
            for r in range(2):
                u = 2 * j + r
                part = dot(lifted[:, u * PB : (u + 1) * PB], nears[u], ((1,), (1,)))
                stage[g * 8 + j, r * C : (r + 1) * C, :] = part.astype(BF)
        for j in range(8):
            copy = pltpu.make_async_remote_copy(
                src_ref=stage.at[g * 8 + j],
                dst_ref=out_ref.at[me],
                send_sem=send_sem,
                recv_sem=recv_sem,
                device_id=(targets[j], chan),
                device_id_type=pl.DeviceIdType.MESH,
            )
            if j < 7:
                copy.start()
            else:
                pl.when(g > 0)(copy.start)
        return carry

    lax.fori_loop(0, 16, group, 0)
    own = pltpu.make_async_copy(stage.at[7], out_ref.at[me], own_sem)
    own.start()
    own.wait()
    sent = stage.at[pl.ds(0, G - 1)]
    pltpu.make_async_copy(sent, sent, send_sem).wait()
    got = out_ref.at[pl.ds(0, G - 1)]
    pltpu.make_async_copy(got, got, recv_sem).wait()


def gather_kernel(chan_ref, line_ref, parts_ref, own_ref, other_ref, acc):
    acc[...] = jnp.zeros_like(acc)

    def add(src, carry):
        for r in range(2):
            line = line_ref[2 * src + r]
            rows = pl.ds(pl.multiple_of(line * HALF, HALF), HALF)
            for h in range(2):
                first = r * C + h * HALF
                acc[h, rows, :] += parts_ref[src, first : first + HALF, :].astype(F32)
        return carry

    lax.fori_loop(0, G, add, 0)
    chan = chan_ref[0]
    own_ref[...] = acc[chan, 0 : G * HALF, :]
    other_ref[...] = acc[1 - chan, 0 : G * HALF, :].astype(BF)


def forward_kernel(own_ref, other_ref, dy_ref, dz_ref, latent_ref, spec_ref, acc, ybuf):
    acc[...] = own_ref[...] + other_ref[...].astype(F32)
    latent_ref[...] = acc[...].astype(BF)
    for c in range(HALF):
        plane = acc[pl.ds(c, G, stride=HALF), :].astype(BF)
        ybuf[pl.ds(c, 3 * M, stride=HALF), :] = dot(dy_ref[...], plane)
    for q in range(M):
        real = ybuf[q * HALF : (q + 1) * HALF, :].astype(BF)
        imag = ybuf[(M + q) * HALF : (M + q + 1) * HALF, :].astype(BF)
        minus = ybuf[(2 * M + q) * HALF : (2 * M + q + 1) * HALF, :].astype(BF)
        first = jnp.concatenate([real, imag, imag, minus], axis=0)
        second = jnp.concatenate([imag, minus, minus, -imag], axis=0)
        both = jnp.concatenate([first, second], axis=1)
        spec_ref[q * M : (q + 1) * M, :] = dot(dz_ref[...], both, ((1,), (1,))).astype(BF)


def mix_kernel(spec_ref, weight_ref, fwd_ref, bwd_ref, out_ref, xbuf, rhs):
    prod = dot(fwd_ref[...], spec_ref[...])
    for h in range(2):
        cos = prod[h * 256 : h * 256 + 128, 0:64]
        sin = prod[h * 256 + 128 : h * 256 + 256, 64:128]
        xbuf[h] = cos + sin

    def chunk(t, carry):
        rows = pl.ds(pl.multiple_of(t * 32, 32), 32)
        real = jnp.zeros((32, C), F32)
        imag = jnp.zeros((32, C), F32)
        for h in range(2):
            x = xbuf[h, rows, :]
            for c in range(HALF):
                wr = weight_ref[0, h * HALF + c, rows, :].astype(F32)
                wi = weight_ref[1, h * HALF + c, rows, :].astype(F32)
                xr = x[:, c : c + 1]
                xi = x[:, HALF + c : HALF + c + 1]
                real = real + xr * wr - xi * wi
                imag = imag + xr * wi + xi * wr
        for h in range(2):
            mr = real[:, h * HALF : (h + 1) * HALF]
            mi = imag[:, h * HALF : (h + 1) * HALF]
            top = jnp.concatenate([mr, mi, -mi, mr], axis=1).astype(BF)
            low = jnp.concatenate([-mi, mr, -mr, -mi], axis=1).astype(BF)
            rhs[pl.ds(pl.multiple_of(h * 256 + t * 32, 32), 32), :] = top
            rhs[pl.ds(pl.multiple_of(h * 256 + 128 + t * 32, 32), 32), :] = low
        return carry

    lax.fori_loop(0, 4, chunk, 0)
    out_ref[...] = dot(bwd_ref[...], rhs[...]).astype(BF)


def inverse_kernel(back_ref, own_ref, other_ref, skip_ref, bias_ref, ez_ref, ey_ref, out_ref, ubuf, sbuf):
    for q in range(M):
        both = dot(back_ref[q * M : (q + 1) * M, :], ez_ref[...], ((0,), (0,)))
        ubuf[q * C : (q + 1) * C, :] = both[0:C, 0:G] + both[C : 2 * C, G : 2 * G]
    for c in range(HALF):
        lines = ubuf[pl.ds(c, 2 * M, stride=HALF), :].astype(BF)
        sbuf[pl.ds(c, G, stride=HALF), :] = dot(ey_ref[...], lines)

    def step(group, carry):
        for u in range(4):
            rows = pl.ds(pl.multiple_of((group * 4 + u) * HALF, HALF), HALF)
            latent = jnp.concatenate([own_ref[rows, :], other_ref[rows, :]], axis=0)
            total = sbuf[rows, :] + dot(skip_ref[...], latent) + bias_ref[...]
            out_ref[rows, :] = gelu(total).astype(BF)
        return carry

    lax.fori_loop(0, G // 4, step, 0)


def decode_kernel(line_ref, meta_ref, own_ref, other_ref, proj_in_ref, proj_out_ref, out_ref, todo):
    def collect(s, count):
        todo[count] = s
        return count + jnp.where(line_ref[s] < G, 1, 0)

    count = lax.fori_loop(0, 256, collect, 0)

    def step(group, carry):
        slots, cells, nears = [], [], []
        for u in range(WIDE):
            s = todo[jnp.minimum(group * WIDE + u, count - 1)]
            src, rank = s >> 1, s & 1
            rows = pl.ds(pl.multiple_of(line_ref[s] * HALF, HALF), HALF)
            info = meta_ref[src, 16:24, :].astype(F32)
            start = jnp.where(rank == 0, info[0:1, :], info[1:2, :]).astype(jnp.int32)
            weight = meta_ref[src, pl.ds(pl.multiple_of(rank * 8, 8), 8), :].astype(F32)
            slots.append(s)
            cells.append(jnp.concatenate([own_ref[rows, :], other_ref[rows, :]], axis=0))
            nears.append(near_transposed(start, weight))
        values = [dot(cells[u], nears[u]).astype(BF) for u in range(WIDE)]
        hidden = gelu(dot(proj_in_ref[...], jnp.concatenate(values, axis=1))).astype(BF)
        result = dot(proj_out_ref[...], hidden)
        for u in range(WIDE):
            out_ref[pl.ds(slots[u], 1), :] = result[0:1, u * PB : (u + 1) * PB]
        return carry

    lax.fori_loop(0, (count + WIDE - 1) // WIDE, step, 0)


def unpack_kernel(slot_ref, values_ref, out_ref):
    def step(b, carry):
        slot = slot_ref[b]
        row = values_ref[pl.ds(jnp.maximum(slot, 0), 1), :]
        out_ref[pl.ds(b, 1), :] = jnp.where(slot >= 0, row, 0.0)
        return carry

    lax.fori_loop(0, 128, step, 0, unroll=8)


def shards(
    points,
    near_start,
    near_weight,
    dest_slab,
    dest_block,
    live_count,
    lift_w,
    spec_weight,
    skip_w,
    skip_bias,
    proj_in,
    proj_out,
):
    cos, sin = trig()
    chan = lax.axis_index("chan")
    every = ("slab", "chan")

    ids = jnp.arange(128, dtype=jnp.int32)
    live = ids < live_count[0]
    target = jnp.where(live, dest_slab[:, 0], -1)
    same = (target[:, None] == target[None, :]) & (ids[None, :] < ids[:, None])
    rank = jnp.sum(same.astype(jnp.int32), axis=1)
    slot = jnp.where(live, target * 2 + rank, -1)
    slot_ids = jnp.arange(256, dtype=jnp.int32)
    block = jnp.max(jnp.where(slot[None, :] == slot_ids[:, None], ids[None, :], -1), axis=1)

    parts = pl.pallas_call(
        dispatch_kernel,
        out_shape=jax.ShapeDtypeStruct((G, ROWS, PB), BF),
        in_specs=[SM, SM] + [VM] * 4,
        out_specs=pl.BlockSpec(memory_space=pl.ANY),
        scratch_shapes=[pltpu.VMEM((G, ROWS, PB), BF)] + [pltpu.SemaphoreType.DMA] * 3,
        compiler_params=pltpu.CompilerParams(
            vmem_limit_bytes=LIMIT, collective_id=0, has_side_effects=True
        ),
    )(block, dest_block, points, near_start, near_weight, lift_w.T)
    meta = parts[:, 128:152, :]
    lines = meta[:, 18:20, 0].astype(jnp.int32)
    lines = jnp.where(lines > 0, lines - 1, G).reshape(256)
    mine, theirs = call(
        gather_kernel,
        (jax.ShapeDtypeStruct((G * HALF, G), F32), jax.ShapeDtypeStruct((G * HALF, G), BF)),
        [SM, SM, VM],
        [pltpu.VMEM((2, (G + 1) * HALF, G), F32)],
        (VM, VM),
    )(chan.reshape(1), lines, parts)
    received = lax.ppermute(theirs, "chan", [(0, 1), (1, 0)])

    dy = jnp.asarray(np.concatenate([cos.T, -sin.T, -cos.T], axis=0), BF)
    dz = jnp.asarray(np.concatenate([cos.T, sin.T], axis=1), BF)
    latent, spectra = call(
        forward_kernel,
        (jax.ShapeDtypeStruct((G * HALF, G), BF), jax.ShapeDtypeStruct((M * M, 128), BF)),
        [VM] * 4,
        [pltpu.VMEM((G * HALF, G), F32), pltpu.VMEM((3 * M * HALF, G), F32)],
        (VM, VM),
    )(mine, received, dy, dz)
    latent_other = lax.ppermute(latent, "chan", [(0, 1), (1, 0)])
    spectra = lax.all_to_all(spectra.reshape(256, 4, 128), every, split_axis=0, concat_axis=0, tiled=True)

    eye4, eye2 = np.eye(4), np.eye(2)
    table = np.stack([cos.T, sin.T])
    forward = np.einsum("hg,vkx,mn->hvkmxgn", eye2, table, eye4).reshape(512, 1024)
    weight = jnp.transpose(spec_weight, (0, 1, 3, 4, 2)).reshape(2, C, 128, C)
    back = call(
        mix_kernel,
        jax.ShapeDtypeStruct((1024, 128), BF),
        [VM] * 4,
        [pltpu.VMEM((2, 128, C), F32), pltpu.VMEM((512, 128), BF)],
    )(spectra.reshape(1024, 128), weight, jnp.asarray(forward, BF), jnp.asarray(forward.T, BF))
    back = lax.all_to_all(back.reshape(256, 4, 128), every, split_axis=0, concat_axis=0, tiled=True)

    own = chan * HALF
    other = (1 - chan) * HALF
    skip_own = lax.dynamic_slice_in_dim(skip_w, own, HALF, 1)
    skip = jnp.concatenate(
        [
            lax.dynamic_slice_in_dim(skip_own, own, HALF, 0),
            lax.dynamic_slice_in_dim(skip_own, other, HALF, 0),
        ],
        axis=0,
    ).T
    bias = jnp.broadcast_to(lax.dynamic_slice_in_dim(skip_bias, own, HALF, 0)[:, None], (HALF, G))
    ez = jnp.asarray(np.concatenate([cos.T, sin.T], axis=1), BF)
    ey = jnp.asarray(np.stack([cos, -sin], axis=2).reshape(G, 2 * M) / G**3, BF)
    grid = call(
        inverse_kernel,
        jax.ShapeDtypeStruct((G * HALF, G), BF),
        [VM] * 7,
        [pltpu.VMEM((M * C, G), F32), pltpu.VMEM((G * HALF, G), F32)],
    )(back.reshape(1024, 128), latent, latent_other, skip, bias, ez, ey)
    grid_other = lax.ppermute(grid, "chan", [(0, 1), (1, 0)])

    proj = jnp.concatenate(
        [
            lax.dynamic_slice_in_dim(proj_in, own, HALF, 0),
            lax.dynamic_slice_in_dim(proj_in, other, HALF, 0),
        ],
        axis=0,
    ).T
    proj_row = jnp.broadcast_to(proj_out[None, :], (8, 128))
    values = call(
        decode_kernel,
        jax.ShapeDtypeStruct((256, PB), F32),
        [SM] + [VM] * 5,
        [pltpu.SMEM((257,), jnp.int32)],
    )(lines, meta, grid, grid_other, proj, proj_row)
    values = lax.all_to_all(values.reshape(128, 2, PB), "slab", split_axis=0, concat_axis=0, tiled=True)
    return call(unpack_kernel, jax.ShapeDtypeStruct((128, PB), F32), [SM, VM])(slot, values.reshape(256, PB))


def solution(mesh):
    placed = (
        P(("slab", "chan"), None, None),
        P(("slab", "chan"), None),
        P(("slab", "chan"), None, None),
        P(("slab", "chan"), None),
        P(("slab", "chan")),
        P(("slab", "chan")),
        P(),
        P(None, None, None, None, ("slab", "chan")),
        P(),
        P(),
        P(),
        P(),
    )
    return jax.shard_map(
        shards, mesh=mesh, in_specs=placed, out_specs=P(("slab", "chan"), None), check_vma=False
    )
```

```python
import math

import jax
import jax.numpy as jnp
import numpy as np
from jax import lax
from jax.experimental import pallas as pl
from jax.experimental.pallas import tpu as pltpu
from jax.sharding import PartitionSpec as P

G = 128
M = 32
PB = 128
NB = 8
C = 64
HALF = 32
BF = jnp.bfloat16
F32 = jnp.float32
LIMIT = 48 * 1024 * 1024
VM = pl.BlockSpec(memory_space=pltpu.VMEM)
SM = pl.BlockSpec(memory_space=pltpu.SMEM)
WIDE = 16
ROWS = 152


def trig():
    modes = np.concatenate([np.arange(M // 2), np.arange(M // 2) - M // 2])
    phase = (np.arange(G)[:, None] * modes[None, :] % G) * (2.0 * math.pi / G)
    return np.cos(phase), np.sin(phase)


def call(kernel, out_shape, in_specs, scratch=(), out_specs=None):
    return pl.pallas_call(
        kernel,
        out_shape=out_shape,
        in_specs=in_specs,
        out_specs=VM if out_specs is None else out_specs,
        scratch_shapes=list(scratch),
        compiler_params=pltpu.CompilerParams(vmem_limit_bytes=LIMIT),
    )


def dot(left, right, dims=((1,), (0,))):
    return lax.dot_general(left, right, (dims, ((), ())), preferred_element_type=F32)


def gelu(x):
    inner = x * (0.7978845608028654 + 0.035677408136300125 * (x * x))
    half = 0.5 * x
    return half + half * jnp.tanh(inner)


def near_transposed(start, weight):
    base = lax.broadcasted_iota(jnp.int32, (NB, PB), 0) - start
    which = base & 7
    tile = -(base >> 3)
    picked = jnp.zeros((NB, PB), F32)
    for j in range(NB):
        picked = jnp.where(which == j, weight[j : j + 1, :], picked)
    rows = [jnp.where(tile == t, picked, 0.0) for t in range(G // NB)]
    return jnp.concatenate(rows, axis=0).astype(BF)


def dispatch_kernel(
    blk_ref, line_ref, points_ref, start_ref, weight_ref, lift_ref, out_ref, stage, send_sem, recv_sem, own_sem
):
    me, chan = lax.axis_index("slab"), lax.axis_index("chan")
    x, z, y = me // 32, (me // 4) % 8, me % 4
    pl.semaphore_wait(greet_all(me, chan), G - 1)
    row = lax.broadcasted_iota(jnp.int32, (8, PB), 0)

    def group(g, carry):
        line_x = (x + g // 4) % 4 * 32 + (y + g % 4) % 4
        targets, blocks, nears = [], [], []
        for j in range(8):
            hop = (j + 1) // 2
            target = line_x + (z + (4 + hop if j % 2 else 4 - hop)) % 8 * 4
            found = [blk_ref[2 * target + r] for r in range(2)]
            taken = [jnp.maximum(b, 0) for b in found]
            lines = [jnp.where(b >= 0, line_ref[c] + 1, 0) for b, c in zip(found, taken)]
            starts = [start_ref[pl.ds(c, 1), :] for c in taken]
            info = jnp.where(row == 2, lines[0], jnp.where(row == 3, lines[1], 0))
            info = jnp.where(row == 0, starts[0], jnp.where(row == 1, starts[1], info))
            weights = [weight_ref[c] for c in taken]
            stage[g * 8 + j, 128:136, :] = weights[0]
            stage[g * 8 + j, 136:144, :] = weights[1]
            stage[g * 8 + j, 144:152, :] = info.astype(F32).astype(BF)
            targets.append(target)
            blocks.extend(taken)
            nears.extend(near_transposed(s, w.astype(F32)) for s, w in zip(starts, weights))
        points = jnp.concatenate([points_ref[b] for b in blocks], axis=1)
        lifted = dot(lift_ref[...], points).astype(BF)
        for j in range(8):
            for r in range(2):
                u = 2 * j + r
                part = dot(lifted[:, u * PB : (u + 1) * PB], nears[u], ((1,), (1,)))
                stage[g * 8 + j, r * C : (r + 1) * C, :] = part.astype(BF)
        for j in range(8):
            copy = pltpu.make_async_remote_copy(
                src_ref=stage.at[g * 8 + j],
                dst_ref=out_ref.at[me],
                send_sem=send_sem,
                recv_sem=recv_sem,
                device_id=(targets[j], chan),
                device_id_type=pl.DeviceIdType.MESH,
            )
            if j < 7:
                copy.start()
            else:
                pl.when(g > 0)(copy.start)
        return carry

    lax.fori_loop(0, 16, group, 0)
    own = pltpu.make_async_copy(stage.at[7], out_ref.at[me], own_sem)
    own.start()
    own.wait()
    sent = stage.at[pl.ds(0, G - 1)]
    pltpu.make_async_copy(sent, sent, send_sem).wait()
    got = out_ref.at[pl.ds(0, G - 1)]
    pltpu.make_async_copy(got, got, recv_sem).wait()


def gather_kernel(chan_ref, line_ref, parts_ref, own_ref, other_ref, acc):
    acc[...] = jnp.zeros_like(acc)

    def add(src, carry):
        for r in range(2):
            line = line_ref[2 * src + r]
            rows = pl.ds(pl.multiple_of(line * HALF, HALF), HALF)
            for h in range(2):
                first = r * C + h * HALF
                acc[h, rows, :] += parts_ref[src, first : first + HALF, :].astype(F32)
        return carry

    lax.fori_loop(0, G, add, 0)
    chan = chan_ref[0]
    own_ref[...] = acc[chan, 0 : G * HALF, :]
    other_ref[...] = acc[1 - chan, 0 : G * HALF, :].astype(BF)


def greet_all(me, chan):
    barrier = pltpu.get_barrier_semaphore()

    def greet(i, carry):
        pl.semaphore_signal(
            barrier, inc=1, device_id=((me + i) % G, chan), device_id_type=pl.DeviceIdType.MESH
        )
        return carry

    lax.fori_loop(1, G, greet, 0)
    return barrier


def scatter(me, chan, src, dst, send_sem, recv_sem):
    def send(i, carry):
        target = (me + i) % G
        pltpu.make_async_remote_copy(
            src_ref=src.at[target],
            dst_ref=dst.at[me],
            send_sem=send_sem,
            recv_sem=recv_sem,
            device_id=(target, chan),
            device_id_type=pl.DeviceIdType.MESH,
        ).start()
        return carry

    lax.fori_loop(1, G, send, 0)
    dst[me] = src[me]


def settle(src, dst, send_sem, recv_sem):
    sent, got = src.at[pl.ds(0, G - 1)], dst.at[pl.ds(0, G - 1)]
    pltpu.make_async_copy(sent, sent, send_sem).wait()
    pltpu.make_async_copy(got, got, recv_sem).wait()


def middle_kernel(
    mine_ref, theirs_ref, weight_ref, fwd_ref, bwd_ref, dy_ref, dz_ref, ez_ref, ey_ref, skip_ref, bias_ref,
    grid_ref, grid_other_ref,
    got, latent, latent_other, total, ybuf, spec, spec_other, send_b, recv_b, xbuf, rhs, send_c, recv_c, recv_d, ubuf,
    send_sem, recv_sem,
):
    me, chan = lax.axis_index("slab"), lax.axis_index("chan")
    barrier = greet_all(me, chan)
    pl.semaphore_signal(barrier, inc=1, device_id=(me, 1 - chan), device_id_type=pl.DeviceIdType.MESH)
    pl.semaphore_wait(barrier, G)

    def swap(src, dst, index):
        return pltpu.make_async_remote_copy(
            src_ref=src,
            dst_ref=dst,
            send_sem=send_sem.at[index],
            recv_sem=recv_sem.at[index],
            device_id=(me, 1 - chan),
            device_id_type=pl.DeviceIdType.MESH,
        )

    swap_latent = swap(theirs_ref, got, 0)
    swap_latent.start()
    swap_latent.wait()
    total[...] = mine_ref[...] + got[...].astype(F32)
    latent[...] = total[...].astype(BF)
    swap_other = swap(latent, latent_other, 1)
    swap_other.start()

    for c in range(HALF):
        plane = total[pl.ds(c, G, stride=HALF), :].astype(BF)
        ybuf[pl.ds(c, 3 * M, stride=HALF), :] = dot(dy_ref[...], plane)
    for q in range(M):
        real = ybuf[q * HALF : (q + 1) * HALF, :].astype(BF)
        imag = ybuf[(M + q) * HALF : (M + q + 1) * HALF, :].astype(BF)
        minus = ybuf[(2 * M + q) * HALF : (2 * M + q + 1) * HALF, :].astype(BF)
        first = jnp.concatenate([real, imag, imag, minus], axis=0)
        second = jnp.concatenate([imag, minus, minus, -imag], axis=0)
        both = jnp.concatenate([first, second], axis=1)
        modes = dot(dz_ref[...], both, ((1,), (1,))).astype(BF)
        spec[0, q * M : (q + 1) * M, :] = modes[:M]
        spec[1, q * M : (q + 1) * M, :] = modes[M:]

    swap_spec = swap(spec.at[1 - chan], spec_other, 2)
    swap_spec.start()
    swap_spec.wait()
    row = lax.broadcasted_iota(jnp.int32, (8, 128), 0)
    from_own = (row // 4) == chan
    for q in range(M):
        own = spec[chan, q * M : (q + 1) * M, :].astype(F32)
        other = spec_other[q * M : (q + 1) * M, :].astype(F32)
        for j in range(4):
            rows = slice(j * 8, (j + 1) * 8)
            send_b[q * 4 + j] = jnp.where(from_own, own[rows], other[rows]).astype(BF)
    scatter(me, chan, send_b, recv_b, send_sem.at[3], recv_sem.at[3])

    swap_other.wait()

    def mix_channels(group, carry):
        for u in range(8):
            rows = pl.ds(pl.multiple_of((group * 8 + u) * HALF, HALF), HALF)
            both = jnp.concatenate([latent[rows, :], latent_other[rows, :]], axis=0)
            total[rows, :] = dot(skip_ref[...], both) + bias_ref[...]
        return carry

    lax.fori_loop(0, G // 8, mix_channels, 0)
    settle(send_b, recv_b, send_sem.at[3], recv_sem.at[3])

    spectra = recv_b[...].astype(F32).reshape(1024, 128).astype(BF)
    prod = dot(fwd_ref[...], spectra)
    for h in range(2):
        xbuf[h] = prod[h * 256 : h * 256 + 128, 0:64] + prod[h * 256 + 128 : h * 256 + 256, 64:128]

    def chunk(t, carry):
        rows = pl.ds(pl.multiple_of(t * 32, 32), 32)
        real = jnp.zeros((32, C), F32)
        imag = jnp.zeros((32, C), F32)
        for h in range(2):
            x = xbuf[h, rows, :]
            for c in range(HALF):
                wr = weight_ref[0, h * HALF + c, rows, :].astype(F32)
                wi = weight_ref[1, h * HALF + c, rows, :].astype(F32)
                xr = x[:, c : c + 1]
                xi = x[:, HALF + c : HALF + c + 1]
                real = real + xr * wr - xi * wi
                imag = imag + xr * wi + xi * wr
        for h in range(2):
            mr = real[:, h * HALF : (h + 1) * HALF]
            mi = imag[:, h * HALF : (h + 1) * HALF]
            top = jnp.concatenate([mr, mi, -mi, mr], axis=1).astype(BF)
            low = jnp.concatenate([-mi, mr, -mr, -mi], axis=1).astype(BF)
            rhs[pl.ds(pl.multiple_of(h * 256 + t * 32, 32), 32), :] = top
            rhs[pl.ds(pl.multiple_of(h * 256 + 128 + t * 32, 32), 32), :] = low
        return carry

    lax.fori_loop(0, 4, chunk, 0)
    send_c[...] = dot(bwd_ref[...], rhs[...]).reshape(G, 8, 128).astype(BF)
    scatter(me, chan, send_c, recv_c, send_sem.at[4], recv_sem.at[4])
    settle(send_c, recv_c, send_sem.at[4], recv_sem.at[4])
    swap_back = swap(recv_c, recv_d, 5)
    swap_back.start()
    swap_back.wait()

    for q in range(M):
        own = recv_c[q * 4 : (q + 1) * 4].astype(F32).reshape(M, 128).astype(BF)
        other = recv_d[q * 4 : (q + 1) * 4].astype(F32).reshape(M, 128).astype(BF)
        lines = jnp.concatenate([own, other], axis=0)
        both = dot(lines, ez_ref[chan], ((0,), (0,)))
        ubuf[q * C : (q + 1) * C, :] = both[0:C, 0:G] + both[C : 2 * C, G : 2 * G]
    for c in range(HALF):
        lines = ubuf[pl.ds(c, 2 * M, stride=HALF), :].astype(BF)
        total[pl.ds(c, G, stride=HALF), :] = total[pl.ds(c, G, stride=HALF), :] + dot(ey_ref[...], lines)

    def finish(group, carry):
        for u in range(4):
            rows = pl.ds(pl.multiple_of((group * 4 + u) * HALF, HALF), HALF)
            grid_ref[rows, :] = gelu(total[rows, :]).astype(BF)
        return carry

    lax.fori_loop(0, G // 4, finish, 0)
    swap_grid = swap(grid_ref, grid_other_ref, 6)
    swap_grid.start()
    swap_grid.wait()


def decode_kernel(line_ref, meta_ref, own_ref, other_ref, proj_in_ref, proj_out_ref, out_ref, todo):
    def collect(s, count):
        todo[count] = s
        return count + jnp.where(line_ref[s] < G, 1, 0)

    count = lax.fori_loop(0, 256, collect, 0)

    def step(group, carry):
        slots, cells, nears = [], [], []
        for u in range(WIDE):
            s = todo[jnp.minimum(group * WIDE + u, count - 1)]
            src, rank = s >> 1, s & 1
            rows = pl.ds(pl.multiple_of(line_ref[s] * HALF, HALF), HALF)
            info = meta_ref[src, 16:24, :].astype(F32)
            start = jnp.where(rank == 0, info[0:1, :], info[1:2, :]).astype(jnp.int32)
            weight = meta_ref[src, pl.ds(pl.multiple_of(rank * 8, 8), 8), :].astype(F32)
            slots.append(s)
            cells.append(jnp.concatenate([own_ref[rows, :], other_ref[rows, :]], axis=0))
            nears.append(near_transposed(start, weight))
        values = [dot(cells[u], nears[u]).astype(BF) for u in range(WIDE)]
        hidden = gelu(dot(proj_in_ref[...], jnp.concatenate(values, axis=1))).astype(BF)
        result = dot(proj_out_ref[...], hidden)
        for u in range(WIDE):
            out_ref[pl.ds(slots[u], 1), :] = result[0:1, u * PB : (u + 1) * PB]
        return carry

    lax.fori_loop(0, (count + WIDE - 1) // WIDE, step, 0)


def return_kernel(slot_ref, values_ref, out_ref, got, send_sem, recv_sem):
    me, chan = lax.axis_index("slab"), lax.axis_index("chan")
    pl.semaphore_wait(greet_all(me, chan), G - 1)
    scatter(me, chan, values_ref, got, send_sem, recv_sem)
    settle(values_ref, got, send_sem, recv_sem)

    def step(b, carry):
        slot = slot_ref[b]
        taken = jnp.maximum(slot, 0)
        out_ref[pl.ds(b, 1), :] = jnp.where(slot >= 0, got[taken >> 1, pl.ds(taken & 1, 1), :], 0.0)
        return carry

    lax.fori_loop(0, 128, step, 0, unroll=8)


def shards(
    points,
    near_start,
    near_weight,
    dest_slab,
    dest_block,
    live_count,
    lift_w,
    spec_weight,
    skip_w,
    skip_bias,
    proj_in,
    proj_out,
):
    cos, sin = trig()
    chan = lax.axis_index("chan")

    ids = jnp.arange(128, dtype=jnp.int32)
    live = ids < live_count[0]
    target = jnp.where(live, dest_slab[:, 0], -1)
    same = (target[:, None] == target[None, :]) & (ids[None, :] < ids[:, None])
    rank = jnp.sum(same.astype(jnp.int32), axis=1)
    slot = jnp.where(live, target * 2 + rank, -1)
    slot_ids = jnp.arange(256, dtype=jnp.int32)
    block = jnp.max(jnp.where(slot[None, :] == slot_ids[:, None], ids[None, :], -1), axis=1)

    parts = pl.pallas_call(
        dispatch_kernel,
        out_shape=jax.ShapeDtypeStruct((G, ROWS, PB), BF),
        in_specs=[SM, SM] + [VM] * 4,
        out_specs=pl.BlockSpec(memory_space=pl.ANY),
        scratch_shapes=[pltpu.VMEM((G, ROWS, PB), BF)] + [pltpu.SemaphoreType.DMA] * 3,
        compiler_params=pltpu.CompilerParams(
            vmem_limit_bytes=LIMIT, collective_id=0, has_side_effects=True
        ),
    )(block, dest_block, points, near_start, near_weight, lift_w.T)
    meta = parts[:, 128:152, :]
    lines = meta[:, 18:20, 0].astype(jnp.int32)
    lines = jnp.where(lines > 0, lines - 1, G).reshape(256)
    mine, theirs = call(
        gather_kernel,
        (jax.ShapeDtypeStruct((G * HALF, G), F32), jax.ShapeDtypeStruct((G * HALF, G), BF)),
        [SM, SM, VM],
        [pltpu.VMEM((2, (G + 1) * HALF, G), F32)],
        (VM, VM),
    )(chan.reshape(1), lines, parts)

    dy = jnp.asarray(np.concatenate([cos.T, -sin.T, -cos.T], axis=0), BF)
    quads = np.concatenate([cos.T, sin.T], axis=1).reshape(4, 2, 1, 4, 2 * G)
    dz = np.broadcast_to(quads, (4, 2, 2, 4, 2 * G)).transpose(1, 0, 2, 3, 4).reshape(2 * M, 2 * G)
    eye4, eye2 = np.eye(4), np.eye(2)
    table = np.stack([cos.T, sin.T])
    forward = np.einsum("hg,vkx,mn->hvkmxgn", eye2, table, eye4).reshape(512, 1024)
    ez = np.zeros((2, 2, 4, 2, 4, 2 * G))
    for h in range(2):
        for side in range(2):
            ez[h, side, :, h, :, :] = quads[:, h if side == 0 else 1 - h, 0]
    ez = ez.reshape(2, 2 * M, 2 * G)
    ey = np.stack([cos, -sin], axis=2).reshape(G, 2 * M) / G**3
    weight = jnp.transpose(spec_weight, (0, 1, 3, 4, 2)).reshape(2, C, 128, C)
    own = chan * HALF
    other = (1 - chan) * HALF
    skip_own = lax.dynamic_slice_in_dim(skip_w, own, HALF, 1)
    skip = jnp.concatenate(
        [
            lax.dynamic_slice_in_dim(skip_own, own, HALF, 0),
            lax.dynamic_slice_in_dim(skip_own, other, HALF, 0),
        ],
        axis=0,
    ).T
    bias = jnp.broadcast_to(lax.dynamic_slice_in_dim(skip_bias, own, HALF, 0)[:, None], (HALF, G))
    plane = (G * HALF, G)
    block8 = pltpu.VMEM((G, 8, 128), BF)
    grid, grid_other = pl.pallas_call(
        middle_kernel,
        out_shape=(jax.ShapeDtypeStruct(plane, BF), jax.ShapeDtypeStruct(plane, BF)),
        in_specs=[VM] * 11,
        out_specs=(VM, VM),
        scratch_shapes=[
            pltpu.VMEM(plane, BF),
            pltpu.VMEM(plane, BF),
            pltpu.VMEM(plane, BF),
            pltpu.VMEM(plane, F32),
            pltpu.VMEM((3 * M * HALF, G), F32),
            pltpu.VMEM((2, 1024, 128), BF),
            pltpu.VMEM((1024, 128), BF),
            block8,
            block8,
            pltpu.VMEM((2, 128, C), F32),
            pltpu.VMEM((512, 128), BF),
            block8,
            block8,
            block8,
            pltpu.VMEM((M * C, G), F32),
            pltpu.SemaphoreType.DMA((7,)),
            pltpu.SemaphoreType.DMA((7,)),
        ],
        compiler_params=pltpu.CompilerParams(
            vmem_limit_bytes=LIMIT, collective_id=1, has_side_effects=True
        ),
    )(
        mine, theirs, weight, jnp.asarray(forward, BF), jnp.asarray(forward.T, BF), dy, jnp.asarray(dz, BF),
        jnp.asarray(ez, BF), jnp.asarray(ey, BF), skip, bias,
    )

    proj = jnp.concatenate(
        [
            lax.dynamic_slice_in_dim(proj_in, own, HALF, 0),
            lax.dynamic_slice_in_dim(proj_in, other, HALF, 0),
        ],
        axis=0,
    ).T
    proj_row = jnp.broadcast_to(proj_out[None, :], (8, 128))
    values = call(
        decode_kernel,
        jax.ShapeDtypeStruct((256, PB), F32),
        [SM] + [VM] * 5,
        [pltpu.SMEM((257,), jnp.int32)],
    )(lines, meta, grid, grid_other, proj, proj_row)
    return pl.pallas_call(
        return_kernel,
        out_shape=jax.ShapeDtypeStruct((128, PB), F32),
        in_specs=[SM, VM],
        out_specs=VM,
        scratch_shapes=[pltpu.VMEM((G, 2, PB), F32)] + [pltpu.SemaphoreType.DMA] * 2,
        compiler_params=pltpu.CompilerParams(
            vmem_limit_bytes=LIMIT, collective_id=2, has_side_effects=True
        ),
    )(slot, values.reshape(G, 2, PB))


def solution(mesh):
    placed = (
        P(("slab", "chan"), None, None),
        P(("slab", "chan"), None),
        P(("slab", "chan"), None, None),
        P(("slab", "chan"), None),
        P(("slab", "chan")),
        P(("slab", "chan")),
        P(),
        P(None, None, None, None, ("slab", "chan")),
        P(),
        P(),
        P(),
        P(),
    )
    return jax.shard_map(
        shards, mesh=mesh, in_specs=placed, out_specs=P(("slab", "chan"), None), check_vma=False
    )
```

```python
import math

import jax
import jax.numpy as jnp
import numpy as np
from jax import lax
from jax.experimental import pallas as pl
from jax.experimental.pallas import tpu as pltpu
from jax.sharding import PartitionSpec as P

G = 128
M = 32
PB = 128
NB = 8
C = 64
HALF = 32
BF = jnp.bfloat16
F32 = jnp.float32
LIMIT = 48 * 1024 * 1024
VM = pl.BlockSpec(memory_space=pltpu.VMEM)
SM = pl.BlockSpec(memory_space=pltpu.SMEM)


def trig():
    modes = np.concatenate([np.arange(M // 2), np.arange(M // 2) - M // 2])
    phase = (np.arange(G)[:, None] * modes[None, :] % G) * (2.0 * math.pi / G)
    return np.cos(phase), np.sin(phase)


def call(kernel, out_shape, in_specs, scratch=(), out_specs=None):
    return pl.pallas_call(
        kernel,
        out_shape=out_shape,
        in_specs=in_specs,
        out_specs=VM if out_specs is None else out_specs,
        scratch_shapes=list(scratch),
        compiler_params=pltpu.CompilerParams(vmem_limit_bytes=LIMIT),
    )


def dot(left, right, dims=((1,), (0,))):
    return lax.dot_general(left, right, (dims, ((), ())), preferred_element_type=F32)


def gelu(x):
    inner = x * (0.7978845608028654 + 0.035677408136300125 * (x * x))
    half = 0.5 * x
    return half + half * jnp.tanh(inner)


def near_transposed(start, weight):
    base = lax.broadcasted_iota(jnp.int32, (NB, PB), 0) - start
    which = base & 7
    tile = -(base >> 3)
    picked = jnp.zeros((NB, PB), F32)
    for j in range(NB):
        picked = jnp.where(which == j, weight[j : j + 1, :], picked)
    rows = [jnp.where(tile == t, picked, 0.0) for t in range(G // NB)]
    return jnp.concatenate(rows, axis=0).astype(BF)


def dispatch_kernel(
    blk_ref, line_ref, points_hbm, start_hbm, weight_hbm, lift_ref,
    out_ref, got_line_ref, meta_ref,
    points_ref, start_ref, weight_ref, stage, stage_line, send_sem, recv_sem, own_sem,
):
    me, chan = lax.axis_index("slab"), lax.axis_index("chan")
    x, z, y = me // 32, (me // 4) % 8, me % 4
    loads = [
        pltpu.make_async_copy(src, dst, own_sem.at[2 + n])
        for n, (src, dst) in enumerate(
            ((points_hbm, points_ref), (start_hbm, start_ref), (weight_hbm, weight_ref))
        )
    ]
    for load in loads:
        load.start()
    barrier = greet_all(me, chan)
    for load in loads:
        load.wait()
    pl.semaphore_wait(barrier, G - 1)
    lane = lax.broadcasted_iota(jnp.int32, (1, PB), 1)
    row = lax.broadcasted_iota(jnp.int32, (8, PB), 0)

    def group(g, carry):
        line_x = (x + g // 4) % 4 * 32 + (y + g % 4) % 4
        targets, blocks, nears = [], [], []
        for j in range(8):
            hop = (j + 1) // 2
            target = line_x + (z + (4 + hop if j % 2 else 4 - hop)) % 8 * 4
            found = [blk_ref[2 * target + r] for r in range(2)]
            taken = [jnp.maximum(b, 0) for b in found]
            lines = [jnp.where(b >= 0, line_ref[c] + 1, 0) for b, c in zip(found, taken)]
            starts = [start_ref[pl.ds(c, 1), :] for c in taken]
            info = jnp.where(row == 0, starts[0], jnp.where(row == 1, starts[1], 0))
            weights = [weight_ref[c] for c in taken]
            meta_ref[target, 0:8, :] = weights[0]
            meta_ref[target, 8:16, :] = weights[1]
            meta_ref[target, 16:24, :] = info.astype(F32).astype(BF)
            stage_line[g * 8 + j] = jnp.where(lane == 0, lines[0], jnp.where(lane == 1, lines[1], 0))
            targets.append(target)
            blocks.extend(taken)
            nears.extend(near_transposed(s, w.astype(F32)) for s, w in zip(starts, weights))
        points = jnp.concatenate([points_ref[b] for b in blocks], axis=1)
        lifted = dot(lift_ref[...], points).astype(BF)
        for j in range(8):
            for r in range(2):
                u = 2 * j + r
                part = dot(lifted[:, u * PB : (u + 1) * PB], nears[u], ((1,), (1,)))
                stage[g * 8 + j, r * C : (r + 1) * C, :] = part.astype(BF)
        for j in range(8):
            for n, (src, dst) in enumerate(((stage_line, got_line_ref), (stage, out_ref))):
                copy = pltpu.make_async_remote_copy(
                    src_ref=src.at[g * 8 + j],
                    dst_ref=dst.at[me],
                    send_sem=send_sem.at[n],
                    recv_sem=recv_sem.at[n],
                    device_id=(targets[j], chan),
                    device_id_type=pl.DeviceIdType.MESH,
                )
                if j < 7:
                    copy.start()
                else:
                    pl.when(g > 0)(copy.start)
        return carry

    lax.fori_loop(0, 16, group, 0)
    own = [
        pltpu.make_async_copy(stage_line.at[7], got_line_ref.at[me], own_sem.at[0]),
        pltpu.make_async_copy(stage.at[7], out_ref.at[me], own_sem.at[1]),
    ]
    for copy in own:
        copy.start()
    for copy in own:
        copy.wait()
    settle(stage_line, got_line_ref, send_sem.at[0], recv_sem.at[0])
    settle(stage, out_ref, send_sem.at[1], recv_sem.at[1])


def gather_kernel(chan_ref, line_ref, parts_ref, own_ref, other_ref, acc):
    acc[...] = jnp.zeros_like(acc)

    def add(src, carry):
        for r in range(2):
            line = line_ref[src, 0, r]
            line = jnp.where(line > 0, line - 1, G)
            rows = pl.ds(pl.multiple_of(line * HALF, HALF), HALF)
            for h in range(2):
                first = r * C + h * HALF
                acc[h, rows, :] += parts_ref[src, first : first + HALF, :].astype(F32)
        return carry

    lax.fori_loop(0, G, add, 0)
    chan = chan_ref[0]
    own_ref[...] = acc[chan, 0 : G * HALF, :]
    other_ref[...] = acc[1 - chan, 0 : G * HALF, :].astype(BF)


def greet_all(me, chan):
    barrier = pltpu.get_barrier_semaphore()

    def greet(i, carry):
        pl.semaphore_signal(
            barrier, inc=1, device_id=((me + i) % G, chan), device_id_type=pl.DeviceIdType.MESH
        )
        return carry

    lax.fori_loop(1, G, greet, 0)
    return barrier


def send_blocks(first, last, me, chan, src, dst, send_sem, recv_sem):
    def send(i, carry):
        target = (me + i) % G
        pltpu.make_async_remote_copy(
            src_ref=src.at[target],
            dst_ref=dst.at[me],
            send_sem=send_sem,
            recv_sem=recv_sem,
            device_id=(target, chan),
            device_id_type=pl.DeviceIdType.MESH,
        ).start()
        return carry

    lax.fori_loop(first, last, send, 0)


def scatter(me, chan, src, dst, send_sem, recv_sem):
    send_blocks(1, G, me, chan, src, dst, send_sem, recv_sem)
    dst[me] = src[me]


def settle(src, dst, send_sem, recv_sem):
    sent, got = src.at[pl.ds(0, G - 1)], dst.at[pl.ds(0, G - 1)]
    pltpu.make_async_copy(sent, sent, send_sem).wait()
    pltpu.make_async_copy(got, got, recv_sem).wait()


def middle_kernel(
    line_ref, slot_ref, mine_ref, theirs_ref, weight_ref, fwd_ref, bwd_ref, dy_ref, dz_ref, ez_ref, ey_ref, skip_ref,
    bias_ref, meta_ref, proj_in_ref, proj_out_ref,
    out_ref,
    grid_ref, grid_other_ref, got_meta, send_v, recv_v,
    got, latent, latent_other, total, ybuf, spec, spec_other, send_b, recv_b, xbuf, rhs, send_c, recv_c, recv_d, ubuf,
    send_sem, recv_sem,
):
    me, chan = lax.axis_index("slab"), lax.axis_index("chan")
    barrier = greet_all(me, chan)
    pl.semaphore_signal(barrier, inc=1, device_id=(me, 1 - chan), device_id_type=pl.DeviceIdType.MESH)
    pl.semaphore_wait(barrier, G)

    def swap(src, dst, index):
        return pltpu.make_async_remote_copy(
            src_ref=src,
            dst_ref=dst,
            send_sem=send_sem.at[index],
            recv_sem=recv_sem.at[index],
            device_id=(me, 1 - chan),
            device_id_type=pl.DeviceIdType.MESH,
        )

    swap_latent = swap(theirs_ref, got, 0)
    swap_latent.start()
    send_blocks(1, G // 2, me, chan, meta_ref, got_meta, send_sem.at[7], recv_sem.at[7])
    got_meta[me] = meta_ref[me]
    swap_latent.wait()
    total[...] = mine_ref[...] + got[...].astype(F32)
    latent[...] = total[...].astype(BF)
    swap_other = swap(latent, latent_other, 1)
    swap_other.start()

    for c in range(HALF):
        plane = total[pl.ds(c, G, stride=HALF), :].astype(BF)
        ybuf[pl.ds(c, 3 * M, stride=HALF), :] = dot(dy_ref[...], plane)
    for q in range(M):
        real = ybuf[q * HALF : (q + 1) * HALF, :].astype(BF)
        imag = ybuf[(M + q) * HALF : (M + q + 1) * HALF, :].astype(BF)
        minus = ybuf[(2 * M + q) * HALF : (2 * M + q + 1) * HALF, :].astype(BF)
        first = jnp.concatenate([real, imag, imag, minus], axis=0)
        second = jnp.concatenate([imag, minus, minus, -imag], axis=0)
        both = jnp.concatenate([first, second], axis=1)
        modes = dot(dz_ref[...], both, ((1,), (1,))).astype(BF)
        spec[0, q * M : (q + 1) * M, :] = modes[:M]
        spec[1, q * M : (q + 1) * M, :] = modes[M:]

    swap_spec = swap(spec.at[1 - chan], spec_other, 2)
    swap_spec.start()
    swap_spec.wait()
    row = lax.broadcasted_iota(jnp.int32, (8, 128), 0)
    from_own = (row // 4) == chan
    for q in range(M):
        own = spec[chan, q * M : (q + 1) * M, :].astype(F32)
        other = spec_other[q * M : (q + 1) * M, :].astype(F32)
        for j in range(4):
            rows = slice(j * 8, (j + 1) * 8)
            send_b[q * 4 + j] = jnp.where(from_own, own[rows], other[rows]).astype(BF)
    scatter(me, chan, send_b, recv_b, send_sem.at[3], recv_sem.at[3])

    swap_other.wait()

    def mix_channels(group, carry):
        for u in range(8):
            rows = pl.ds(pl.multiple_of((group * 8 + u) * HALF, HALF), HALF)
            both = jnp.concatenate([latent[rows, :], latent_other[rows, :]], axis=0)
            total[rows, :] = dot(skip_ref[...], both) + bias_ref[...]
        return carry

    lax.fori_loop(0, G // 8, mix_channels, 0)
    settle(send_b, recv_b, send_sem.at[3], recv_sem.at[3])
    send_blocks(G // 2, G, me, chan, meta_ref, got_meta, send_sem.at[7], recv_sem.at[7])

    spectra = recv_b[...].astype(F32).reshape(1024, 128).astype(BF)
    prod = dot(fwd_ref[...], spectra)
    for h in range(2):
        xbuf[h] = prod[h * 256 : h * 256 + 128, 0:64] + prod[h * 256 + 128 : h * 256 + 256, 64:128]

    def chunk(t, carry):
        rows = pl.ds(pl.multiple_of(t * 32, 32), 32)
        real = jnp.zeros((32, C), F32)
        imag = jnp.zeros((32, C), F32)
        for h in range(2):
            x = xbuf[h, rows, :]
            for c in range(HALF):
                wr = weight_ref[0, h * HALF + c, rows, :].astype(F32)
                wi = weight_ref[1, h * HALF + c, rows, :].astype(F32)
                xr = x[:, c : c + 1]
                xi = x[:, HALF + c : HALF + c + 1]
                real = real + xr * wr - xi * wi
                imag = imag + xr * wi + xi * wr
        for h in range(2):
            mr = real[:, h * HALF : (h + 1) * HALF]
            mi = imag[:, h * HALF : (h + 1) * HALF]
            top = jnp.concatenate([mr, mi, -mi, mr], axis=1).astype(BF)
            low = jnp.concatenate([-mi, mr, -mr, -mi], axis=1).astype(BF)
            rhs[pl.ds(pl.multiple_of(h * 256 + t * 32, 32), 32), :] = top
            rhs[pl.ds(pl.multiple_of(h * 256 + 128 + t * 32, 32), 32), :] = low
        return carry

    lax.fori_loop(0, 4, chunk, 0)
    send_c[...] = dot(bwd_ref[...], rhs[...]).reshape(G, 8, 128).astype(BF)
    scatter(me, chan, send_c, recv_c, send_sem.at[4], recv_sem.at[4])
    settle(send_c, recv_c, send_sem.at[4], recv_sem.at[4])
    swap_back = swap(recv_c, recv_d, 5)
    swap_back.start()
    swap_back.wait()

    for q in range(M):
        own = recv_c[q * 4 : (q + 1) * 4].astype(F32).reshape(M, 128).astype(BF)
        other = recv_d[q * 4 : (q + 1) * 4].astype(F32).reshape(M, 128).astype(BF)
        lines = jnp.concatenate([own, other], axis=0)
        both = dot(lines, ez_ref[chan], ((0,), (0,)))
        ubuf[q * C : (q + 1) * C, :] = both[0:C, 0:G] + both[C : 2 * C, G : 2 * G]
    for c in range(HALF):
        lines = ubuf[pl.ds(c, 2 * M, stride=HALF), :].astype(BF)
        total[pl.ds(c, G, stride=HALF), :] = total[pl.ds(c, G, stride=HALF), :] + dot(ey_ref[...], lines)

    def finish(group, carry):
        for u in range(4):
            y = group * 4 + u
            rows = pl.ds(pl.multiple_of(y * HALF, HALF), HALF)
            grid_ref[y] = gelu(total[rows, :]).astype(BF)
        return carry

    lax.fori_loop(0, G // 4, finish, 0)
    swap_grid = swap(grid_ref, grid_other_ref, 6)
    swap_grid.start()
    settle(meta_ref, got_meta, send_sem.at[7], recv_sem.at[7])
    swap_grid.wait()

    def decode(group, carry):
        slabs, cells, nears = [], [], []
        for j in range(8):
            slab = (me + group * 8 + j) % G
            slabs.append(slab)
            info = got_meta[slab, 16:24, :].astype(F32).astype(jnp.int32)
            for r in range(2):
                line = jnp.maximum(line_ref[slab, 0, r] - 1, 0)
                weight = got_meta[slab, r * 8 : (r + 1) * 8, :].astype(F32)
                cells.append(jnp.concatenate([grid_ref[line], grid_other_ref[line]], axis=0))
                nears.append(near_transposed(info[r : r + 1, :], weight))
        values = [dot(cell, near).astype(BF) for cell, near in zip(cells, nears)]
        hidden = gelu(dot(proj_in_ref[...], jnp.concatenate(values, axis=1))).astype(BF)
        result = dot(proj_out_ref[...], hidden)
        for j in range(8):
            for r in range(2):
                u = 2 * j + r
                send_v[slabs[j], r : r + 1, :] = result[0:1, u * PB : (u + 1) * PB]
        for j in range(8):
            copy = pltpu.make_async_remote_copy(
                src_ref=send_v.at[slabs[j]],
                dst_ref=recv_v.at[me],
                send_sem=send_sem.at[8],
                recv_sem=recv_sem.at[8],
                device_id=(slabs[j], chan),
                device_id_type=pl.DeviceIdType.MESH,
            )
            if j > 0:
                copy.start()
            else:
                pl.when(group > 0)(copy.start)
        return carry

    lax.fori_loop(0, 16, decode, 0)
    recv_v[me] = send_v[me]
    settle(send_v, recv_v, send_sem.at[8], recv_sem.at[8])

    def unpack(b, carry):
        slot = slot_ref[b]
        taken = jnp.maximum(slot, 0)
        out_ref[pl.ds(b, 1), :] = jnp.where(slot >= 0, recv_v[taken >> 1, pl.ds(taken & 1, 1), :], 0.0)
        return carry

    lax.fori_loop(0, 128, unpack, 0, unroll=8)


def shards(
    points,
    near_start,
    near_weight,
    dest_slab,
    dest_block,
    live_count,
    lift_w,
    spec_weight,
    skip_w,
    skip_bias,
    proj_in,
    proj_out,
):
    cos, sin = trig()
    chan = lax.axis_index("chan")

    ids = jnp.arange(128, dtype=jnp.int32)
    live = ids < live_count[0]
    target = jnp.where(live, dest_slab[:, 0], -1)
    same = (target[:, None] == target[None, :]) & (ids[None, :] < ids[:, None])
    rank = jnp.sum(same.astype(jnp.int32), axis=1)
    slot = jnp.where(live, target * 2 + rank, -1)
    slot_ids = jnp.arange(256, dtype=jnp.int32)
    block = jnp.max(jnp.where(slot[None, :] == slot_ids[:, None], ids[None, :], -1), axis=1)

    ANY = pl.BlockSpec(memory_space=pl.ANY)
    parts, lines, meta = pl.pallas_call(
        dispatch_kernel,
        out_shape=(
            jax.ShapeDtypeStruct((G, 2 * C, PB), BF),
            jax.ShapeDtypeStruct((G, 1, PB), jnp.int32),
            jax.ShapeDtypeStruct((G, 24, PB), BF),
        ),
        in_specs=[SM, SM, ANY, ANY, ANY, VM],
        out_specs=(ANY, ANY, VM),
        scratch_shapes=[
            pltpu.VMEM((128, C, PB), BF),
            pltpu.VMEM((128, PB), jnp.int32),
            pltpu.VMEM((128, NB, PB), BF),
            pltpu.VMEM((G, 2 * C, PB), BF),
            pltpu.VMEM((G, 1, PB), jnp.int32),
            pltpu.SemaphoreType.DMA((2,)),
            pltpu.SemaphoreType.DMA((2,)),
            pltpu.SemaphoreType.DMA((5,)),
        ],
        compiler_params=pltpu.CompilerParams(
            vmem_limit_bytes=LIMIT, collective_id=0, has_side_effects=True
        ),
    )(block, dest_block, points, near_start, near_weight, lift_w.T)
    mine, theirs = call(
        gather_kernel,
        (jax.ShapeDtypeStruct((G * HALF, G), F32), jax.ShapeDtypeStruct((G * HALF, G), BF)),
        [SM, SM, VM],
        [pltpu.VMEM((2, (G + 1) * HALF, G), F32)],
        (VM, VM),
    )(chan.reshape(1), lines, parts)

    dy = jnp.asarray(np.concatenate([cos.T, -sin.T, -cos.T], axis=0), BF)
    quads = np.concatenate([cos.T, sin.T], axis=1).reshape(4, 2, 1, 4, 2 * G)
    dz = np.broadcast_to(quads, (4, 2, 2, 4, 2 * G)).transpose(1, 0, 2, 3, 4).reshape(2 * M, 2 * G)
    eye4, eye2 = np.eye(4), np.eye(2)
    table = np.stack([cos.T, sin.T])
    forward = np.einsum("hg,vkx,mn->hvkmxgn", eye2, table, eye4).reshape(512, 1024)
    ez = np.zeros((2, 2, 4, 2, 4, 2 * G))
    for h in range(2):
        for side in range(2):
            ez[h, side, :, h, :, :] = quads[:, h if side == 0 else 1 - h, 0]
    ez = ez.reshape(2, 2 * M, 2 * G)
    ey = np.stack([cos, -sin], axis=2).reshape(G, 2 * M) / G**3
    weight = jnp.transpose(spec_weight, (0, 1, 3, 4, 2)).reshape(2, C, 128, C)
    own = chan * HALF
    other = (1 - chan) * HALF
    skip_own = lax.dynamic_slice_in_dim(skip_w, own, HALF, 1)
    skip = jnp.concatenate(
        [
            lax.dynamic_slice_in_dim(skip_own, own, HALF, 0),
            lax.dynamic_slice_in_dim(skip_own, other, HALF, 0),
        ],
        axis=0,
    ).T
    bias = jnp.broadcast_to(lax.dynamic_slice_in_dim(skip_bias, own, HALF, 0)[:, None], (HALF, G))
    plane = (G * HALF, G)
    block8 = pltpu.VMEM((G, 8, 128), BF)
    proj = jnp.concatenate(
        [
            lax.dynamic_slice_in_dim(proj_in, own, HALF, 0),
            lax.dynamic_slice_in_dim(proj_in, other, HALF, 0),
        ],
        axis=0,
    ).T
    proj_row = jnp.broadcast_to(proj_out[None, :], (8, 128))
    return pl.pallas_call(
        middle_kernel,
        out_shape=jax.ShapeDtypeStruct((128, PB), F32),
        in_specs=[SM, SM] + [VM] * 14,
        out_specs=VM,
        scratch_shapes=[
            pltpu.VMEM((G, HALF, G), BF),
            pltpu.VMEM((G, HALF, G), BF),
            pltpu.VMEM((G, 24, PB), BF),
            pltpu.VMEM((G, 2, PB), F32),
            pltpu.VMEM((G, 2, PB), F32),
            pltpu.VMEM(plane, BF),
            pltpu.VMEM(plane, BF),
            pltpu.VMEM(plane, BF),
            pltpu.VMEM(plane, F32),
            pltpu.VMEM((3 * M * HALF, G), F32),
            pltpu.VMEM((2, 1024, 128), BF),
            pltpu.VMEM((1024, 128), BF),
            block8,
            block8,
            pltpu.VMEM((2, 128, C), F32),
            pltpu.VMEM((512, 128), BF),
            block8,
            block8,
            block8,
            pltpu.VMEM((M * C, G), F32),
            pltpu.SemaphoreType.DMA((9,)),
            pltpu.SemaphoreType.DMA((9,)),
        ],
        compiler_params=pltpu.CompilerParams(
            vmem_limit_bytes=LIMIT, collective_id=1, has_side_effects=True
        ),
    )(
        lines, slot, mine, theirs, weight, jnp.asarray(forward, BF), jnp.asarray(forward.T, BF), dy, jnp.asarray(dz, BF),
        jnp.asarray(ez, BF), jnp.asarray(ey, BF), skip, bias, meta, proj, proj_row,
    )


def solution(mesh):
    placed = (
        P(("slab", "chan"), None, None),
        P(("slab", "chan"), None),
        P(("slab", "chan"), None, None),
        P(("slab", "chan"), None),
        P(("slab", "chan")),
        P(("slab", "chan")),
        P(),
        P(None, None, None, None, ("slab", "chan")),
        P(),
        P(),
        P(),
        P(),
    )
    return jax.shard_map(
        shards, mesh=mesh, in_specs=placed, out_specs=P(("slab", "chan"), None), check_vma=False
    )
```

```python
import math

import jax
import jax.numpy as jnp
import numpy as np
from jax import lax
from jax.experimental import pallas as pl
from jax.experimental.pallas import tpu as pltpu
from jax.sharding import PartitionSpec as P

G = 128
M = 32
PB = 128
NB = 8
C = 64
HALF = 32
BF = jnp.bfloat16
F32 = jnp.float32
LIMIT = 60 * 1024 * 1024
VM = pl.BlockSpec(memory_space=pltpu.VMEM)
SM = pl.BlockSpec(memory_space=pltpu.SMEM)
ANY = pl.BlockSpec(memory_space=pl.ANY)
SELF = 7


def trig():
    modes = np.concatenate([np.arange(M // 2), np.arange(M // 2) - M // 2])
    phase = (np.arange(G)[:, None] * modes[None, :] % G) * (2.0 * math.pi / G)
    return np.cos(phase), np.sin(phase)


def call(kernel, out_shape, in_specs, scratch=(), out_specs=None):
    return pl.pallas_call(
        kernel,
        out_shape=out_shape,
        in_specs=in_specs,
        out_specs=VM if out_specs is None else out_specs,
        scratch_shapes=list(scratch),
        compiler_params=pltpu.CompilerParams(vmem_limit_bytes=LIMIT),
    )


def dot(left, right, dims=((1,), (0,))):
    return lax.dot_general(left, right, (dims, ((), ())), preferred_element_type=F32)


def gelu(x):
    inner = x * (0.7978845608028654 + 0.035677408136300125 * (x * x))
    half = 0.5 * x
    return half + half * jnp.tanh(inner)


def near_transposed(start, weight):
    base = lax.broadcasted_iota(jnp.int32, (NB, PB), 0) - start
    which = base & 7
    tile = -(base >> 3)
    picked = jnp.zeros((NB, PB), F32)
    for j in range(NB):
        picked = jnp.where(which == j, weight[j : j + 1, :], picked)
    rows = [jnp.where(tile == t, picked, 0.0) for t in range(G // NB)]
    return jnp.concatenate(rows, axis=0).astype(BF)


def dispatch_kernel(
    lo_ref, hi_ref, line_ref, points_hbm, start_hbm, weight_hbm, lift_ref,
    out_ref, got_line_ref, meta_ref,
    points_ref, start_ref, weight_ref, stage, stage_line, send_sem, recv_sem, own_sem,
):
    me, chan = lax.axis_index("slab"), lax.axis_index("chan")
    x, z, y = me // 32, (me // 4) % 8, me % 4
    loads = [
        pltpu.make_async_copy(src, dst, own_sem.at[2 + n])
        for n, (src, dst) in enumerate(
            ((points_hbm, points_ref), (start_hbm, start_ref), (weight_hbm, weight_ref))
        )
    ]
    for load in loads:
        load.start()
    barrier = greet_all(me, chan)
    for load in loads:
        load.wait()
    pl.semaphore_wait(barrier, G - 1)
    lane = lax.broadcasted_iota(jnp.int32, (1, PB), 1)
    row = lax.broadcasted_iota(jnp.int32, (8, PB), 0)

    def group(g, carry):
        targets, blocks, nears = [], [], []
        for j in range(8):
            hop = (j + 1) // 2
            to_z = (z + (4 + hop if j % 2 else 4 - hop)) % 8
            to_x = (x + g // 4 + j) % 4
            to_y = (y + g + j + j // 4 * 2) % 4
            target = to_x * 32 + to_z * 4 + to_y
            lo, hi = lo_ref[target], hi_ref[target]
            found = [jnp.where(hi >= 0, lo, -1), jnp.where(hi > lo, hi, -1)]
            taken = [jnp.maximum(b, 0) for b in found]
            lines = [jnp.where(b >= 0, line_ref[c] + 1, 0) for b, c in zip(found, taken)]
            starts = [start_ref[pl.ds(c, 1), :] for c in taken]
            info = jnp.where(row == 0, starts[0], jnp.where(row == 1, starts[1], 0))
            weights = [weight_ref[c] for c in taken]
            meta_ref[target, 0:8, :] = weights[0]
            meta_ref[target, 8:16, :] = weights[1]
            meta_ref[target, 16:24, :] = info.astype(F32).astype(BF)
            stage_line[g * 8 + j] = jnp.where(lane == 0, lines[0], jnp.where(lane == 1, lines[1], 0))
            targets.append(target)
            blocks.extend(taken)
            nears.extend(near_transposed(s, w.astype(F32)) for s, w in zip(starts, weights))
        points = jnp.concatenate([points_ref[b] for b in blocks], axis=1)
        lifted = dot(lift_ref[...], points, ((0,), (0,))).astype(BF)
        for j in range(8):
            for r in range(2):
                u = 2 * j + r
                part = dot(lifted[:, u * PB : (u + 1) * PB], nears[u], ((1,), (1,)))
                stage[g * 8 + j, r * C : (r + 1) * C, :] = part.astype(BF)
        for j in range(8):
            for n, (src, dst) in enumerate(((stage_line, got_line_ref), (stage, out_ref))):
                copy = pltpu.make_async_remote_copy(
                    src_ref=src.at[g * 8 + j],
                    dst_ref=dst.at[me],
                    send_sem=send_sem.at[n],
                    recv_sem=recv_sem.at[n],
                    device_id=(targets[j], chan),
                    device_id_type=pl.DeviceIdType.MESH,
                )
                if j < 7:
                    copy.start()
                else:
                    pl.when(g != SELF)(copy.start)
        return carry

    lax.fori_loop(0, 16, group, 0)
    own = [
        pltpu.make_async_copy(stage_line.at[SELF * 8 + 7], got_line_ref.at[me], own_sem.at[0]),
        pltpu.make_async_copy(stage.at[SELF * 8 + 7], out_ref.at[me], own_sem.at[1]),
    ]
    for copy in own:
        copy.start()
    for copy in own:
        copy.wait()
    settle(stage_line, got_line_ref, send_sem.at[0], recv_sem.at[0])
    settle(stage, out_ref, send_sem.at[1], recv_sem.at[1])


def gather_kernel(chan_ref, line_ref, parts_ref, own_ref, other_ref, acc):
    step = pl.program_id(0)
    chan = chan_ref[0]

    @pl.when(step == 0)
    def clear():
        own_ref[...] = jnp.zeros_like(own_ref)
        acc[...] = jnp.zeros_like(acc)

    def add(i, carry):
        for r in range(2):
            line = line_ref[step * 16 + i, 0, r]
            line = jnp.where(line > 0, line - 1, G)
            rows = pl.ds(pl.multiple_of(line * HALF, HALF), HALF)
            for half, total in ((chan, own_ref), (1 - chan, acc)):
                first = pl.multiple_of(r * C + half * HALF, HALF)
                total[rows, :] += parts_ref[i, pl.ds(first, HALF), :].astype(F32)
        return carry

    lax.fori_loop(0, 16, add, 0, unroll=4)

    @pl.when(step == 7)
    def finish():
        other_ref[...] = acc[0 : G * HALF, :].astype(BF)


def greet_all(me, chan):
    barrier = pltpu.get_barrier_semaphore()

    def greet(i, carry):
        pl.semaphore_signal(
            barrier, inc=1, device_id=((me + i) % G, chan), device_id_type=pl.DeviceIdType.MESH
        )
        return carry

    lax.fori_loop(1, G, greet, 0)
    return barrier


def send_blocks(first, last, me, chan, src, dst, send_sem, recv_sem):
    def send(i, carry):
        target = (me + i) % G
        pltpu.make_async_remote_copy(
            src_ref=src.at[target],
            dst_ref=dst.at[me],
            send_sem=send_sem,
            recv_sem=recv_sem,
            device_id=(target, chan),
            device_id_type=pl.DeviceIdType.MESH,
        ).start()
        return carry

    lax.fori_loop(first, last, send, 0)


def scatter(me, chan, src, dst, send_sem, recv_sem):
    send_blocks(1, G, me, chan, src, dst, send_sem, recv_sem)
    dst[me] = src[me]


def settle(src, dst, send_sem, recv_sem):
    sent, got = src.at[pl.ds(0, G - 1)], dst.at[pl.ds(0, G - 1)]
    pltpu.make_async_copy(sent, sent, send_sem).wait()
    pltpu.make_async_copy(got, got, recv_sem).wait()


def middle_kernel(
    line_ref, low_ref, slab_ref, count_ref, mine_ref, theirs_ref, weight_hbm, fwd_hbm, bwd_hbm, meta_ref,
    dy_ref, dz_ref, ez_ref, ey_ref, skip_ref, bias_ref, proj_in_ref, proj_out_ref,
    out_ref,
    weight_ref, fwd_ref, bwd_ref, load_sem,
    grid_ref, grid_other_ref, got_meta, send_v, recv_v,
    got, latent, latent_other, total, ybuf, spec, spec_other, send_b, recv_b, xbuf, rhs, send_c, recv_c, recv_d, ubuf,
    send_sem, recv_sem,
):
    me, chan = lax.axis_index("slab"), lax.axis_index("chan")
    loads = [
        pltpu.make_async_copy(src, dst, load_sem.at[n])
        for n, (src, dst) in enumerate(
            (
                (mine_ref.at[pl.ds(0, G * HALF)], total),
                (meta_ref.at[me], got_meta.at[me]),
                (fwd_hbm, fwd_ref),
                (weight_hbm, weight_ref),
                (bwd_hbm, bwd_ref),
            )
        )
    ]
    for load in loads:
        load.start()
    barrier = greet_all(me, chan)
    pl.semaphore_signal(barrier, inc=1, device_id=(me, 1 - chan), device_id_type=pl.DeviceIdType.MESH)
    pl.semaphore_wait(barrier, G)

    def swap(src, dst, index):
        return pltpu.make_async_remote_copy(
            src_ref=src,
            dst_ref=dst,
            send_sem=send_sem.at[index],
            recv_sem=recv_sem.at[index],
            device_id=(me, 1 - chan),
            device_id_type=pl.DeviceIdType.MESH,
        )

    swap_latent = swap(theirs_ref, got, 0)
    swap_latent.start()
    send_blocks(1, G // 2, me, chan, meta_ref, got_meta, send_sem.at[7], recv_sem.at[7])
    loads[0].wait()
    swap_latent.wait()
    total[...] = total[...] + got[...].astype(F32)
    latent[...] = total[...].astype(BF)
    swap_other = swap(latent, latent_other, 1)
    swap_other.start()

    for c in range(HALF):
        plane = total[pl.ds(c, G, stride=HALF), :].astype(BF)
        ybuf[pl.ds(c, 3 * M, stride=HALF), :] = dot(dy_ref[...], plane)
    for q in range(M):
        real = ybuf[q * HALF : (q + 1) * HALF, :].astype(BF)
        imag = ybuf[(M + q) * HALF : (M + q + 1) * HALF, :].astype(BF)
        minus = ybuf[(2 * M + q) * HALF : (2 * M + q + 1) * HALF, :].astype(BF)
        first = jnp.concatenate([real, imag, imag, minus], axis=0)
        second = jnp.concatenate([imag, minus, minus, -imag], axis=0)
        both = jnp.concatenate([first, second], axis=1)
        modes = dot(dz_ref[...], both, ((1,), (1,))).astype(BF)
        spec[0, q * M : (q + 1) * M, :] = modes[:M]
        spec[1, q * M : (q + 1) * M, :] = modes[M:]

    swap_spec = swap(spec.at[1 - chan], spec_other, 2)
    swap_spec.start()
    swap_spec.wait()
    row = lax.broadcasted_iota(jnp.int32, (8, 128), 0)
    from_own = (row // 4) == chan
    for q in range(M):
        own = spec[chan, q * M : (q + 1) * M, :].astype(F32)
        other = spec_other[q * M : (q + 1) * M, :].astype(F32)
        for j in range(4):
            rows = slice(j * 8, (j + 1) * 8)
            send_b[q * 4 + j] = jnp.where(from_own, own[rows], other[rows]).astype(BF)
    scatter(me, chan, send_b, recv_b, send_sem.at[3], recv_sem.at[3])

    swap_other.wait()

    def mix_channels(group, carry):
        for u in range(8):
            rows = pl.ds(pl.multiple_of((group * 8 + u) * HALF, HALF), HALF)
            both = jnp.concatenate([latent[rows, :], latent_other[rows, :]], axis=0)
            total[rows, :] = dot(skip_ref[...], both) + bias_ref[...]
        return carry

    lax.fori_loop(0, G // 8, mix_channels, 0)
    settle(send_b, recv_b, send_sem.at[3], recv_sem.at[3])
    send_blocks(G // 2, G, me, chan, meta_ref, got_meta, send_sem.at[7], recv_sem.at[7])

    for load in loads[1:]:
        load.wait()
    spectra = recv_b[...].astype(F32).reshape(1024, 128).astype(BF)
    prod = dot(fwd_ref[...], spectra)
    for h in range(2):
        xbuf[h] = prod[h * 256 : h * 256 + 128, 0:64] + prod[h * 256 + 128 : h * 256 + 256, 64:128]

    def chunk(t, carry):
        rows = pl.ds(pl.multiple_of(t * 32, 32), 32)
        real = jnp.zeros((32, C), F32)
        imag = jnp.zeros((32, C), F32)
        for h in range(2):
            x = xbuf[h, rows, :]
            for c in range(HALF):
                wr = weight_ref[0, h * HALF + c, rows, :].astype(F32)
                wi = weight_ref[1, h * HALF + c, rows, :].astype(F32)
                xr = x[:, c : c + 1]
                xi = x[:, HALF + c : HALF + c + 1]
                real = real + xr * wr - xi * wi
                imag = imag + xr * wi + xi * wr
        for h in range(2):
            mr = real[:, h * HALF : (h + 1) * HALF]
            mi = imag[:, h * HALF : (h + 1) * HALF]
            top = jnp.concatenate([mr, mi, -mi, mr], axis=1).astype(BF)
            low = jnp.concatenate([-mi, mr, -mr, -mi], axis=1).astype(BF)
            rhs[pl.ds(pl.multiple_of(h * 256 + t * 32, 32), 32), :] = top
            rhs[pl.ds(pl.multiple_of(h * 256 + 128 + t * 32, 32), 32), :] = low
        return carry

    lax.fori_loop(0, 4, chunk, 0)
    send_c[...] = dot(bwd_ref[...], rhs[...]).reshape(G, 8, 128).astype(BF)
    scatter(me, chan, send_c, recv_c, send_sem.at[4], recv_sem.at[4])
    settle(send_c, recv_c, send_sem.at[4], recv_sem.at[4])
    swap_back = swap(recv_c, recv_d, 5)
    swap_back.start()
    swap_back.wait()

    for q in range(M):
        own = recv_c[q * 4 : (q + 1) * 4].astype(F32).reshape(M, 128).astype(BF)
        other = recv_d[q * 4 : (q + 1) * 4].astype(F32).reshape(M, 128).astype(BF)
        lines = jnp.concatenate([own, other], axis=0)
        both = dot(lines, ez_ref[chan], ((0,), (0,)))
        ubuf[q * C : (q + 1) * C, :] = both[0:C, 0:G] + both[C : 2 * C, G : 2 * G]
    for c in range(HALF):
        lines = ubuf[pl.ds(c, 2 * M, stride=HALF), :].astype(BF)
        total[pl.ds(c, G, stride=HALF), :] = total[pl.ds(c, G, stride=HALF), :] + dot(ey_ref[...], lines)

    def finish(group, carry):
        for u in range(4):
            y = group * 4 + u
            rows = pl.ds(pl.multiple_of(y * HALF, HALF), HALF)
            grid_ref[y] = gelu(total[rows, :]).astype(BF)
        return carry

    lax.fori_loop(0, G // 4, finish, 0)
    swap_grid = swap(grid_ref, grid_other_ref, 6)
    swap_grid.start()
    settle(meta_ref, got_meta, send_sem.at[7], recv_sem.at[7])
    swap_grid.wait()

    def decode(group, carry):
        slabs, cells, nears = [], [], []
        for j in range(8):
            slab = (me + group * 8 + j) % G
            slabs.append(slab)
            info = got_meta[slab, 16:24, :].astype(F32).astype(jnp.int32)
            for r in range(2):
                line = jnp.maximum(line_ref[slab, 0, r] - 1, 0)
                weight = got_meta[slab, r * 8 : (r + 1) * 8, :].astype(F32)
                cells.append(jnp.concatenate([grid_ref[line], grid_other_ref[line]], axis=0))
                nears.append(near_transposed(info[r : r + 1, :], weight))
        values = [dot(cell, near).astype(BF) for cell, near in zip(cells, nears)]
        hidden = gelu(dot(proj_in_ref[...], jnp.concatenate(values, axis=1))).astype(BF)
        result = dot(proj_out_ref[...], hidden)
        for j in range(8):
            for r in range(2):
                u = 2 * j + r
                send_v[slabs[j], r : r + 1, :] = result[0:1, u * PB : (u + 1) * PB]
        for j in range(8):
            copy = pltpu.make_async_remote_copy(
                src_ref=send_v.at[slabs[j]],
                dst_ref=recv_v.at[me],
                send_sem=send_sem.at[8],
                recv_sem=recv_sem.at[8],
                device_id=(slabs[j], chan),
                device_id_type=pl.DeviceIdType.MESH,
            )
            if j > 0:
                copy.start()
            else:
                pl.when(group > 0)(copy.start)
        return carry

    lax.fori_loop(0, 16, decode, 0)
    recv_v[me] = send_v[me]
    settle(send_v, recv_v, send_sem.at[8], recv_sem.at[8])

    def unpack(b, carry):
        slab = slab_ref[b]
        rank = jnp.where(low_ref[slab] == b, 0, 1)
        value = recv_v[slab, pl.ds(rank, 1), :]
        out_ref[pl.ds(b, 1), :] = jnp.where(b < count_ref[0], value, 0.0)
        return carry

    lax.fori_loop(0, 128, unpack, 0, unroll=8)


def shards(
    points,
    near_start,
    near_weight,
    dest_slab,
    dest_block,
    live_count,
    lift_w,
    spec_weight,
    skip_w,
    skip_bias,
    proj_in,
    proj_out,
):
    cos, sin = trig()
    chan = lax.axis_index("chan")

    ids = jnp.arange(128, dtype=jnp.int32)
    target = jnp.where(ids < live_count[0], dest_slab[:, 0], -1)
    match = target[None, :] == ids[:, None]
    low = jnp.min(jnp.where(match, ids[None, :], 128), axis=1)
    high = jnp.max(jnp.where(match, ids[None, :], -1), axis=1)

    parts, lines, meta = pl.pallas_call(
        dispatch_kernel,
        out_shape=(
            jax.ShapeDtypeStruct((G, 2 * C, PB), BF),
            jax.ShapeDtypeStruct((G, 1, PB), jnp.int32),
            jax.ShapeDtypeStruct((G, 24, PB), BF),
        ),
        in_specs=[SM, SM, SM, ANY, ANY, ANY, VM],
        out_specs=(ANY, ANY, VM),
        scratch_shapes=[
            pltpu.VMEM((128, C, PB), BF),
            pltpu.VMEM((128, PB), jnp.int32),
            pltpu.VMEM((128, NB, PB), BF),
            pltpu.VMEM((G, 2 * C, PB), BF),
            pltpu.VMEM((G, 1, PB), jnp.int32),
            pltpu.SemaphoreType.DMA((2,)),
            pltpu.SemaphoreType.DMA((2,)),
            pltpu.SemaphoreType.DMA((5,)),
        ],
        compiler_params=pltpu.CompilerParams(
            vmem_limit_bytes=LIMIT, collective_id=0, has_side_effects=True
        ),
    )(low, high, dest_block, points, near_start, near_weight, lift_w)
    mine, theirs = pl.pallas_call(
        gather_kernel,
        grid=(8,),
        out_shape=(
            jax.ShapeDtypeStruct(((G + 1) * HALF, G), F32),
            jax.ShapeDtypeStruct((G * HALF, G), BF),
        ),
        in_specs=[SM, SM, pl.BlockSpec((16, 2 * C, PB), lambda i: (i, 0, 0))],
        out_specs=(
            pl.BlockSpec(((G + 1) * HALF, G), lambda i: (0, 0)),
            pl.BlockSpec((G * HALF, G), lambda i: (0, 0)),
        ),
        scratch_shapes=[pltpu.VMEM(((G + 1) * HALF, G), F32)],
        compiler_params=pltpu.CompilerParams(vmem_limit_bytes=LIMIT),
    )(chan.reshape(1), lines, parts)

    dy = jnp.asarray(np.concatenate([cos.T, -sin.T, -cos.T], axis=0), BF)
    quads = np.concatenate([cos.T, sin.T], axis=1).reshape(4, 2, 1, 4, 2 * G)
    dz = np.broadcast_to(quads, (4, 2, 2, 4, 2 * G)).transpose(1, 0, 2, 3, 4).reshape(2 * M, 2 * G)
    eye4, eye2 = np.eye(4), np.eye(2)
    table = np.stack([cos.T, sin.T])
    forward = np.einsum("hg,vkx,mn->hvkmxgn", eye2, table, eye4).reshape(512, 1024)
    ez = np.zeros((2, 2, 4, 2, 4, 2 * G))
    for h in range(2):
        for side in range(2):
            ez[h, side, :, h, :, :] = quads[:, h if side == 0 else 1 - h, 0]
    ez = ez.reshape(2, 2 * M, 2 * G)
    ey = np.stack([cos, -sin], axis=2).reshape(G, 2 * M) / G**3
    weight = jnp.transpose(spec_weight, (0, 1, 3, 4, 2)).reshape(2, C, 128, C)
    own = chan * HALF
    other = (1 - chan) * HALF
    skip_own = lax.dynamic_slice_in_dim(skip_w, own, HALF, 1)
    skip = jnp.concatenate(
        [
            lax.dynamic_slice_in_dim(skip_own, own, HALF, 0),
            lax.dynamic_slice_in_dim(skip_own, other, HALF, 0),
        ],
        axis=0,
    ).T
    bias = jnp.broadcast_to(lax.dynamic_slice_in_dim(skip_bias, own, HALF, 0)[:, None], (HALF, G))
    plane = (G * HALF, G)
    block8 = pltpu.VMEM((G, 8, 128), BF)
    proj = jnp.concatenate(
        [
            lax.dynamic_slice_in_dim(proj_in, own, HALF, 0),
            lax.dynamic_slice_in_dim(proj_in, other, HALF, 0),
        ],
        axis=0,
    ).T
    proj_row = jnp.broadcast_to(proj_out[None, :], (8, 128))
    return pl.pallas_call(
        middle_kernel,
        out_shape=jax.ShapeDtypeStruct((128, PB), F32),
        in_specs=[SM] * 4 + [ANY] * 6 + [VM] * 8,
        out_specs=VM,
        scratch_shapes=[
            pltpu.VMEM((2, C, 128, C), BF),
            pltpu.VMEM((512, 1024), BF),
            pltpu.VMEM((1024, 512), BF),
            pltpu.SemaphoreType.DMA((5,)),
            pltpu.VMEM((G, HALF, G), BF),
            pltpu.VMEM((G, HALF, G), BF),
            pltpu.VMEM((G, 24, PB), BF),
            pltpu.VMEM((G, 2, PB), F32),
            pltpu.VMEM((G, 2, PB), F32),
            pltpu.VMEM(plane, BF),
            pltpu.VMEM(plane, BF),
            pltpu.VMEM(plane, BF),
            pltpu.VMEM(plane, F32),
            pltpu.VMEM((3 * M * HALF, G), F32),
            pltpu.VMEM((2, 1024, 128), BF),
            pltpu.VMEM((1024, 128), BF),
            block8,
            block8,
            pltpu.VMEM((2, 128, C), F32),
            pltpu.VMEM((512, 128), BF),
            block8,
            block8,
            block8,
            pltpu.VMEM((M * C, G), F32),
            pltpu.SemaphoreType.DMA((9,)),
            pltpu.SemaphoreType.DMA((9,)),
        ],
        compiler_params=pltpu.CompilerParams(
            vmem_limit_bytes=LIMIT, collective_id=1, has_side_effects=True
        ),
    )(
        lines, low, dest_slab[:, 0], live_count, mine, theirs, weight,
        jnp.asarray(forward, BF), jnp.asarray(forward.T, BF), meta,
        dy, jnp.asarray(dz, BF), jnp.asarray(ez, BF), jnp.asarray(ey, BF), skip, bias, proj, proj_row,
    )


def solution(mesh):
    placed = (
        P(("slab", "chan"), None, None),
        P(("slab", "chan"), None),
        P(("slab", "chan"), None, None),
        P(("slab", "chan"), None),
        P(("slab", "chan")),
        P(("slab", "chan")),
        P(),
        P(None, None, None, None, ("slab", "chan")),
        P(),
        P(),
        P(),
        P(),
    )
    return jax.shard_map(
        shards, mesh=mesh, in_specs=placed, out_specs=P(("slab", "chan"), None), check_vma=False
    )
```

```python
import math

import jax
import jax.numpy as jnp
import numpy as np
from jax import lax
from jax.experimental import pallas as pl
from jax.experimental.pallas import tpu as pltpu
from jax.sharding import PartitionSpec as P

G = 128
M = 32
PB = 128
NB = 8
C = 64
HALF = 32
BF = jnp.bfloat16
F32 = jnp.float32
LIMIT = 60 * 1024 * 1024
VM = pl.BlockSpec(memory_space=pltpu.VMEM)
SM = pl.BlockSpec(memory_space=pltpu.SMEM)
ANY = pl.BlockSpec(memory_space=pl.ANY)
SELF = 7


def trig():
    modes = np.concatenate([np.arange(M // 2), np.arange(M // 2) - M // 2])
    phase = (np.arange(G)[:, None] * modes[None, :] % G) * (2.0 * math.pi / G)
    return np.cos(phase), np.sin(phase)


def call(kernel, out_shape, in_specs, scratch=(), out_specs=None):
    return pl.pallas_call(
        kernel,
        out_shape=out_shape,
        in_specs=in_specs,
        out_specs=VM if out_specs is None else out_specs,
        scratch_shapes=list(scratch),
        compiler_params=pltpu.CompilerParams(vmem_limit_bytes=LIMIT),
    )


def dot(left, right, dims=((1,), (0,))):
    return lax.dot_general(left, right, (dims, ((), ())), preferred_element_type=F32)


def gelu(x):
    inner = x * (0.7978845608028654 + 0.035677408136300125 * (x * x))
    half = 0.5 * x
    return half + half * jnp.tanh(inner)


def near_transposed(start, weight):
    base = lax.broadcasted_iota(jnp.int32, (NB, PB), 0) - start
    which = base & 7
    tile = -(base >> 3)
    picked = jnp.zeros((NB, PB), F32)
    for j in range(NB):
        picked = jnp.where(which == j, weight[j : j + 1, :], picked)
    rows = [jnp.where(tile == t, picked, 0.0) for t in range(G // NB)]
    return jnp.concatenate(rows, axis=0).astype(BF)


def dispatch_kernel(
    lo_ref, hi_ref, line_ref, points_hbm, start_hbm, weight_hbm, lift_ref,
    out_ref, got_line_ref, meta_ref,
    points_ref, start_ref, weight_ref, stage, stage_line, send_sem, recv_sem, own_sem,
):
    me, chan = lax.axis_index("slab"), lax.axis_index("chan")
    x, z, y = me >> 5, (me >> 2) & 7, me & 3
    loads = [
        pltpu.make_async_copy(src, dst, own_sem.at[2 + n])
        for n, (src, dst) in enumerate(
            ((points_hbm, points_ref), (start_hbm, start_ref), (weight_hbm, weight_ref))
        )
    ]
    for load in loads:
        load.start()
    barrier = greet_all(me, chan)
    for load in loads:
        load.wait()
    pl.semaphore_wait(barrier, G - 1)
    lane = lax.broadcasted_iota(jnp.int32, (1, PB), 1)
    row = lax.broadcasted_iota(jnp.int32, (8, PB), 0)

    def group(g, carry):
        targets, blocks, nears = [], [], []
        for j in range(8):
            hop = (j + 1) // 2
            to_z = (z + (4 + hop if j % 2 else 4 - hop)) & 7
            to_x = (x + (g >> 2) + j) & 3
            to_y = (y + g + j + j // 4 * 2) & 3
            target = to_x * 32 + to_z * 4 + to_y
            lo, hi = lo_ref[target], hi_ref[target]
            found = [jnp.where(hi >= 0, lo, -1), jnp.where(hi > lo, hi, -1)]
            taken = [jnp.maximum(b, 0) for b in found]
            lines = [jnp.where(b >= 0, line_ref[c] + 1, 0) for b, c in zip(found, taken)]
            starts = [start_ref[pl.ds(c, 1), :] for c in taken]
            info = jnp.where(row == 0, starts[0], jnp.where(row == 1, starts[1], 0))
            weights = [weight_ref[c] for c in taken]
            meta_ref[target, 0:8, :] = weights[0]
            meta_ref[target, 8:16, :] = weights[1]
            meta_ref[target, 16:24, :] = info.astype(F32).astype(BF)
            stage_line[g * 8 + j] = jnp.where(lane == 0, lines[0], jnp.where(lane == 1, lines[1], 0))
            targets.append(target)
            blocks.extend(taken)
            nears.extend(near_transposed(s, w.astype(F32)) for s, w in zip(starts, weights))
        points = jnp.concatenate([points_ref[b] for b in blocks], axis=1)
        lifted = dot(lift_ref[...], points, ((0,), (0,))).astype(BF)
        for j in range(8):
            for r in range(2):
                u = 2 * j + r
                part = dot(lifted[:, u * PB : (u + 1) * PB], nears[u], ((1,), (1,)))
                stage[g * 8 + j, r * C : (r + 1) * C, :] = part.astype(BF)
        for j in range(8):
            for n, (src, dst) in enumerate(((stage_line, got_line_ref), (stage, out_ref))):
                copy = pltpu.make_async_remote_copy(
                    src_ref=src.at[g * 8 + j],
                    dst_ref=dst.at[me],
                    send_sem=send_sem.at[n],
                    recv_sem=recv_sem.at[n],
                    device_id=(targets[j], chan),
                    device_id_type=pl.DeviceIdType.MESH,
                )
                if j < 7:
                    copy.start()
                else:
                    pl.when(g != SELF)(copy.start)
        return carry

    lax.fori_loop(0, 16, group, 0)
    own = [
        pltpu.make_async_copy(stage_line.at[SELF * 8 + 7], got_line_ref.at[me], own_sem.at[0]),
        pltpu.make_async_copy(stage.at[SELF * 8 + 7], out_ref.at[me], own_sem.at[1]),
    ]
    for copy in own:
        copy.start()
    for copy in own:
        copy.wait()
    settle(stage_line, got_line_ref, send_sem.at[0], recv_sem.at[0])
    settle(stage, out_ref, send_sem.at[1], recv_sem.at[1])


def gather_kernel(chan_ref, line_ref, parts_hbm, own_hbm, other_hbm, parts_ref, acc, other, sem):
    def load(k):
        rows = pl.ds(k * 16, 16)
        return pltpu.make_async_copy(parts_hbm.at[rows], parts_ref.at[rows], sem.at[k])

    for k in range(8):
        load(k).start()
    acc[...] = jnp.zeros_like(acc)

    def add(src):
        for r in range(2):
            line = line_ref[src, 0, r]
            line = jnp.where(line > 0, line - 1, G)
            rows = pl.ds(pl.multiple_of(line * HALF, HALF), HALF)
            for h in range(2):
                first = r * C + h * HALF
                acc[h, rows, :] += parts_ref[src, first : first + HALF, :].astype(F32)

    def chunk(k, carry):
        load(k).wait()

        def four(i, carry):
            for u in range(4):
                add(k * 16 + i * 4 + u)
            return carry

        return lax.fori_loop(0, 4, four, carry)

    lax.fori_loop(0, 8, chunk, 0)
    chan = chan_ref[0]
    keep = pltpu.make_async_copy(acc.at[chan, pl.ds(0, G * HALF)], own_hbm, sem.at[8])
    keep.start()
    other[...] = acc[1 - chan, 0 : G * HALF, :].astype(BF)
    give = pltpu.make_async_copy(other, other_hbm, sem.at[9])
    give.start()
    keep.wait()
    give.wait()


def each(first, last, step):
    edge = -(-first // 8) * 8
    for i in range(first, edge):
        step(i)

    def eight(group, carry):
        for u in range(8):
            step(group * 8 + u)
        return carry

    lax.fori_loop(edge // 8, last // 8, eight, 0)


def greet_all(me, chan):
    barrier = pltpu.get_barrier_semaphore()

    def greet(i):
        pl.semaphore_signal(
            barrier, inc=1, device_id=((me + i) & (G - 1), chan), device_id_type=pl.DeviceIdType.MESH
        )

    each(1, G, greet)
    return barrier


def send_blocks(first, last, me, chan, src, dst, send_sem, recv_sem):
    def send(i):
        target = (me + i) & (G - 1)
        pltpu.make_async_remote_copy(
            src_ref=src.at[target],
            dst_ref=dst.at[me],
            send_sem=send_sem,
            recv_sem=recv_sem,
            device_id=(target, chan),
            device_id_type=pl.DeviceIdType.MESH,
        ).start()

    each(first, last, send)


def scatter(me, chan, src, dst, send_sem, recv_sem):
    send_blocks(1, G, me, chan, src, dst, send_sem, recv_sem)
    dst[me] = src[me]


def settle(src, dst, send_sem, recv_sem):
    sent, got = src.at[pl.ds(0, G - 1)], dst.at[pl.ds(0, G - 1)]
    pltpu.make_async_copy(sent, sent, send_sem).wait()
    pltpu.make_async_copy(got, got, recv_sem).wait()


def middle_kernel(
    line_ref, low_ref, slab_ref, count_ref, bias_ref, mine_ref, theirs_ref, weight_hbm, fwd_hbm, bwd_hbm, meta_ref,
    dy_ref, dz_ref, ez_ref, ey_ref, skip_ref, proj_in_ref, proj_out_ref,
    out_ref,
    weight_ref, fwd_ref, bwd_ref, load_sem, nears, skip_rows, bias_rows, proj_rows,
    grid, got_meta, send_v, recv_v,
    got, latent, total, ybuf, spec, spec_other, send_b, recv_b, xbuf, rhs, send_c, recv_c, recv_d, ubuf,
    send_sem, recv_sem,
):
    me, chan = lax.axis_index("slab"), lax.axis_index("chan")
    loads = [
        pltpu.make_async_copy(src, dst, load_sem.at[n])
        for n, (src, dst) in enumerate(
            (
                (mine_ref, total),
                (meta_ref.at[me], got_meta.at[me]),
                (fwd_hbm, fwd_ref),
                (weight_hbm, weight_ref),
                (bwd_hbm, bwd_ref),
            )
        )
    ]
    for load in loads:
        load.start()
    barrier = greet_all(me, chan)
    pl.semaphore_signal(barrier, inc=1, device_id=(me, 1 - chan), device_id_type=pl.DeviceIdType.MESH)
    pl.semaphore_wait(barrier, G)

    def swap(src, dst, index):
        return pltpu.make_async_remote_copy(
            src_ref=src,
            dst_ref=dst,
            send_sem=send_sem.at[index],
            recv_sem=recv_sem.at[index],
            device_id=(me, 1 - chan),
            device_id_type=pl.DeviceIdType.MESH,
        )

    swap_latent = swap(theirs_ref, got, 0)
    swap_latent.start()
    send_blocks(1, G // 2, me, chan, meta_ref, got_meta, send_sem.at[7], recv_sem.at[7])
    skip_rows[...] = skip_ref[...].astype(F32).T
    proj_rows[...] = proj_in_ref[...].astype(F32).T.astype(BF)
    for c in range(HALF):
        bias_rows[c : c + 1, :] = jnp.full((1, G), bias_ref[chan * HALF + c], F32)
    proj_out = jnp.broadcast_to(proj_out_ref[...].astype(F32), (8, 128)).astype(BF)
    loads[0].wait()
    swap_latent.wait()
    total[...] = total[...] + got[...].astype(F32)
    latent[chan] = total[...].astype(BF)
    swap_other = swap(latent.at[chan], latent.at[chan], 1)
    swap_other.start()

    for c in range(HALF):
        plane = total[pl.ds(c, G, stride=HALF), :].astype(BF)
        ybuf[pl.ds(c, 3 * M, stride=HALF), :] = dot(dy_ref[...], plane)
    for q in range(M):
        real = ybuf[q * HALF : (q + 1) * HALF, :].astype(BF)
        imag = ybuf[(M + q) * HALF : (M + q + 1) * HALF, :].astype(BF)
        minus = ybuf[(2 * M + q) * HALF : (2 * M + q + 1) * HALF, :].astype(BF)
        first = jnp.concatenate([real, imag, imag, minus], axis=0)
        second = jnp.concatenate([imag, minus, minus, -imag], axis=0)
        both = jnp.concatenate([first, second], axis=1)
        modes = dot(dz_ref[...], both, ((1,), (1,))).astype(BF)
        spec[0, q * M : (q + 1) * M, :] = modes[:M]
        spec[1, q * M : (q + 1) * M, :] = modes[M:]

    swap_spec = swap(spec.at[1 - chan], spec_other, 2)
    swap_spec.start()
    swap_spec.wait()
    row = lax.broadcasted_iota(jnp.int32, (8, 128), 0)
    from_own = (row // 4) == chan
    for q in range(M):
        own = spec[chan, q * M : (q + 1) * M, :].astype(F32)
        other = spec_other[q * M : (q + 1) * M, :].astype(F32)
        for j in range(4):
            rows = slice(j * 8, (j + 1) * 8)
            send_b[q * 4 + j] = jnp.where(from_own, own[rows], other[rows]).astype(BF)
    scatter(me, chan, send_b, recv_b, send_sem.at[3], recv_sem.at[3])

    swap_other.wait()
    skip = skip_rows[pl.ds(pl.multiple_of(chan * HALF, HALF), HALF), :].astype(BF)

    def mix_channels(group, carry):
        for u in range(8):
            rows = pl.ds(pl.multiple_of((group * 8 + u) * HALF, HALF), HALF)
            both = jnp.concatenate([latent[0, rows, :], latent[1, rows, :]], axis=0)
            total[rows, :] = dot(skip, both) + bias_rows[...]
        return carry

    lax.fori_loop(0, G // 8, mix_channels, 0)
    settle(send_b, recv_b, send_sem.at[3], recv_sem.at[3])
    send_blocks(G // 2, G, me, chan, meta_ref, got_meta, send_sem.at[7], recv_sem.at[7])

    for load in loads[1:]:
        load.wait()
    spectra = recv_b[...].astype(F32).reshape(1024, 128).astype(BF)
    prod = dot(fwd_ref[...], spectra)
    for h in range(2):
        xbuf[h] = prod[h * 256 : h * 256 + 128, 0:64] + prod[h * 256 + 128 : h * 256 + 256, 64:128]

    def chunk(t, carry):
        rows = pl.ds(pl.multiple_of(t * 32, 32), 32)
        real = jnp.zeros((32, C), F32)
        imag = jnp.zeros((32, C), F32)
        for h in range(2):
            x = xbuf[h, rows, :]
            for c in range(HALF):
                wr = weight_ref[0, h * HALF + c, rows, :].astype(F32)
                wi = weight_ref[1, h * HALF + c, rows, :].astype(F32)
                xr = x[:, c : c + 1]
                xi = x[:, HALF + c : HALF + c + 1]
                real = real + xr * wr - xi * wi
                imag = imag + xr * wi + xi * wr
        for h in range(2):
            mr = real[:, h * HALF : (h + 1) * HALF]
            mi = imag[:, h * HALF : (h + 1) * HALF]
            top = jnp.concatenate([mr, mi, -mi, mr], axis=1).astype(BF)
            low = jnp.concatenate([-mi, mr, -mr, -mi], axis=1).astype(BF)
            rhs[pl.ds(pl.multiple_of(h * 256 + t * 32, 32), 32), :] = top
            rhs[pl.ds(pl.multiple_of(h * 256 + 128 + t * 32, 32), 32), :] = low
        return carry

    lax.fori_loop(0, 4, chunk, 0)
    send_c[...] = dot(bwd_ref[...], rhs[...]).reshape(G, 8, 128).astype(BF)
    scatter(me, chan, send_c, recv_c, send_sem.at[4], recv_sem.at[4])

    settle(meta_ref, got_meta, send_sem.at[7], recv_sem.at[7])

    def build(group, carry):
        for u in range(4):
            slab = group * 4 + u
            info = got_meta[slab, 16:24, :].astype(F32).astype(jnp.int32)
            for r in range(2):
                weight = got_meta[slab, r * 8 : (r + 1) * 8, :].astype(F32)
                nears[2 * slab + r] = near_transposed(info[r : r + 1, :], weight)
        return carry

    lax.fori_loop(0, G // 4, build, 0)
    settle(send_c, recv_c, send_sem.at[4], recv_sem.at[4])
    swap_back = swap(recv_c, recv_d, 5)
    swap_back.start()
    swap_back.wait()

    for q in range(M):
        own = recv_c[q * 4 : (q + 1) * 4].astype(F32).reshape(M, 128).astype(BF)
        other = recv_d[q * 4 : (q + 1) * 4].astype(F32).reshape(M, 128).astype(BF)
        lines = jnp.concatenate([own, other], axis=0)
        both = dot(lines, ez_ref[chan], ((0,), (0,)))
        ubuf[q * C : (q + 1) * C, :] = both[0:C, 0:G] + both[C : 2 * C, G : 2 * G]
    for c in range(HALF):
        lines = ubuf[pl.ds(c, 2 * M, stride=HALF), :].astype(BF)
        total[pl.ds(c, G, stride=HALF), :] = total[pl.ds(c, G, stride=HALF), :] + dot(ey_ref[...], lines)

    def finish(group, carry):
        for u in range(4):
            y = group * 4 + u
            rows = pl.ds(pl.multiple_of(y * HALF, HALF), HALF)
            grid[chan, y] = gelu(total[rows, :]).astype(BF)
        return carry

    swaps = []
    for k in range(4):
        lax.fori_loop(k * 8, k * 8 + 8, finish, 0)
        piece = grid.at[chan, pl.ds(k * 32, 32)]
        swaps.append(swap(piece, piece, 9 + k))
        swaps[-1].start()
    for piece in swaps:
        piece.wait()

    def decode(group, carry):
        slabs, values = [], []
        for j in range(8):
            slab = (me + group * 8 + j) & (G - 1)
            slabs.append(slab)
            for r in range(2):
                line = jnp.maximum(line_ref[slab, 0, r] - 1, 0)
                cells = jnp.concatenate([grid[0, line], grid[1, line]], axis=0)
                values.append(dot(cells, nears[2 * slab + r]).astype(BF))
        hidden = gelu(dot(proj_rows[...], jnp.concatenate(values, axis=1))).astype(BF)
        result = dot(proj_out, hidden)
        for j in range(8):
            for r in range(2):
                u = 2 * j + r
                send_v[slabs[j], r : r + 1, :] = result[0:1, u * PB : (u + 1) * PB]
        for j in range(8):
            copy = pltpu.make_async_remote_copy(
                src_ref=send_v.at[slabs[j]],
                dst_ref=recv_v.at[me],
                send_sem=send_sem.at[8],
                recv_sem=recv_sem.at[8],
                device_id=(slabs[j], chan),
                device_id_type=pl.DeviceIdType.MESH,
            )
            if j > 0:
                copy.start()
            else:
                pl.when(group > 0)(copy.start)
        return carry

    lax.fori_loop(0, 16, decode, 0)
    recv_v[me] = send_v[me]
    settle(send_v, recv_v, send_sem.at[8], recv_sem.at[8])

    def unpack(b, carry):
        slab = slab_ref[b]
        rank = jnp.where(low_ref[slab] == b, 0, 1)
        value = recv_v[slab, pl.ds(rank, 1), :]
        out_ref[pl.ds(b, 1), :] = jnp.where(b < count_ref[0], value, 0.0)
        return carry

    lax.fori_loop(0, 128, unpack, 0, unroll=8)


def shards(
    points,
    near_start,
    near_weight,
    dest_slab,
    dest_block,
    live_count,
    lift_w,
    spec_weight,
    skip_w,
    skip_bias,
    proj_in,
    proj_out,
):
    cos, sin = trig()
    chan = lax.axis_index("chan")

    ids = jnp.arange(128, dtype=jnp.int32)
    target = jnp.where(ids < live_count[0], dest_slab[:, 0], -1)
    match = target[None, :] == ids[:, None]
    low = jnp.min(jnp.where(match, ids[None, :], 128), axis=1)
    high = jnp.max(jnp.where(match, ids[None, :], -1), axis=1)

    parts, lines, meta = pl.pallas_call(
        dispatch_kernel,
        out_shape=(
            jax.ShapeDtypeStruct((G, 2 * C, PB), BF),
            jax.ShapeDtypeStruct((G, 1, PB), jnp.int32),
            jax.ShapeDtypeStruct((G, 24, PB), BF),
        ),
        in_specs=[SM, SM, SM, ANY, ANY, ANY, VM],
        out_specs=(ANY, ANY, VM),
        scratch_shapes=[
            pltpu.VMEM((128, C, PB), BF),
            pltpu.VMEM((128, PB), jnp.int32),
            pltpu.VMEM((128, NB, PB), BF),
            pltpu.VMEM((G, 2 * C, PB), BF),
            pltpu.VMEM((G, 1, PB), jnp.int32),
            pltpu.SemaphoreType.DMA((2,)),
            pltpu.SemaphoreType.DMA((2,)),
            pltpu.SemaphoreType.DMA((5,)),
        ],
        compiler_params=pltpu.CompilerParams(
            vmem_limit_bytes=LIMIT, collective_id=0, has_side_effects=True
        ),
    )(low, high, dest_block, points, near_start, near_weight, lift_w)
    mine, theirs = call(
        gather_kernel,
        (jax.ShapeDtypeStruct((G * HALF, G), F32), jax.ShapeDtypeStruct((G * HALF, G), BF)),
        [SM, SM, ANY],
        [
            pltpu.VMEM((G, 2 * C, PB), BF),
            pltpu.VMEM((2, (G + 1) * HALF, G), F32),
            pltpu.VMEM((G * HALF, G), BF),
            pltpu.SemaphoreType.DMA((10,)),
        ],
        (ANY, ANY),
    )(chan.reshape(1), lines, parts)

    dy = jnp.asarray(np.concatenate([cos.T, -sin.T, -cos.T], axis=0), BF)
    quads = np.concatenate([cos.T, sin.T], axis=1).reshape(4, 2, 1, 4, 2 * G)
    dz = np.broadcast_to(quads, (4, 2, 2, 4, 2 * G)).transpose(1, 0, 2, 3, 4).reshape(2 * M, 2 * G)
    eye4, eye2 = np.eye(4), np.eye(2)
    table = np.stack([cos.T, sin.T])
    forward = np.einsum("hg,vkx,mn->hvkmxgn", eye2, table, eye4).reshape(512, 1024)
    ez = np.zeros((2, 2, 4, 2, 4, 2 * G))
    for h in range(2):
        for side in range(2):
            ez[h, side, :, h, :, :] = quads[:, h if side == 0 else 1 - h, 0]
    ez = ez.reshape(2, 2 * M, 2 * G)
    ey = np.stack([cos, -sin], axis=2).reshape(G, 2 * M) / G**3
    weight = jnp.transpose(spec_weight, (0, 1, 3, 4, 2)).reshape(2, C, 128, C)
    plane = (G * HALF, G)
    block8 = pltpu.VMEM((G, 8, 128), BF)
    return pl.pallas_call(
        middle_kernel,
        out_shape=jax.ShapeDtypeStruct((128, PB), F32),
        in_specs=[SM] * 5 + [ANY] * 6 + [VM] * 7,
        out_specs=VM,
        scratch_shapes=[
            pltpu.VMEM((2, C, 128, C), BF),
            pltpu.VMEM((512, 1024), BF),
            pltpu.VMEM((1024, 512), BF),
            pltpu.SemaphoreType.DMA((5,)),
            pltpu.VMEM((2 * G, G, PB), BF),
            pltpu.VMEM((C, C), F32),
            pltpu.VMEM((HALF, G), F32),
            pltpu.VMEM((128, C), BF),
            pltpu.VMEM((2, G, HALF, G), BF),
            pltpu.VMEM((G, 24, PB), BF),
            pltpu.VMEM((G, 2, PB), F32),
            pltpu.VMEM((G, 2, PB), F32),
            pltpu.VMEM(plane, BF),
            pltpu.VMEM((2,) + plane, BF),
            pltpu.VMEM(plane, F32),
            pltpu.VMEM((3 * M * HALF, G), F32),
            pltpu.VMEM((2, 1024, 128), BF),
            pltpu.VMEM((1024, 128), BF),
            block8,
            block8,
            pltpu.VMEM((2, 128, C), F32),
            pltpu.VMEM((512, 128), BF),
            block8,
            block8,
            block8,
            pltpu.VMEM((M * C, G), F32),
            pltpu.SemaphoreType.DMA((13,)),
            pltpu.SemaphoreType.DMA((13,)),
        ],
        compiler_params=pltpu.CompilerParams(
            vmem_limit_bytes=LIMIT, collective_id=1, has_side_effects=True
        ),
    )(
        lines, low, dest_slab[:, 0], live_count, skip_bias, mine, theirs, weight,
        jnp.asarray(forward, BF), jnp.asarray(forward.T, BF), meta,
        dy, jnp.asarray(dz, BF), jnp.asarray(ez, BF), jnp.asarray(ey, BF), skip_w, proj_in,
        proj_out.reshape(1, 128),
    )


def solution(mesh):
    placed = (
        P(("slab", "chan"), None, None),
        P(("slab", "chan"), None),
        P(("slab", "chan"), None, None),
        P(("slab", "chan"), None),
        P(("slab", "chan")),
        P(("slab", "chan")),
        P(),
        P(None, None, None, None, ("slab", "chan")),
        P(),
        P(),
        P(),
        P(),
    )
    return jax.shard_map(
        shards, mesh=mesh, in_specs=placed, out_specs=P(("slab", "chan"), None), check_vma=False
    )
```

```python
import math

import jax
import jax.numpy as jnp
import numpy as np
from jax import lax
from jax.experimental import pallas as pl
from jax.experimental.pallas import tpu as pltpu
from jax.sharding import PartitionSpec as P

G = 128
M = 32
PB = 128
NB = 8
C = 64
HALF = 32
BF = jnp.bfloat16
F32 = jnp.float32
LIMIT = 60 * 1024 * 1024
VM = pl.BlockSpec(memory_space=pltpu.VMEM)
SM = pl.BlockSpec(memory_space=pltpu.SMEM)
ANY = pl.BlockSpec(memory_space=pl.ANY)
SELF = 7


def trig():
    modes = np.concatenate([np.arange(M // 2), np.arange(M // 2) - M // 2])
    phase = (np.arange(G)[:, None] * modes[None, :] % G) * (2.0 * math.pi / G)
    return np.cos(phase), np.sin(phase)


def call(kernel, out_shape, in_specs, scratch=(), out_specs=None):
    return pl.pallas_call(
        kernel,
        out_shape=out_shape,
        in_specs=in_specs,
        out_specs=VM if out_specs is None else out_specs,
        scratch_shapes=list(scratch),
        compiler_params=pltpu.CompilerParams(vmem_limit_bytes=LIMIT),
    )


def dot(left, right, dims=((1,), (0,))):
    return lax.dot_general(left, right, (dims, ((), ())), preferred_element_type=F32)


def gelu(x):
    inner = x * (0.7978845608028654 + 0.035677408136300125 * (x * x))
    half = 0.5 * x
    return half + half * jnp.tanh(inner)


def near_transposed(start, weight):
    base = lax.broadcasted_iota(jnp.int32, (NB, PB), 0) - start
    which = base & 7
    tile = -(base >> 3)
    picked = jnp.zeros((NB, PB), F32)
    for j in range(NB):
        picked = jnp.where(which == j, weight[j : j + 1, :], picked)
    rows = [jnp.where(tile == t, picked, 0.0) for t in range(G // NB)]
    return jnp.concatenate(rows, axis=0).astype(BF)


def dispatch_kernel(
    lo_ref, hi_ref, line_ref, points_hbm, start_hbm, weight_hbm, lift_ref,
    out_ref, got_line_ref, meta_ref,
    points_ref, start_ref, weight_ref, stage, stage_line, send_sem, recv_sem, own_sem,
):
    me, chan = lax.axis_index("slab"), lax.axis_index("chan")
    x, z, y = me >> 5, (me >> 2) & 7, me & 3
    loads = [
        pltpu.make_async_copy(src, dst, own_sem.at[2 + n])
        for n, (src, dst) in enumerate(
            ((points_hbm, points_ref), (start_hbm, start_ref), (weight_hbm, weight_ref))
        )
    ]
    for load in loads:
        load.start()
    barrier = greet_all(me, chan)
    for load in loads:
        load.wait()
    pl.semaphore_wait(barrier, G - 1)
    lane = lax.broadcasted_iota(jnp.int32, (1, PB), 1)
    row = lax.broadcasted_iota(jnp.int32, (8, PB), 0)

    def group(g, carry):
        targets, blocks, nears = [], [], []
        for j in range(8):
            hop = (j + 1) // 2
            to_z = (z + (4 + hop if j % 2 else 4 - hop)) & 7
            to_x = (x + (g >> 2) + j) & 3
            to_y = (y + g + j + j // 4 * 2) & 3
            target = to_x * 32 + to_z * 4 + to_y
            lo, hi = lo_ref[target], hi_ref[target]
            found = [jnp.where(hi >= 0, lo, -1), jnp.where(hi > lo, hi, -1)]
            taken = [jnp.maximum(b, 0) for b in found]
            lines = [jnp.where(b >= 0, line_ref[c] + 1, 0) for b, c in zip(found, taken)]
            starts = [start_ref[pl.ds(c, 1), :] for c in taken]
            info = jnp.where(row == 0, starts[0], jnp.where(row == 1, starts[1], 0))
            weights = [weight_ref[c] for c in taken]
            meta_ref[target, 0:8, :] = weights[0]
            meta_ref[target, 8:16, :] = weights[1]
            meta_ref[target, 16:24, :] = info.astype(F32).astype(BF)
            stage_line[g * 8 + j] = jnp.where(lane == 0, lines[0], jnp.where(lane == 1, lines[1], 0))
            targets.append(target)
            blocks.extend(taken)
            nears.extend(near_transposed(s, w.astype(F32)) for s, w in zip(starts, weights))
        points = jnp.concatenate([points_ref[b] for b in blocks], axis=1)
        lifted = dot(lift_ref[...], points, ((0,), (0,))).astype(BF)
        for j in range(8):
            for r in range(2):
                u = 2 * j + r
                part = dot(lifted[:, u * PB : (u + 1) * PB], nears[u], ((1,), (1,)))
                stage[g * 8 + j, r * C : (r + 1) * C, :] = part.astype(BF)
        for j in range(8):
            for n, (src, dst) in enumerate(((stage_line, got_line_ref), (stage, out_ref))):
                copy = pltpu.make_async_remote_copy(
                    src_ref=src.at[g * 8 + j],
                    dst_ref=dst.at[me],
                    send_sem=send_sem.at[n],
                    recv_sem=recv_sem.at[n],
                    device_id=(targets[j], chan),
                    device_id_type=pl.DeviceIdType.MESH,
                )
                if j < 7:
                    copy.start()
                else:
                    pl.when(g != SELF)(copy.start)
        return carry

    lax.fori_loop(0, 16, group, 0)
    own = [
        pltpu.make_async_copy(stage_line.at[SELF * 8 + 7], got_line_ref.at[me], own_sem.at[0]),
        pltpu.make_async_copy(stage.at[SELF * 8 + 7], out_ref.at[me], own_sem.at[1]),
    ]
    for copy in own:
        copy.start()
    for copy in own:
        copy.wait()
    settle(stage_line, got_line_ref, send_sem.at[0], recv_sem.at[0])
    settle(stage, out_ref, send_sem.at[1], recv_sem.at[1])


def gather_kernel(chan_ref, line_ref, parts_hbm, own_hbm, other_hbm, parts_ref, acc, other, sem):
    def load(k):
        rows = pl.ds(k * 16, 16)
        return pltpu.make_async_copy(parts_hbm.at[rows], parts_ref.at[rows], sem.at[k])

    for k in range(8):
        load(k).start()
    acc[...] = jnp.zeros_like(acc)

    def add(src):
        for r in range(2):
            line = line_ref[src, 0, r]
            line = jnp.where(line > 0, line - 1, G)
            rows = pl.ds(pl.multiple_of(line * HALF, HALF), HALF)
            for h in range(2):
                first = r * C + h * HALF
                acc[h, rows, :] += parts_ref[src, first : first + HALF, :].astype(F32)

    def chunk(k, carry):
        load(k).wait()

        def four(i, carry):
            for u in range(4):
                add(k * 16 + i * 4 + u)
            return carry

        return lax.fori_loop(0, 4, four, carry)

    lax.fori_loop(0, 8, chunk, 0)
    chan = chan_ref[0]
    keep = pltpu.make_async_copy(acc.at[chan, pl.ds(0, G * HALF)], own_hbm, sem.at[8])
    keep.start()
    other[...] = acc[1 - chan, 0 : G * HALF, :].astype(BF)
    give = pltpu.make_async_copy(other, other_hbm, sem.at[9])
    give.start()
    keep.wait()
    give.wait()


def each(first, last, step):
    edge = -(-first // 8) * 8
    for i in range(first, edge):
        step(i)

    def eight(group, carry):
        for u in range(8):
            step(group * 8 + u)
        return carry

    lax.fori_loop(edge // 8, last // 8, eight, 0)


def greet_all(me, chan):
    barrier = pltpu.get_barrier_semaphore()

    def greet(i):
        pl.semaphore_signal(
            barrier, inc=1, device_id=((me + i) & (G - 1), chan), device_id_type=pl.DeviceIdType.MESH
        )

    each(1, G, greet)
    return barrier


def send_blocks(first, last, me, chan, src, dst, send_sem, recv_sem):
    def send(i):
        target = (me + i) & (G - 1)
        pltpu.make_async_remote_copy(
            src_ref=src.at[target],
            dst_ref=dst.at[me],
            send_sem=send_sem,
            recv_sem=recv_sem,
            device_id=(target, chan),
            device_id_type=pl.DeviceIdType.MESH,
        ).start()

    each(first, last, send)


def scatter(me, chan, src, dst, send_sem, recv_sem):
    send_blocks(1, G, me, chan, src, dst, send_sem, recv_sem)
    dst[me] = src[me]


def settle(src, dst, send_sem, recv_sem):
    sent, got = src.at[pl.ds(0, G - 1)], dst.at[pl.ds(0, G - 1)]
    pltpu.make_async_copy(sent, sent, send_sem).wait()
    pltpu.make_async_copy(got, got, recv_sem).wait()


def middle_kernel(
    line_ref, low_ref, slab_ref, count_ref, bias_ref, mine_ref, theirs_ref, weight_hbm, fwd_hbm, bwd_hbm, meta_ref,
    dy_ref, dz_ref, ez_ref, ey_ref, skip_ref, proj_in_ref, proj_out_ref,
    out_ref,
    weight_ref, fwd_ref, bwd_ref, load_sem, nears, skip_rows, bias_rows, proj_rows,
    grid, got_meta, send_v, recv_v,
    got, latent, total, ybuf, spec, spec_other, send_b, recv_b, xbuf, rhs, send_c, recv_c, recv_d, ubuf,
    send_sem, recv_sem,
):
    me, chan = lax.axis_index("slab"), lax.axis_index("chan")
    loads = [
        pltpu.make_async_copy(src, dst, load_sem.at[n])
        for n, (src, dst) in enumerate(
            (
                (mine_ref, total),
                (meta_ref.at[me], got_meta.at[me]),
                (fwd_hbm, fwd_ref),
                (weight_hbm, weight_ref),
                (bwd_hbm, bwd_ref),
            )
        )
    ]
    for load in loads:
        load.start()
    barrier = greet_all(me, chan)
    pl.semaphore_signal(barrier, inc=1, device_id=(me, 1 - chan), device_id_type=pl.DeviceIdType.MESH)
    pl.semaphore_wait(barrier, G)

    def swap(src, dst, index):
        return pltpu.make_async_remote_copy(
            src_ref=src,
            dst_ref=dst,
            send_sem=send_sem.at[index],
            recv_sem=recv_sem.at[index],
            device_id=(me, 1 - chan),
            device_id_type=pl.DeviceIdType.MESH,
        )

    swap_latent = swap(theirs_ref, got, 0)
    swap_latent.start()
    send_blocks(1, G // 2, me, chan, meta_ref, got_meta, send_sem.at[7], recv_sem.at[7])
    skip_rows[...] = skip_ref[...].astype(F32).T
    proj_rows[...] = proj_in_ref[...].astype(F32).T.astype(BF)
    for c in range(HALF):
        bias_rows[c : c + 1, :] = jnp.full((1, G), bias_ref[chan * HALF + c], F32)
    proj_out = jnp.broadcast_to(proj_out_ref[...].astype(F32), (8, 128)).astype(BF)
    loads[0].wait()
    swap_latent.wait()
    total[...] = total[...] + got[...].astype(F32)
    latent[chan] = total[...].astype(BF)
    swap_other = swap(latent.at[chan], latent.at[chan], 1)
    swap_other.start()

    for c in range(HALF):
        plane = total[pl.ds(c, G, stride=HALF), :].astype(BF)
        ybuf[pl.ds(c, 3 * M, stride=HALF), :] = dot(dy_ref[...], plane)
    for q in range(M):
        real = ybuf[q * HALF : (q + 1) * HALF, :].astype(BF)
        imag = ybuf[(M + q) * HALF : (M + q + 1) * HALF, :].astype(BF)
        minus = ybuf[(2 * M + q) * HALF : (2 * M + q + 1) * HALF, :].astype(BF)
        first = jnp.concatenate([real, imag, imag, minus], axis=0)
        second = jnp.concatenate([imag, minus, minus, -imag], axis=0)
        both = jnp.concatenate([first, second], axis=1)
        modes = dot(dz_ref[...], both, ((1,), (1,))).astype(BF)
        spec[0, q * M : (q + 1) * M, :] = modes[:M]
        spec[1, q * M : (q + 1) * M, :] = modes[M:]

    swap_spec = swap(spec.at[1 - chan], spec_other, 2)
    swap_spec.start()

    swap_other.wait()
    skip = skip_rows[pl.ds(pl.multiple_of(chan * HALF, HALF), HALF), :].astype(BF)

    def mix_channels(group, carry):
        for u in range(8):
            rows = pl.ds(pl.multiple_of((group * 8 + u) * HALF, HALF), HALF)
            both = jnp.concatenate([latent[0, rows, :], latent[1, rows, :]], axis=0)
            total[rows, :] = dot(skip, both) + bias_rows[...]
        return carry

    lax.fori_loop(0, G // 16, mix_channels, 0)
    swap_spec.wait()
    row = lax.broadcasted_iota(jnp.int32, (8, 128), 0)
    from_own = (row // 4) == chan
    for q in range(M):
        own = spec[chan, q * M : (q + 1) * M, :].astype(F32)
        other = spec_other[q * M : (q + 1) * M, :].astype(F32)
        for j in range(4):
            rows = slice(j * 8, (j + 1) * 8)
            send_b[q * 4 + j] = jnp.where(from_own, own[rows], other[rows]).astype(BF)
    scatter(me, chan, send_b, recv_b, send_sem.at[3], recv_sem.at[3])

    lax.fori_loop(G // 16, G // 8, mix_channels, 0)
    settle(send_b, recv_b, send_sem.at[3], recv_sem.at[3])
    send_blocks(G // 2, G, me, chan, meta_ref, got_meta, send_sem.at[7], recv_sem.at[7])

    for load in loads[1:]:
        load.wait()
    spectra = recv_b[...].astype(F32).reshape(1024, 128).astype(BF)
    prod = dot(fwd_ref[...], spectra)
    for h in range(2):
        xbuf[h] = prod[h * 256 : h * 256 + 128, 0:64] + prod[h * 256 + 128 : h * 256 + 256, 64:128]

    def chunk(t, carry):
        rows = pl.ds(pl.multiple_of(t * 32, 32), 32)
        real = jnp.zeros((32, C), F32)
        imag = jnp.zeros((32, C), F32)
        for h in range(2):
            x = xbuf[h, rows, :]
            for c in range(HALF):
                wr = weight_ref[0, h * HALF + c, rows, :].astype(F32)
                wi = weight_ref[1, h * HALF + c, rows, :].astype(F32)
                xr = x[:, c : c + 1]
                xi = x[:, HALF + c : HALF + c + 1]
                real = real + xr * wr - xi * wi
                imag = imag + xr * wi + xi * wr
        for h in range(2):
            mr = real[:, h * HALF : (h + 1) * HALF]
            mi = imag[:, h * HALF : (h + 1) * HALF]
            top = jnp.concatenate([mr, mi, -mi, mr], axis=1).astype(BF)
            low = jnp.concatenate([-mi, mr, -mr, -mi], axis=1).astype(BF)
            rhs[pl.ds(pl.multiple_of(h * 256 + t * 32, 32), 32), :] = top
            rhs[pl.ds(pl.multiple_of(h * 256 + 128 + t * 32, 32), 32), :] = low
        return carry

    lax.fori_loop(0, 4, chunk, 0)
    send_c[...] = dot(bwd_ref[...], rhs[...]).reshape(G, 8, 128).astype(BF)
    scatter(me, chan, send_c, recv_c, send_sem.at[4], recv_sem.at[4])

    settle(meta_ref, got_meta, send_sem.at[7], recv_sem.at[7])

    def build(group, carry):
        for u in range(4):
            slab = group * 4 + u
            info = got_meta[slab, 16:24, :].astype(F32).astype(jnp.int32)
            for r in range(2):
                weight = got_meta[slab, r * 8 : (r + 1) * 8, :].astype(F32)
                nears[2 * slab + r] = near_transposed(info[r : r + 1, :], weight)
        return carry

    lax.fori_loop(0, G // 8, build, 0)
    settle(send_c, recv_c, send_sem.at[4], recv_sem.at[4])
    swap_back = swap(recv_c, recv_d, 5)
    swap_back.start()
    lax.fori_loop(G // 8, G // 4, build, 0)
    swap_back.wait()

    for q in range(M):
        own = recv_c[q * 4 : (q + 1) * 4].astype(F32).reshape(M, 128).astype(BF)
        other = recv_d[q * 4 : (q + 1) * 4].astype(F32).reshape(M, 128).astype(BF)
        lines = jnp.concatenate([own, other], axis=0)
        both = dot(lines, ez_ref[chan], ((0,), (0,)))
        ubuf[q * C : (q + 1) * C, :] = both[0:C, 0:G] + both[C : 2 * C, G : 2 * G]
    for c in range(HALF):
        lines = ubuf[pl.ds(c, 2 * M, stride=HALF), :].astype(BF)
        total[pl.ds(c, G, stride=HALF), :] = total[pl.ds(c, G, stride=HALF), :] + dot(ey_ref[...], lines)

    def finish(group, carry):
        for u in range(4):
            y = group * 4 + u
            rows = pl.ds(pl.multiple_of(y * HALF, HALF), HALF)
            grid[chan, y] = gelu(total[rows, :]).astype(BF)
        return carry

    swaps = []
    for k in range(4):
        lax.fori_loop(k * 8, k * 8 + 8, finish, 0)
        piece = grid.at[chan, pl.ds(k * 32, 32)]
        swaps.append(swap(piece, piece, 9 + k))
        swaps[-1].start()
    for piece in swaps:
        piece.wait()

    def decode(group, carry):
        slabs, values = [], []
        for j in range(16):
            slab = (me + group * 16 + j) & (G - 1)
            slabs.append(slab)
            for r in range(2):
                line = jnp.maximum(line_ref[slab, 0, r] - 1, 0)
                cells = jnp.concatenate([grid[0, line], grid[1, line]], axis=0)
                values.append(dot(cells, nears[2 * slab + r]).astype(BF))
        hidden = gelu(dot(proj_rows[...], jnp.concatenate(values, axis=1))).astype(BF)
        result = dot(proj_out, hidden)
        for j in range(16):
            for r in range(2):
                u = 2 * j + r
                send_v[slabs[j], r : r + 1, :] = result[0:1, u * PB : (u + 1) * PB]
        for j in range(16):
            copy = pltpu.make_async_remote_copy(
                src_ref=send_v.at[slabs[j]],
                dst_ref=recv_v.at[me],
                send_sem=send_sem.at[8],
                recv_sem=recv_sem.at[8],
                device_id=(slabs[j], chan),
                device_id_type=pl.DeviceIdType.MESH,
            )
            if j > 0:
                copy.start()
            else:
                pl.when(group > 0)(copy.start)
        return carry

    lax.fori_loop(0, 8, decode, 0)
    recv_v[me] = send_v[me]
    settle(send_v, recv_v, send_sem.at[8], recv_sem.at[8])

    def unpack(b, carry):
        slab = slab_ref[b]
        rank = jnp.where(low_ref[slab] == b, 0, 1)
        value = recv_v[slab, pl.ds(rank, 1), :]
        out_ref[pl.ds(b, 1), :] = jnp.where(b < count_ref[0], value, 0.0)
        return carry

    lax.fori_loop(0, 128, unpack, 0, unroll=8)


def shards(
    points,
    near_start,
    near_weight,
    dest_slab,
    dest_block,
    live_count,
    lift_w,
    spec_weight,
    skip_w,
    skip_bias,
    proj_in,
    proj_out,
):
    cos, sin = trig()
    chan = lax.axis_index("chan")

    ids = jnp.arange(128, dtype=jnp.int32)
    target = jnp.where(ids < live_count[0], dest_slab[:, 0], -1)
    match = target[None, :] == ids[:, None]
    low = jnp.min(jnp.where(match, ids[None, :], 128), axis=1)
    high = jnp.max(jnp.where(match, ids[None, :], -1), axis=1)

    parts, lines, meta = pl.pallas_call(
        dispatch_kernel,
        out_shape=(
            jax.ShapeDtypeStruct((G, 2 * C, PB), BF),
            jax.ShapeDtypeStruct((G, 1, PB), jnp.int32),
            jax.ShapeDtypeStruct((G, 24, PB), BF),
        ),
        in_specs=[SM, SM, SM, ANY, ANY, ANY, VM],
        out_specs=(ANY, ANY, VM),
        scratch_shapes=[
            pltpu.VMEM((128, C, PB), BF),
            pltpu.VMEM((128, PB), jnp.int32),
            pltpu.VMEM((128, NB, PB), BF),
            pltpu.VMEM((G, 2 * C, PB), BF),
            pltpu.VMEM((G, 1, PB), jnp.int32),
            pltpu.SemaphoreType.DMA((2,)),
            pltpu.SemaphoreType.DMA((2,)),
            pltpu.SemaphoreType.DMA((5,)),
        ],
        compiler_params=pltpu.CompilerParams(
            vmem_limit_bytes=LIMIT, collective_id=0, has_side_effects=True
        ),
    )(low, high, dest_block, points, near_start, near_weight, lift_w)
    mine, theirs = call(
        gather_kernel,
        (jax.ShapeDtypeStruct((G * HALF, G), F32), jax.ShapeDtypeStruct((G * HALF, G), BF)),
        [SM, SM, ANY],
        [
            pltpu.VMEM((G, 2 * C, PB), BF),
            pltpu.VMEM((2, (G + 1) * HALF, G), F32),
            pltpu.VMEM((G * HALF, G), BF),
            pltpu.SemaphoreType.DMA((10,)),
        ],
        (ANY, ANY),
    )(chan.reshape(1), lines, parts)

    dy = jnp.asarray(np.concatenate([cos.T, -sin.T, -cos.T], axis=0), BF)
    quads = np.concatenate([cos.T, sin.T], axis=1).reshape(4, 2, 1, 4, 2 * G)
    dz = np.broadcast_to(quads, (4, 2, 2, 4, 2 * G)).transpose(1, 0, 2, 3, 4).reshape(2 * M, 2 * G)
    eye4, eye2 = np.eye(4), np.eye(2)
    table = np.stack([cos.T, sin.T])
    forward = np.einsum("hg,vkx,mn->hvkmxgn", eye2, table, eye4).reshape(512, 1024)
    ez = np.zeros((2, 2, 4, 2, 4, 2 * G))
    for h in range(2):
        for side in range(2):
            ez[h, side, :, h, :, :] = quads[:, h if side == 0 else 1 - h, 0]
    ez = ez.reshape(2, 2 * M, 2 * G)
    ey = np.stack([cos, -sin], axis=2).reshape(G, 2 * M) / G**3
    weight = jnp.transpose(spec_weight, (0, 1, 3, 4, 2)).reshape(2, C, 128, C)
    plane = (G * HALF, G)
    block8 = pltpu.VMEM((G, 8, 128), BF)
    return pl.pallas_call(
        middle_kernel,
        out_shape=jax.ShapeDtypeStruct((128, PB), F32),
        in_specs=[SM] * 5 + [ANY] * 6 + [VM] * 7,
        out_specs=VM,
        scratch_shapes=[
            pltpu.VMEM((2, C, 128, C), BF),
            pltpu.VMEM((512, 1024), BF),
            pltpu.VMEM((1024, 512), BF),
            pltpu.SemaphoreType.DMA((5,)),
            pltpu.VMEM((2 * G, G, PB), BF),
            pltpu.VMEM((C, C), F32),
            pltpu.VMEM((HALF, G), F32),
            pltpu.VMEM((128, C), BF),
            pltpu.VMEM((2, G, HALF, G), BF),
            pltpu.VMEM((G, 24, PB), BF),
            pltpu.VMEM((G, 2, PB), F32),
            pltpu.VMEM((G, 2, PB), F32),
            pltpu.VMEM(plane, BF),
            pltpu.VMEM((2,) + plane, BF),
            pltpu.VMEM(plane, F32),
            pltpu.VMEM((3 * M * HALF, G), F32),
            pltpu.VMEM((2, 1024, 128), BF),
            pltpu.VMEM((1024, 128), BF),
            block8,
            block8,
            pltpu.VMEM((2, 128, C), F32),
            pltpu.VMEM((512, 128), BF),
            block8,
            block8,
            block8,
            pltpu.VMEM((M * C, G), F32),
            pltpu.SemaphoreType.DMA((13,)),
            pltpu.SemaphoreType.DMA((13,)),
        ],
        compiler_params=pltpu.CompilerParams(
            vmem_limit_bytes=LIMIT, collective_id=1, has_side_effects=True
        ),
    )(
        lines, low, dest_slab[:, 0], live_count, skip_bias, mine, theirs, weight,
        jnp.asarray(forward, BF), jnp.asarray(forward.T, BF), meta,
        dy, jnp.asarray(dz, BF), jnp.asarray(ez, BF), jnp.asarray(ey, BF), skip_w, proj_in,
        proj_out.reshape(1, 128),
    )


def solution(mesh):
    placed = (
        P(("slab", "chan"), None, None),
        P(("slab", "chan"), None),
        P(("slab", "chan"), None, None),
        P(("slab", "chan"), None),
        P(("slab", "chan")),
        P(("slab", "chan")),
        P(),
        P(None, None, None, None, ("slab", "chan")),
        P(),
        P(),
        P(),
        P(),
    )
    return jax.shard_map(
        shards, mesh=mesh, in_specs=placed, out_specs=P(("slab", "chan"), None), check_vma=False
    )
```

```python
import math

import jax
import jax.numpy as jnp
import numpy as np
from jax import lax
from jax.experimental import pallas as pl
from jax.experimental.pallas import tpu as pltpu
from jax.sharding import PartitionSpec as P

G = 128
M = 32
PB = 128
NB = 8
C = 64
HALF = 32
BF = jnp.bfloat16
F32 = jnp.float32
LIMIT = 60 * 1024 * 1024
VM = pl.BlockSpec(memory_space=pltpu.VMEM)
SM = pl.BlockSpec(memory_space=pltpu.SMEM)
ANY = pl.BlockSpec(memory_space=pl.ANY)
SELF = 7


def trig():
    modes = np.concatenate([np.arange(M // 2), np.arange(M // 2) - M // 2])
    phase = (np.arange(G)[:, None] * modes[None, :] % G) * (2.0 * math.pi / G)
    return np.cos(phase), np.sin(phase)


def call(kernel, out_shape, in_specs, scratch=(), out_specs=None):
    return pl.pallas_call(
        kernel,
        out_shape=out_shape,
        in_specs=in_specs,
        out_specs=VM if out_specs is None else out_specs,
        scratch_shapes=list(scratch),
        compiler_params=pltpu.CompilerParams(vmem_limit_bytes=LIMIT),
    )


def dot(left, right, dims=((1,), (0,))):
    return lax.dot_general(left, right, (dims, ((), ())), preferred_element_type=F32)


def gelu(x):
    inner = x * (0.7978845608028654 + 0.035677408136300125 * (x * x))
    half = 0.5 * x
    return half + half * jnp.tanh(inner)


def near_transposed(start, weight):
    base = lax.broadcasted_iota(jnp.int32, (NB, PB), 0) - start
    which = base & 7
    tile = -(base >> 3)
    picked = jnp.zeros((NB, PB), F32)
    for j in range(NB):
        picked = jnp.where(which == j, weight[j : j + 1, :], picked)
    rows = [jnp.where(tile == t, picked, 0.0) for t in range(G // NB)]
    return jnp.concatenate(rows, axis=0).astype(BF)


def dispatch_kernel(
    lo_ref, hi_ref, line_ref, points_hbm, start_hbm, weight_hbm, lift_ref,
    out_ref, got_line_ref, meta_ref,
    points_ref, start_ref, weight_ref, stage, stage_line, send_sem, recv_sem, own_sem,
):
    me, chan = lax.axis_index("slab"), lax.axis_index("chan")
    x, z, y = me >> 5, (me >> 2) & 7, me & 3
    loads = [
        pltpu.make_async_copy(src, dst, own_sem.at[2 + n])
        for n, (src, dst) in enumerate(
            ((points_hbm, points_ref), (start_hbm, start_ref), (weight_hbm, weight_ref))
        )
    ]
    for load in loads:
        load.start()
    barrier = greet_all(me, chan)
    for load in loads:
        load.wait()
    pl.semaphore_wait(barrier, G - 1)
    lane = lax.broadcasted_iota(jnp.int32, (1, PB), 1)
    row = lax.broadcasted_iota(jnp.int32, (8, PB), 0)

    def group(g, carry):
        targets, blocks, nears = [], [], []
        for j in range(8):
            hop = (j + 1) // 2
            to_z = (z + (4 + hop if j % 2 else 4 - hop)) & 7
            to_x = (x + (g >> 2) + j) & 3
            to_y = (y + g + j + j // 4 * 2) & 3
            target = to_x * 32 + to_z * 4 + to_y
            lo, hi = lo_ref[target], hi_ref[target]
            found = [jnp.where(hi >= 0, lo, -1), jnp.where(hi > lo, hi, -1)]
            taken = [jnp.maximum(b, 0) for b in found]
            lines = [jnp.where(b >= 0, line_ref[c] + 1, 0) for b, c in zip(found, taken)]
            starts = [start_ref[pl.ds(c, 1), :] for c in taken]
            info = jnp.where(row == 0, starts[0], jnp.where(row == 1, starts[1], 0))
            weights = [weight_ref[c] for c in taken]
            meta_ref[target, 0:8, :] = weights[0]
            meta_ref[target, 8:16, :] = weights[1]
            meta_ref[target, 16:24, :] = info.astype(F32).astype(BF)
            stage_line[g * 8 + j] = jnp.where(lane == 0, lines[0], jnp.where(lane == 1, lines[1], 0))
            targets.append(target)
            blocks.extend(taken)
            nears.extend(near_transposed(s, w.astype(F32)) for s, w in zip(starts, weights))
        points = jnp.concatenate([points_ref[b] for b in blocks], axis=1)
        lifted = dot(lift_ref[...], points, ((0,), (0,))).astype(BF)
        for j in range(8):
            for r in range(2):
                u = 2 * j + r
                part = dot(lifted[:, u * PB : (u + 1) * PB], nears[u], ((1,), (1,)))
                stage[g * 8 + j, r * C : (r + 1) * C, :] = part.astype(BF)
        for j in range(8):
            for n, (src, dst) in enumerate(((stage_line, got_line_ref), (stage, out_ref))):
                copy = pltpu.make_async_remote_copy(
                    src_ref=src.at[g * 8 + j],
                    dst_ref=dst.at[me],
                    send_sem=send_sem.at[n],
                    recv_sem=recv_sem.at[n],
                    device_id=(targets[j], chan),
                    device_id_type=pl.DeviceIdType.MESH,
                )
                if j < 7:
                    copy.start()
                else:
                    pl.when(g != SELF)(copy.start)
        return carry

    lax.fori_loop(0, 16, group, 0)
    own = [
        pltpu.make_async_copy(stage_line.at[SELF * 8 + 7], got_line_ref.at[me], own_sem.at[0]),
        pltpu.make_async_copy(stage.at[SELF * 8 + 7], out_ref.at[me], own_sem.at[1]),
    ]
    for copy in own:
        copy.start()
    for copy in own:
        copy.wait()
    settle(stage_line, got_line_ref, send_sem.at[0], recv_sem.at[0])
    settle(stage, out_ref, send_sem.at[1], recv_sem.at[1])


def gather_kernel(chan_ref, line_ref, parts_hbm, own_hbm, other_hbm, parts_ref, acc, other, sem):
    def load(k):
        rows = pl.ds(k * 16, 16)
        return pltpu.make_async_copy(parts_hbm.at[rows], parts_ref.at[rows], sem.at[k])

    for k in range(8):
        load(k).start()
    acc[...] = jnp.zeros_like(acc)

    def add(src):
        for r in range(2):
            line = line_ref[src, 0, r]
            line = jnp.where(line > 0, line - 1, G)
            rows = pl.ds(pl.multiple_of(line * HALF, HALF), HALF)
            for h in range(2):
                first = r * C + h * HALF
                acc[h, rows, :] += parts_ref[src, first : first + HALF, :].astype(F32)

    def chunk(k, carry):
        load(k).wait()

        def four(i, carry):
            for u in range(4):
                add(k * 16 + i * 4 + u)
            return carry

        return lax.fori_loop(0, 4, four, carry)

    lax.fori_loop(0, 8, chunk, 0)
    chan = chan_ref[0]
    keep = pltpu.make_async_copy(acc.at[chan, pl.ds(0, G * HALF)], own_hbm, sem.at[8])
    keep.start()
    other[...] = acc[1 - chan, 0 : G * HALF, :].astype(BF)
    give = pltpu.make_async_copy(other, other_hbm, sem.at[9])
    give.start()
    keep.wait()
    give.wait()


def each(first, last, step):
    edge = -(-first // 8) * 8
    for i in range(first, edge):
        step(i)

    def eight(group, carry):
        for u in range(8):
            step(group * 8 + u)
        return carry

    lax.fori_loop(edge // 8, last // 8, eight, 0)


def greet_all(me, chan):
    barrier = pltpu.get_barrier_semaphore()

    def greet(i):
        pl.semaphore_signal(
            barrier, inc=1, device_id=(me ^ i, chan), device_id_type=pl.DeviceIdType.MESH
        )

    each(1, G, greet)
    return barrier


def send_blocks(first, last, me, chan, src, dst, send_sem, recv_sem):
    def send(i):
        target = me ^ i
        pltpu.make_async_remote_copy(
            src_ref=src.at[target],
            dst_ref=dst.at[me],
            send_sem=send_sem,
            recv_sem=recv_sem,
            device_id=(target, chan),
            device_id_type=pl.DeviceIdType.MESH,
        ).start()

    each(first, last, send)


def scatter(me, chan, src, dst, send_sem, recv_sem):
    send_blocks(1, G, me, chan, src, dst, send_sem, recv_sem)
    dst[me] = src[me]


def settle(src, dst, send_sem, recv_sem):
    sent, got = src.at[pl.ds(0, G - 1)], dst.at[pl.ds(0, G - 1)]
    pltpu.make_async_copy(sent, sent, send_sem).wait()
    pltpu.make_async_copy(got, got, recv_sem).wait()


def middle_kernel(
    line_ref, low_ref, slab_ref, count_ref, bias_ref, mine_ref, theirs_ref, weight_hbm, fwd_hbm, bwd_hbm, meta_ref,
    dy_ref, dz_ref, ez_ref, ey_ref, skip_ref, proj_in_ref, proj_out_ref,
    out_ref,
    weight_ref, fwd_ref, bwd_ref, load_sem, nears, skip_rows, bias_rows, proj_rows,
    grid, got_meta, send_v, recv_v,
    got, latent, total, ybuf, spec, spec_other, send_b, recv_b, xbuf, rhs, send_c, recv_c, recv_d, ubuf,
    send_sem, recv_sem,
):
    me, chan = lax.axis_index("slab"), lax.axis_index("chan")
    loads = [
        pltpu.make_async_copy(src, dst, load_sem.at[n])
        for n, (src, dst) in enumerate(
            (
                (mine_ref, total),
                (meta_ref.at[me], got_meta.at[me]),
                (fwd_hbm, fwd_ref),
                (weight_hbm, weight_ref),
                (bwd_hbm, bwd_ref),
            )
        )
    ]
    for load in loads:
        load.start()
    barrier = greet_all(me, chan)
    pl.semaphore_signal(barrier, inc=1, device_id=(me, 1 - chan), device_id_type=pl.DeviceIdType.MESH)
    pl.semaphore_wait(barrier, G)

    def swap(src, dst, index):
        return pltpu.make_async_remote_copy(
            src_ref=src,
            dst_ref=dst,
            send_sem=send_sem.at[index],
            recv_sem=recv_sem.at[index],
            device_id=(me, 1 - chan),
            device_id_type=pl.DeviceIdType.MESH,
        )

    swap_latent = swap(theirs_ref, got, 0)
    swap_latent.start()
    send_blocks(1, G // 2, me, chan, meta_ref, got_meta, send_sem.at[7], recv_sem.at[7])
    skip_rows[...] = skip_ref[...].astype(F32).T
    proj_rows[...] = proj_in_ref[...].astype(F32).T.astype(BF)
    for c in range(HALF):
        bias_rows[c : c + 1, :] = jnp.full((1, G), bias_ref[chan * HALF + c], F32)
    proj_out = jnp.broadcast_to(proj_out_ref[...].astype(F32), (8, 128)).astype(BF)
    loads[0].wait()
    swap_latent.wait()
    total[...] = total[...] + got[...].astype(F32)
    latent[chan] = total[...].astype(BF)
    swap_other = swap(latent.at[chan], latent.at[chan], 1)
    swap_other.start()

    for c in range(HALF):
        plane = total[pl.ds(c, G, stride=HALF), :].astype(BF)
        ybuf[pl.ds(c, 3 * M, stride=HALF), :] = dot(dy_ref[...], plane)
    for q in range(M):
        real = ybuf[q * HALF : (q + 1) * HALF, :].astype(BF)
        imag = ybuf[(M + q) * HALF : (M + q + 1) * HALF, :].astype(BF)
        minus = ybuf[(2 * M + q) * HALF : (2 * M + q + 1) * HALF, :].astype(BF)
        first = jnp.concatenate([real, imag, imag, minus], axis=0)
        second = jnp.concatenate([imag, minus, minus, -imag], axis=0)
        both = jnp.concatenate([first, second], axis=1)
        modes = dot(dz_ref[...], both, ((1,), (1,))).astype(BF)
        spec[0, q * M : (q + 1) * M, :] = modes[:M]
        spec[1, q * M : (q + 1) * M, :] = modes[M:]

    swap_spec = swap(spec.at[1 - chan], spec_other, 2)
    swap_spec.start()

    swap_other.wait()
    skip = skip_rows[pl.ds(pl.multiple_of(chan * HALF, HALF), HALF), :].astype(BF)

    def mix_channels(group, carry):
        for u in range(8):
            rows = pl.ds(pl.multiple_of((group * 8 + u) * HALF, HALF), HALF)
            both = jnp.concatenate([latent[0, rows, :], latent[1, rows, :]], axis=0)
            total[rows, :] = dot(skip, both) + bias_rows[...]
        return carry

    lax.fori_loop(0, G // 16, mix_channels, 0)
    swap_spec.wait()
    row = lax.broadcasted_iota(jnp.int32, (8, 128), 0)
    from_own = (row // 4) == chan
    for q in range(M):
        own = spec[chan, q * M : (q + 1) * M, :].astype(F32)
        other = spec_other[q * M : (q + 1) * M, :].astype(F32)
        for j in range(4):
            rows = slice(j * 8, (j + 1) * 8)
            send_b[q * 4 + j] = jnp.where(from_own, own[rows], other[rows]).astype(BF)
    scatter(me, chan, send_b, recv_b, send_sem.at[3], recv_sem.at[3])

    lax.fori_loop(G // 16, G // 8, mix_channels, 0)
    settle(send_b, recv_b, send_sem.at[3], recv_sem.at[3])
    send_blocks(G // 2, G, me, chan, meta_ref, got_meta, send_sem.at[7], recv_sem.at[7])

    for load in loads[1:]:
        load.wait()
    spectra = recv_b[...].astype(F32).reshape(1024, 128).astype(BF)
    prod = dot(fwd_ref[...], spectra)
    for h in range(2):
        xbuf[h] = prod[h * 256 : h * 256 + 128, 0:64] + prod[h * 256 + 128 : h * 256 + 256, 64:128]

    def chunk(t, carry):
        rows = pl.ds(pl.multiple_of(t * 32, 32), 32)
        real = jnp.zeros((32, C), F32)
        imag = jnp.zeros((32, C), F32)
        for h in range(2):
            x = xbuf[h, rows, :]
            for c in range(HALF):
                wr = weight_ref[0, h * HALF + c, rows, :].astype(F32)
                wi = weight_ref[1, h * HALF + c, rows, :].astype(F32)
                xr = x[:, c : c + 1]
                xi = x[:, HALF + c : HALF + c + 1]
                real = real + xr * wr - xi * wi
                imag = imag + xr * wi + xi * wr
        for h in range(2):
            mr = real[:, h * HALF : (h + 1) * HALF]
            mi = imag[:, h * HALF : (h + 1) * HALF]
            top = jnp.concatenate([mr, mi, -mi, mr], axis=1).astype(BF)
            low = jnp.concatenate([-mi, mr, -mr, -mi], axis=1).astype(BF)
            rhs[pl.ds(pl.multiple_of(h * 256 + t * 32, 32), 32), :] = top
            rhs[pl.ds(pl.multiple_of(h * 256 + 128 + t * 32, 32), 32), :] = low
        return carry

    lax.fori_loop(0, 4, chunk, 0)
    send_c[...] = dot(bwd_ref[...], rhs[...]).reshape(G, 8, 128).astype(BF)
    scatter(me, chan, send_c, recv_c, send_sem.at[4], recv_sem.at[4])

    settle(meta_ref, got_meta, send_sem.at[7], recv_sem.at[7])

    def build(group, carry):
        for u in range(4):
            slab = group * 4 + u
            info = got_meta[slab, 16:24, :].astype(F32).astype(jnp.int32)
            for r in range(2):
                weight = got_meta[slab, r * 8 : (r + 1) * 8, :].astype(F32)
                nears[2 * slab + r] = near_transposed(info[r : r + 1, :], weight)
        return carry

    lax.fori_loop(0, G // 8, build, 0)
    settle(send_c, recv_c, send_sem.at[4], recv_sem.at[4])
    swap_back = swap(recv_c, recv_d, 5)
    swap_back.start()
    lax.fori_loop(G // 8, G // 4, build, 0)
    swap_back.wait()

    for q in range(M):
        own = recv_c[q * 4 : (q + 1) * 4].astype(F32).reshape(M, 128).astype(BF)
        other = recv_d[q * 4 : (q + 1) * 4].astype(F32).reshape(M, 128).astype(BF)
        lines = jnp.concatenate([own, other], axis=0)
        both = dot(lines, ez_ref[chan], ((0,), (0,)))
        ubuf[q * C : (q + 1) * C, :] = both[0:C, 0:G] + both[C : 2 * C, G : 2 * G]
    for c in range(HALF):
        lines = ubuf[pl.ds(c, 2 * M, stride=HALF), :].astype(BF)
        total[pl.ds(c, G, stride=HALF), :] = total[pl.ds(c, G, stride=HALF), :] + dot(ey_ref[...], lines)

    def finish(group, carry):
        for u in range(4):
            y = group * 4 + u
            rows = pl.ds(pl.multiple_of(y * HALF, HALF), HALF)
            grid[chan, y] = gelu(total[rows, :]).astype(BF)
        return carry

    swaps = []
    for k in range(4):
        lax.fori_loop(k * 8, k * 8 + 8, finish, 0)
        piece = grid.at[chan, pl.ds(k * 32, 32)]
        swaps.append(swap(piece, piece, 9 + k))
        swaps[-1].start()
    for piece in swaps:
        piece.wait()

    def decode(group, carry):
        slabs, values = [], []
        for j in range(16):
            slab = me ^ (group * 16 + j)
            slabs.append(slab)
            for r in range(2):
                line = jnp.maximum(line_ref[slab, 0, r] - 1, 0)
                cells = jnp.concatenate([grid[0, line], grid[1, line]], axis=0)
                values.append(dot(cells, nears[2 * slab + r]).astype(BF))
        hidden = gelu(dot(proj_rows[...], jnp.concatenate(values, axis=1))).astype(BF)
        result = dot(proj_out, hidden)
        for j in range(16):
            for r in range(2):
                u = 2 * j + r
                send_v[slabs[j], r : r + 1, :] = result[0:1, u * PB : (u + 1) * PB]
        for j in range(16):
            copy = pltpu.make_async_remote_copy(
                src_ref=send_v.at[slabs[j]],
                dst_ref=recv_v.at[me],
                send_sem=send_sem.at[8],
                recv_sem=recv_sem.at[8],
                device_id=(slabs[j], chan),
                device_id_type=pl.DeviceIdType.MESH,
            )
            if j > 0:
                copy.start()
            else:
                pl.when(group > 0)(copy.start)
        return carry

    lax.fori_loop(0, 8, decode, 0)
    recv_v[me] = send_v[me]
    settle(send_v, recv_v, send_sem.at[8], recv_sem.at[8])

    def unpack(b, carry):
        slab = slab_ref[b]
        rank = jnp.where(low_ref[slab] == b, 0, 1)
        value = recv_v[slab, pl.ds(rank, 1), :]
        out_ref[pl.ds(b, 1), :] = jnp.where(b < count_ref[0], value, 0.0)
        return carry

    lax.fori_loop(0, 128, unpack, 0, unroll=8)


def shards(
    points,
    near_start,
    near_weight,
    dest_slab,
    dest_block,
    live_count,
    lift_w,
    spec_weight,
    skip_w,
    skip_bias,
    proj_in,
    proj_out,
):
    cos, sin = trig()
    chan = lax.axis_index("chan")

    ids = jnp.arange(128, dtype=jnp.int32)
    target = jnp.where(ids < live_count[0], dest_slab[:, 0], -1)
    match = target[None, :] == ids[:, None]
    low = jnp.min(jnp.where(match, ids[None, :], 128), axis=1)
    high = jnp.max(jnp.where(match, ids[None, :], -1), axis=1)

    parts, lines, meta = pl.pallas_call(
        dispatch_kernel,
        out_shape=(
            jax.ShapeDtypeStruct((G, 2 * C, PB), BF),
            jax.ShapeDtypeStruct((G, 1, PB), jnp.int32),
            jax.ShapeDtypeStruct((G, 24, PB), BF),
        ),
        in_specs=[SM, SM, SM, ANY, ANY, ANY, VM],
        out_specs=(ANY, ANY, VM),
        scratch_shapes=[
            pltpu.VMEM((128, C, PB), BF),
            pltpu.VMEM((128, PB), jnp.int32),
            pltpu.VMEM((128, NB, PB), BF),
            pltpu.VMEM((G, 2 * C, PB), BF),
            pltpu.VMEM((G, 1, PB), jnp.int32),
            pltpu.SemaphoreType.DMA((2,)),
            pltpu.SemaphoreType.DMA((2,)),
            pltpu.SemaphoreType.DMA((5,)),
        ],
        compiler_params=pltpu.CompilerParams(
            vmem_limit_bytes=LIMIT, collective_id=0, has_side_effects=True
        ),
    )(low, high, dest_block, points, near_start, near_weight, lift_w)
    mine, theirs = call(
        gather_kernel,
        (jax.ShapeDtypeStruct((G * HALF, G), F32), jax.ShapeDtypeStruct((G * HALF, G), BF)),
        [SM, SM, ANY],
        [
            pltpu.VMEM((G, 2 * C, PB), BF),
            pltpu.VMEM((2, (G + 1) * HALF, G), F32),
            pltpu.VMEM((G * HALF, G), BF),
            pltpu.SemaphoreType.DMA((10,)),
        ],
        (ANY, ANY),
    )(chan.reshape(1), lines, parts)

    dy = jnp.asarray(np.concatenate([cos.T, -sin.T, -cos.T], axis=0), BF)
    quads = np.concatenate([cos.T, sin.T], axis=1).reshape(4, 2, 1, 4, 2 * G)
    dz = np.broadcast_to(quads, (4, 2, 2, 4, 2 * G)).transpose(1, 0, 2, 3, 4).reshape(2 * M, 2 * G)
    eye4, eye2 = np.eye(4), np.eye(2)
    table = np.stack([cos.T, sin.T])
    forward = np.einsum("hg,vkx,mn->hvkmxgn", eye2, table, eye4).reshape(512, 1024)
    ez = np.zeros((2, 2, 4, 2, 4, 2 * G))
    for h in range(2):
        for side in range(2):
            ez[h, side, :, h, :, :] = quads[:, h if side == 0 else 1 - h, 0]
    ez = ez.reshape(2, 2 * M, 2 * G)
    ey = np.stack([cos, -sin], axis=2).reshape(G, 2 * M) / G**3
    weight = jnp.transpose(spec_weight, (0, 1, 3, 4, 2)).reshape(2, C, 128, C)
    plane = (G * HALF, G)
    block8 = pltpu.VMEM((G, 8, 128), BF)
    return pl.pallas_call(
        middle_kernel,
        out_shape=jax.ShapeDtypeStruct((128, PB), F32),
        in_specs=[SM] * 5 + [ANY] * 6 + [VM] * 7,
        out_specs=VM,
        scratch_shapes=[
            pltpu.VMEM((2, C, 128, C), BF),
            pltpu.VMEM((512, 1024), BF),
            pltpu.VMEM((1024, 512), BF),
            pltpu.SemaphoreType.DMA((5,)),
            pltpu.VMEM((2 * G, G, PB), BF),
            pltpu.VMEM((C, C), F32),
            pltpu.VMEM((HALF, G), F32),
            pltpu.VMEM((128, C), BF),
            pltpu.VMEM((2, G, HALF, G), BF),
            pltpu.VMEM((G, 24, PB), BF),
            pltpu.VMEM((G, 2, PB), F32),
            pltpu.VMEM((G, 2, PB), F32),
            pltpu.VMEM(plane, BF),
            pltpu.VMEM((2,) + plane, BF),
            pltpu.VMEM(plane, F32),
            pltpu.VMEM((3 * M * HALF, G), F32),
            pltpu.VMEM((2, 1024, 128), BF),
            pltpu.VMEM((1024, 128), BF),
            block8,
            block8,
            pltpu.VMEM((2, 128, C), F32),
            pltpu.VMEM((512, 128), BF),
            block8,
            block8,
            block8,
            pltpu.VMEM((M * C, G), F32),
            pltpu.SemaphoreType.DMA((13,)),
            pltpu.SemaphoreType.DMA((13,)),
        ],
        compiler_params=pltpu.CompilerParams(
            vmem_limit_bytes=LIMIT, collective_id=1, has_side_effects=True
        ),
    )(
        lines, low, dest_slab[:, 0], live_count, skip_bias, mine, theirs, weight,
        jnp.asarray(forward, BF), jnp.asarray(forward.T, BF), meta,
        dy, jnp.asarray(dz, BF), jnp.asarray(ez, BF), jnp.asarray(ey, BF), skip_w, proj_in,
        proj_out.reshape(1, 128),
    )


def solution(mesh):
    placed = (
        P(("slab", "chan"), None, None),
        P(("slab", "chan"), None),
        P(("slab", "chan"), None, None),
        P(("slab", "chan"), None),
        P(("slab", "chan")),
        P(("slab", "chan")),
        P(),
        P(None, None, None, None, ("slab", "chan")),
        P(),
        P(),
        P(),
        P(),
    )
    return jax.shard_map(
        shards, mesh=mesh, in_specs=placed, out_specs=P(("slab", "chan"), None), check_vma=False
    )
```
